128 devices in a mesh: dom: 32 (over x, z, core), feat: 4 (over y).
Axes of the slice: x: 4, y: 4, z: 4, core: 2. Of those that a mesh axis runs over, the one named last changes fastest.
Arguments:
- embeddings: bfloat16 [131072, 512], P('dom', 'feat'), may hold values from -6 to 6
- self_weight: bfloat16 [512, 512], P(None, 'feat'), may hold values from -0.25 to 0.25
- bases: bfloat16 [64, 512, 512], P(None, None, 'feat'), may hold values from -0.25 to 0.25
- basis_coef: bfloat16 [822, 64], replicated, may hold values from -0.75 to 0.75
- out_gain: float32 [512], P('feat'), may hold values from 0.1 to 1.9
- edge_src: int32 [16384, 128], P('dom'), may hold values from 0 to 4095, as said below
- edge_dst: int32 [16384, 128], P('dom'), may hold values from 0 to 8192, as said below
- block_rel: int32 [16384], P('dom'), may hold values from 0 to 821
- mirror_master_rows: int32 [131072], P('dom'), may hold values from 128 to 3071
- block_count: int32 [32], P('dom'), may hold values from 128 to 512, as said below
Outputs:
- updated: bfloat16 [131072, 512], P('dom', 'feat')
The draws below stay inside these ranges and needn't reach their ends.
Inputs may be any that keep to these rules, and one draw needn't show every extreme that they name: `edge_src`: all rows of a block name sources in one aligned run of 128 rows of the slab. `edge_dst`: every block has at least one padding row and at least 64 used rows, row 0 among them; the used rows of a block name slots of one aligned run of 128 slots. `block_count`: some index of dom has all 512 blocks live. `mirror_master_rows`: hub entities are the first 128 rows of each slab; the last 1024 rows of a slab are never destinations.
All inputs are finite; a program needn't handle non-finite values.
Results may differ from the reference program's by a relative error of at most 0.007.
Values may be sent and summed in bfloat16 or wider, within the bound.
No kernel may reach another device: no remote copies, remote signals or barrier semaphores. Data moves between devices by JAX's collectives and lax.ppermute only.
A program may use at most 128 MiB of HBM per device.

```python
import jax
import jax.numpy as jnp
from jax import lax

D = 512
NB = 64
R = 822
EB = 128
TILE = 128
LOCAL_ENTITIES = 4096
BLK = 512
HUB_MIRRORS = 128
CAP = 128
ENT = 131072
MIRROR_SLOTS = 4096
N_DOM = 32


def draw_block_count(key, part):
    key = jax.random.fold_in(key, 11)
    first_key, second_key = jax.random.split(key)
    counted = jax.random.randint(first_key, (N_DOM,), BLK // 4, BLK + 1)
    busiest = jax.random.randint(second_key, (), 0, N_DOM)
    return jnp.where(jnp.arange(N_DOM) == busiest, BLK, counted).astype(jnp.int32)


def draw_edge_src(key, part):
    key = jax.random.fold_in(key, 31)
    first_key, second_key = jax.random.split(key)
    tile_pick = jax.random.randint(first_key, (N_DOM * BLK, 1), 0, LOCAL_ENTITIES // TILE)
    offset = jax.random.randint(second_key, (N_DOM * BLK, EB), 0, TILE)
    return (tile_pick * TILE + offset).astype(jnp.int32)


def draw_edge_dst(key, part):
    key = jax.random.fold_in(key, 23)
    keys = jax.random.split(key, 5)
    hub_total = HUB_MIRRORS * N_DOM
    slot_total = hub_total + CAP * N_DOM
    to_hub = jax.random.randint(keys[0], (N_DOM * BLK, 1), 0, 4) == 0
    hub_tile = jax.random.randint(keys[1], (N_DOM * BLK, 1), 0, hub_total // TILE)
    mirror_tile = jax.random.randint(keys[2], (N_DOM * BLK, 1), hub_total // TILE, slot_total // TILE)
    offset = jax.random.randint(keys[3], (N_DOM * BLK, EB), 0, TILE)
    fill_rows = jax.random.randint(keys[4], (N_DOM * BLK, 1), EB // 2, EB)
    position = jnp.arange(EB)[None, :]
    chosen = jnp.where(to_hub, hub_tile, mirror_tile) * TILE + offset
    return jnp.where(position < fill_rows, chosen, slot_total).astype(jnp.int32)


def with_ends(values, key, smallest, largest):
    index_at = [jax.random.randint(jax.random.fold_in(key, axis), (), 0, length) for axis, length in enumerate(values.shape)]
    longest = values.shape.index(max(values.shape))
    next_to = index_at[:longest] + [(index_at[longest] + 1) % values.shape[longest]] + index_at[longest + 1:]
    return values.at[tuple(index_at)].set(smallest).at[tuple(next_to)].set(largest)


def shard_levels(rng, shape, pieces, smallest, largest):
    gain, own = 1.0, jax.random.fold_in(rng, 6)
    for dim, parts in pieces:
        heights = jnp.exp(jax.random.uniform(jax.random.fold_in(own, dim), (parts,), jnp.float32, smallest / len(pieces), largest / len(pieces)))
        gain = gain * jnp.repeat(heights, shape[dim] // parts).reshape([-1 if axis == dim else 1 for axis in range(len(shape))])
    return gain


def noise(stream_key, dims, width, reach, pieces=(), kind=jnp.bfloat16):
    entries = width * jax.random.normal(stream_key, dims, jnp.float32)
    if pieces:
        entries = entries * shard_levels(stream_key, dims, pieces, -0.22, 0.18)
    return jnp.clip(entries, -reach, reach).astype(kind)


def setup_inputs(seed: int = 0) -> dict:
    key_of = jax.random.split(jax.random.key(seed), 11)
    embeddings = noise(key_of[0], (ENT, D), 1.0, 6.0, ((0, 32), (1, 4)))
    self_weight = noise(key_of[1], (D, D), D ** -0.5, 0.25, ((1, 4),))
    bases = noise(key_of[2], (NB, D, D), D ** -0.5, 0.25, ((2, 4),))
    basis_coef = noise(key_of[3], (R, NB), NB ** -0.5, 0.75)
    out_gain = jnp.clip(1.0 + 0.18 * jax.random.normal(key_of[4], (D,), jnp.float32), 0.1, 1.9)
    edge_src = draw_edge_src(jax.random.fold_in(key_of[10], 71), 0)
    edge_dst = draw_edge_dst(jax.random.fold_in(key_of[10], 71), 0)
    block_rel = with_ends(jax.random.randint(key_of[7], (N_DOM * BLK,), 0, R), jax.random.fold_in(key_of[7], 1), 0, R - 1).astype(jnp.int32)
    mirror_master_rows = with_ends(jax.random.randint(key_of[8], (N_DOM * MIRROR_SLOTS,), HUB_MIRRORS, LOCAL_ENTITIES - LOCAL_ENTITIES // 4), jax.random.fold_in(key_of[8], 1), HUB_MIRRORS, (LOCAL_ENTITIES - LOCAL_ENTITIES // 4) - 1).astype(jnp.int32)
    block_count = draw_block_count(jax.random.fold_in(key_of[10], 71), 0)
    return {"embeddings": embeddings, "self_weight": self_weight, "bases": bases, "basis_coef": basis_coef, "out_gain": out_gain, "edge_src": edge_src, "edge_dst": edge_dst, "block_rel": block_rel, "mirror_master_rows": mirror_master_rows, "block_count": block_count}


def reference(embeddings, self_weight, bases, basis_coef, out_gain, edge_src, edge_dst, block_rel, mirror_master_rows, block_count):
    entity_total = LOCAL_ENTITIES * N_DOM
    hub_total = HUB_MIRRORS * N_DOM
    mirror_total = CAP * N_DOM
    per_group = min(32, BLK)
    flat_bases = bases.reshape(NB, D * D)

    def per_device(carry, device):

        def per_group_step(inner, index):
            sums_in, counts_in = inner
            row_offset = (device * BLK + index * per_group).astype(jnp.int32)
            sources = lax.dynamic_slice_in_dim(edge_src, row_offset, per_group, 0) + device * LOCAL_ENTITIES
            targets = lax.dynamic_slice_in_dim(edge_dst, row_offset, per_group, 0)
            relation = lax.dynamic_slice_in_dim(block_rel, row_offset, per_group, 0)
            mixing = basis_coef[relation]
            combined = jnp.dot(mixing, flat_bases, preferred_element_type=jnp.float32).astype(jnp.bfloat16)
            combined = combined.reshape(per_group, D, D)
            source_rows = embeddings[sources]
            messages = jnp.einsum('ged,gdk->gek', source_rows.astype(jnp.float32), combined.astype(jnp.float32))
            hub_global = targets // HUB_MIRRORS * LOCAL_ENTITIES + targets % HUB_MIRRORS
            mirror_slot = jnp.clip(targets - hub_total, 0, mirror_total - 1)
            owner = mirror_slot // CAP
            master = mirror_master_rows[owner * mirror_total + device * CAP + mirror_slot % CAP]
            mirror_global = owner * LOCAL_ENTITIES + master
            destination = jnp.where(targets < hub_total, hub_global, mirror_global)
            live_block = index * per_group + jnp.arange(per_group, dtype=jnp.int32) < block_count[device]
            keep = (targets < hub_total + mirror_total) & live_block[:, None]
            destination = jnp.where(keep, destination, entity_total).reshape(-1).astype(jnp.int32)
            sums_in = sums_in.at[destination].add(messages.reshape(-1, D))
            counts_in = counts_in.at[destination].add(jnp.ones(destination.shape, jnp.float32))
            return ((sums_in, counts_in), None)
        result, ignored_value = lax.scan(per_group_step, carry, jnp.arange(BLK // per_group, dtype=jnp.int32))
        return (result, None)
    sums_start = jnp.zeros((entity_total + 1, D), jnp.float32)
    initial_counts = jnp.zeros((entity_total + 1,), jnp.float32)
    (sums, counts), ignored_value = lax.scan(per_device, (sums_start, initial_counts), jnp.arange(N_DOM, dtype=jnp.int32))
    scale = lax.rsqrt(jnp.maximum(counts[:entity_total], 1.0))
    mixed = jnp.dot(embeddings, self_weight, preferred_element_type=jnp.float32) + sums[:entity_total] * scale[:, None]
    norm = lax.rsqrt(lax.optimization_barrier(jnp.mean(mixed * mixed, axis=1, keepdims=True)) + 1e-05)
    return (mixed * norm * out_gain).astype(jnp.bfloat16)
```

```python
import functools

import jax
import jax.numpy as jnp
from jax import lax
from jax.experimental import pallas as pl
from jax.experimental.pallas import tpu as pltpu
from jax.sharding import PartitionSpec as P

TILE = 128
HUB_MIRRORS = 128
CAP = 128
DEG_ROWS = 16
VMEM_LIMIT = 56 * 1024 * 1024
BF = jnp.bfloat16
F32 = jnp.float32


def mix_kernel(feat_ref, lhs_ref, bases_ref, w_ref, spread, *, chunk):
    n_bases, depth, cols = bases_ref.shape
    spread[...] = bases_ref[...].astype(F32).reshape(n_bases * depth, cols)

    def rows_of(d):
        return spread[pl.ds(d, n_bases, stride=depth), :].astype(BF)

    rights = []
    for octet in range(depth // 8):
        halves = []
        for half in range(2):
            first = octet * 8 + half * 4
            halves.append(jnp.concatenate([rows_of(first + i) for i in range(4)], axis=0))
        rights.append(jnp.concatenate(halves, axis=1))
    pairs = chunk // 8
    low = lax.broadcasted_iota(jnp.int32, (pairs, 8, cols), 1) < 4

    def body(step, carry):
        row = pl.multiple_of(step * chunk, chunk)
        left = lhs_ref[pl.ds(row, chunk), :]
        evens, odds = [], []
        for right in rights:
            out = jnp.dot(left, right, preferred_element_type=F32)
            first = out[:, :cols].reshape(pairs, 8, cols)
            second = out[:, cols:].reshape(pairs, 8, cols)
            evens.append(jnp.where(low, first, pltpu.roll(second, 4, 1)))
            odds.append(jnp.where(low, pltpu.roll(first, 4, 1), second))
        pair = step * pairs
        w_ref[pl.ds(pair, pairs), 0] = jnp.concatenate(evens, axis=1).astype(BF)
        w_ref[pl.ds(pair, pairs), 1] = jnp.concatenate(odds, axis=1).astype(BF)
        return carry

    lax.fori_loop(0, lhs_ref.shape[0] // chunk, body, 0)


def mix(feat, lhs, bases, blocks):
    n_bases, model_dim, cols = bases.shape
    depth = 16
    steps = model_dim // depth
    per_part = cols // depth
    return pl.pallas_call(
        functools.partial(mix_kernel, chunk=256),
        out_shape=jax.ShapeDtypeStruct((blocks // 2, 2, model_dim, cols), BF),
        grid_spec=pltpu.PrefetchScalarGridSpec(
            num_scalar_prefetch=1,
            grid=(steps,),
            in_specs=[
                pl.BlockSpec(lhs.shape, lambda i, f: (0, 0)),
                pl.BlockSpec(
                    (n_bases, depth, cols),
                    lambda i, f: (0, lax.rem(i + f[0] * per_part, steps), 0),
                ),
            ],
            out_specs=pl.BlockSpec((blocks // 2, 2, depth, cols), lambda i, f: (0, 0, i, 0)),
            scratch_shapes=[pltpu.VMEM((n_bases * depth, cols), F32)],
        ),
        compiler_params=pltpu.CompilerParams(vmem_limit_bytes=VMEM_LIMIT),
        name="mix",
    )(feat, lhs, bases)


def adjacency_kernel(
    src_tile_ref, dst_tile_ref, live_ref, src_ref, dst_ref, adj_ref, deg_ref, *, group
):
    step = pl.program_id(0)

    @pl.when(step == 0)
    def _():
        deg_ref[...] = jnp.zeros_like(deg_ref)

    slot = lax.broadcasted_iota(jnp.int32, (TILE, TILE), 0)
    total = deg_ref[...]
    for i in range(group):
        block = step * group + i
        dst_tile = dst_tile_ref[block]
        base = jnp.where(block < live_ref[0], dst_tile * TILE, 1 << 20)
        dst = dst_ref[i : i + 1, :] - base
        src = src_ref[i : i + 1, :] - src_tile_ref[block] * TILE
        dst_hot = jnp.where(slot == dst, 1.0, 0.0).astype(BF)
        src_hot = jnp.where(slot == src, 1.0, 0.0).astype(BF)
        mark = jnp.where(slot == dst_tile, 1.0, 0.0).astype(BF)
        right = jnp.concatenate([src_hot, mark], axis=0)
        out = lax.dot_general(
            dst_hot, right, (((1,), (1,)), ((), ())), preferred_element_type=F32
        )
        adj_ref[i] = out[:, :TILE].astype(BF)
        total = total + out[:, TILE:]
    deg_ref[...] = total


def adjacency(src_tile, dst_tile, live, edge_src, edge_dst):
    blocks = edge_src.shape[0]
    group = 8
    return pl.pallas_call(
        functools.partial(adjacency_kernel, group=group),
        out_shape=(
            jax.ShapeDtypeStruct((blocks, TILE, TILE), BF),
            jax.ShapeDtypeStruct((TILE, TILE), F32),
        ),
        grid_spec=pltpu.PrefetchScalarGridSpec(
            num_scalar_prefetch=3,
            grid=(blocks // group,),
            in_specs=[
                pl.BlockSpec((group, TILE), lambda i, *_: (i, 0)),
                pl.BlockSpec((group, TILE), lambda i, *_: (i, 0)),
            ],
            out_specs=(
                pl.BlockSpec((group, TILE, TILE), lambda i, *_: (i, 0, 0)),
                pl.BlockSpec((TILE, TILE), lambda i, *_: (0, 0)),
            ),
        ),
        compiler_params=pltpu.CompilerParams(vmem_limit_bytes=VMEM_LIMIT),
        name="adjacency",
    )(src_tile, dst_tile, live, edge_src, edge_dst)


def blocks_kernel(
    src_tile_ref,
    dst_tile_ref,
    live_ref,
    w_ref,
    adj_ref,
    deg_ref,
    x0_ref,
    x1_ref,
    x2_ref,
    x3_ref,
    out_ref,
    acc,
    *,
    group,
):
    step = pl.program_id(0)

    @pl.when(step == 0)
    def _():
        acc[...] = jnp.zeros_like(acc)

    @pl.when(step * group < live_ref[0])
    def _():
        for i in range(group):
            block = step * group + i
            row = pl.multiple_of(src_tile_ref[block] * TILE, TILE)
            rows = pl.ds(row, TILE)
            tile = jnp.concatenate(
                [x0_ref[rows, :], x1_ref[rows, :], x2_ref[rows, :], x3_ref[rows, :]], axis=1
            )
            message = jnp.dot(tile, w_ref[i // 2, i % 2], preferred_element_type=F32).astype(BF)
            dst = dst_tile_ref[block]
            acc[dst] = acc[dst] + jnp.dot(adj_ref[i], message, preferred_element_type=F32)

    @pl.when(step == pl.num_programs(0) - 1)
    def _():
        owners = out_ref.shape[1]
        degree = deg_ref[...].T
        high = jnp.floor(degree * (1.0 / 256.0)) * 256.0
        low = degree - high
        line = lax.broadcasted_iota(jnp.int32, (owners, DEG_ROWS, TILE), 1)
        for part in range(2):
            here = slice(part * owners, (part + 1) * owners)
            out_ref[part, :, :TILE, :] = acc[here].astype(BF)
            rows = jnp.where(
                line == 0, high[here][:, None, :], jnp.where(line == 1, low[here][:, None, :], 0.0)
            )
            out_ref[part, :, TILE:, :] = rows.astype(BF)


def blocks_call(src_tile, dst_tile, live, weights, adj, deg, pieces, owners):
    pairs, _, model_dim, cols = weights.shape
    group = 8
    whole = lambda shape: pl.BlockSpec(shape, lambda i, *_: (0,) * len(shape))
    out = (2, owners, TILE + DEG_ROWS, cols)
    return pl.pallas_call(
        functools.partial(blocks_kernel, group=group),
        out_shape=jax.ShapeDtypeStruct(out, BF),
        grid_spec=pltpu.PrefetchScalarGridSpec(
            num_scalar_prefetch=3,
            grid=(pairs * 2 // group,),
            in_specs=[
                pl.BlockSpec((group // 2, 2, model_dim, cols), lambda i, *_: (i, 0, 0, 0)),
                pl.BlockSpec((group, TILE, TILE), lambda i, *_: (i, 0, 0)),
                whole(deg.shape),
            ]
            + [whole(p.shape) for p in pieces],
            out_specs=whole(out),
            scratch_shapes=[pltpu.VMEM((2 * owners, TILE, cols), F32)],
        ),
        compiler_params=pltpu.CompilerParams(vmem_limit_bytes=VMEM_LIMIT),
        name="blocks",
    )(src_tile, dst_tile, live, weights, adj, deg, *pieces)


def final_kernel(
    hub_ref,
    mirror_ref,
    master_ref,
    self_ref,
    x0_ref,
    x1_ref,
    x2_ref,
    x3_ref,
    mixed_ref,
    squares_ref,
    right,
    *,
    chunk,
):
    step = pl.program_id(0)
    owners = mirror_ref.shape[0]
    cols = mirror_ref.shape[2]
    slots = owners * TILE
    last_chunks = pl.num_programs(0)

    @pl.when(step == 0)
    def _():
        high = mirror_ref[:, TILE, :].astype(F32)
        low = mirror_ref[:, TILE + 1, :].astype(F32)
        pad = jnp.zeros((TILE - 2 * owners, TILE), F32)
        table = jnp.concatenate([high, low, pad], axis=0).T
        lane = lax.broadcasted_iota(jnp.int32, (TILE, TILE), 1)
        for p in range(owners):
            rows = slice(p * TILE, (p + 1) * TILE)
            right[rows, :cols] = mirror_ref[p, :TILE, :]
            keep = (lane == p) | (lane == p + owners)
            right[rows, cols:] = jnp.where(keep, table, 0.0).astype(BF)

    rows = pl.ds(pl.multiple_of(step * chunk, chunk), chunk)
    tile = jnp.concatenate(
        [x0_ref[rows, :], x1_ref[rows, :], x2_ref[rows, :], x3_ref[rows, :]], axis=1
    )
    own = jnp.dot(tile, self_ref[...], preferred_element_type=F32)
    entity = lax.broadcasted_iota(jnp.int32, (chunk, TILE), 0) + step * chunk
    hot = jnp.concatenate(
        [
            jnp.where(entity == master_ref[p : p + 1, :], 1.0, 0.0).astype(BF)
            for p in range(owners)
        ],
        axis=1,
    )
    sums = jnp.dot(hot, right[...], preferred_element_type=F32)
    degree = jnp.sum(sums[:, cols:], axis=1, keepdims=True)
    total = sums[:, :cols]
    scale = lax.rsqrt(jnp.maximum(degree, 1.0))
    mixed = own + total * scale
    mixed_ref[...] = mixed

    @pl.when(step == 0)
    def _():
        hub = jnp.sum(hub_ref[:, :TILE, :].astype(F32), axis=0)
        line = jnp.sum(
            hub_ref[:, TILE, :].astype(F32) + hub_ref[:, TILE + 1, :].astype(F32),
            axis=0,
            keepdims=True,
        )
        column = jnp.broadcast_to(line, (TILE, TILE)).T[:, :1]
        hub_scale = lax.rsqrt(jnp.maximum(column + degree[:TILE], 1.0))
        mixed_ref[:TILE, :] = own[:TILE] + (total[:TILE] + hub) * hub_scale

    value = mixed_ref[...]
    squares = jnp.sum(value * value, axis=1, keepdims=True)
    squares_ref[...] = jnp.broadcast_to(squares, (chunk, TILE)).T[:8, :]


def final(hub, mirror, master, self_weight, pieces):
    n_local, cols = pieces[0].shape
    owners = mirror.shape[0]
    chunk = 256
    whole = lambda shape: pl.BlockSpec(shape, lambda i: (0,) * len(shape))
    return pl.pallas_call(
        functools.partial(final_kernel, chunk=chunk),
        out_shape=(
            jax.ShapeDtypeStruct((n_local, cols), F32),
            jax.ShapeDtypeStruct((8, n_local), F32),
        ),
        grid=(n_local // chunk,),
        in_specs=[whole(hub.shape), whole(mirror.shape), whole(master.shape), whole(self_weight.shape)]
        + [whole(p.shape) for p in pieces],
        out_specs=(
            pl.BlockSpec((chunk, cols), lambda i: (i, 0)),
            pl.BlockSpec((8, chunk), lambda i: (0, i)),
        ),
        scratch_shapes=[pltpu.VMEM((owners * TILE, 2 * cols), BF)],
        compiler_params=pltpu.CompilerParams(vmem_limit_bytes=VMEM_LIMIT),
        name="final",
    )(hub, mirror, master, self_weight, *pieces)


def from_others(x, size):
    return [
        lax.ppermute(x, "feat", [((i + shift) % size, i) for i in range(size)])
        for shift in range(1, size)
    ]


def on_device(
    embeddings,
    self_weight,
    bases,
    basis_coef,
    out_gain,
    edge_src,
    edge_dst,
    block_rel,
    mirror_master_rows,
    block_count,
):
    owners = lax.axis_size("dom")
    feat_size = lax.axis_size("feat")
    feat = lax.axis_index("feat").astype(jnp.int32)
    blocks = edge_src.shape[0]
    n_local, cols = embeddings.shape
    n_bases, model_dim, _ = bases.shape
    relations = basis_coef.shape[0]

    pieces = [embeddings] + from_others(embeddings, feat_size)

    src_tile = edge_src[:, 0] // TILE
    dst_tile = edge_dst[:, 0] // TILE

    spread = 4
    relation = jnp.repeat(block_rel, spread)
    one_hot = (relation[:, None] == jnp.arange(relations)[None, :]).astype(BF)
    wide = jnp.concatenate([basis_coef] * spread, axis=1)
    lhs = jnp.dot(one_hot, wide, preferred_element_type=F32)
    line = lax.broadcasted_iota(jnp.int32, lhs.shape, 0) % spread
    group = lax.broadcasted_iota(jnp.int32, lhs.shape, 1) // n_bases
    lhs = jnp.where(line == group, lhs, 0.0).astype(BF)

    adj, deg = adjacency(src_tile, dst_tile, block_count, edge_src, edge_dst)
    weights = mix(feat.reshape(1), lhs, bases, blocks)
    partial = blocks_call(src_tile, dst_tile, block_count, weights, adj, deg, pieces, owners)

    hub = lax.all_to_all(partial[0], "dom", split_axis=0, concat_axis=0, tiled=True)
    mirror = lax.all_to_all(partial[1], "dom", split_axis=0, concat_axis=0, tiled=True)

    turned = jnp.roll(self_weight, -feat * cols, axis=0)
    mixed, squares = final(hub, mirror, mirror_master_rows.reshape(owners, TILE), turned, pieces)
    line = squares[0].reshape(n_local // TILE, TILE)
    everyone = line
    for other in from_others(line, feat_size):
        everyone = everyone + other
    norm = lax.rsqrt(everyone.reshape(n_local) / model_dim + 1e-05)
    return (mixed * norm[:, None] * out_gain).astype(BF)


def solution(mesh):
    in_specs = (
        P("dom", "feat"),
        P(None, "feat"),
        P(None, None, "feat"),
        P(),
        P("feat"),
        P("dom", None),
        P("dom", None),
        P("dom"),
        P("dom"),
        P("dom"),
    )
    out_specs = P("dom", "feat")
    return jax.shard_map(
        on_device, mesh=mesh, in_specs=in_specs, out_specs=out_specs, check_vma=False
    )
```

```python
import functools

import jax
import jax.numpy as jnp
from jax import lax
from jax.experimental import pallas as pl
from jax.experimental.pallas import tpu as pltpu
from jax.sharding import PartitionSpec as P

TILE = 128
HUB_MIRRORS = 128
CAP = 128
DEG_ROWS = 16
VMEM_LIMIT = 56 * 1024 * 1024
BF = jnp.bfloat16
F32 = jnp.float32


def mix_kernel(feat_ref, lhs_ref, bases_ref, w_ref, spread, *, chunk):
    n_bases, depth, cols = bases_ref.shape
    spread[...] = bases_ref[...].astype(F32).reshape(n_bases * depth, cols)

    def rows_of(d):
        return spread[pl.ds(d, n_bases, stride=depth), :].astype(BF)

    rights = []
    for octet in range(depth // 8):
        halves = []
        for half in range(2):
            first = octet * 8 + half * 4
            halves.append(jnp.concatenate([rows_of(first + i) for i in range(4)], axis=0))
        rights.append(jnp.concatenate(halves, axis=1))
    pairs = chunk // 8
    low = lax.broadcasted_iota(jnp.int32, (pairs, 8, cols), 1) < 4

    def body(step, carry):
        row = pl.multiple_of(step * chunk, chunk)
        left = lhs_ref[pl.ds(row, chunk), :]
        evens, odds = [], []
        for right in rights:
            out = jnp.dot(left, right, preferred_element_type=F32)
            first = out[:, :cols].reshape(pairs, 8, cols)
            second = out[:, cols:].reshape(pairs, 8, cols)
            evens.append(jnp.where(low, first, pltpu.roll(second, 4, 1)))
            odds.append(jnp.where(low, pltpu.roll(first, 4, 1), second))
        pair = step * pairs
        w_ref[pl.ds(pair, pairs), 0] = jnp.concatenate(evens, axis=1).astype(BF)
        w_ref[pl.ds(pair, pairs), 1] = jnp.concatenate(odds, axis=1).astype(BF)
        return carry

    lax.fori_loop(0, lhs_ref.shape[0] // chunk, body, 0)


def mix(feat, lhs, bases, blocks):
    n_bases, model_dim, cols = bases.shape
    depth = 16
    steps = model_dim // depth
    per_part = cols // depth
    return pl.pallas_call(
        functools.partial(mix_kernel, chunk=2048),
        out_shape=jax.ShapeDtypeStruct((blocks // 2, 2, model_dim, cols), BF),
        grid_spec=pltpu.PrefetchScalarGridSpec(
            num_scalar_prefetch=1,
            grid=(steps,),
            in_specs=[
                pl.BlockSpec(lhs.shape, lambda i, f: (0, 0)),
                pl.BlockSpec(
                    (n_bases, depth, cols),
                    lambda i, f: (0, lax.rem(i + f[0] * per_part, steps), 0),
                ),
            ],
            out_specs=pl.BlockSpec((blocks // 2, 2, depth, cols), lambda i, f: (0, 0, i, 0)),
            scratch_shapes=[pltpu.VMEM((n_bases * depth, cols), F32)],
        ),
        compiler_params=pltpu.CompilerParams(vmem_limit_bytes=VMEM_LIMIT),
        name="mix",
    )(feat, lhs, bases)


def unpack(word):
    return word & 511, (word >> 9) & 31, (word >> 14) & 63, word >> 20


def blocks_kernel(
    word_ref,
    span_ref,
    src_ref,
    dst_ref,
    x0_ref,
    x1_ref,
    x2_ref,
    x3_ref,
    w_ref,
    out_ref,
    acc,
    deg,
    held,
    sems,
    *,
    group,
    owners,
    split,
):
    first_group, end_group = span_ref[0], span_ref[1]

    def fetch(at):
        side = at & 1
        for k in range(2 * group):
            block = word_ref[at * (2 * group) + k] & 511
            pltpu.make_async_copy(
                w_ref.at[block >> 1, block & 1], held.at[side, k // 2, k % 2], sems.at[side]
            ).start()

    @pl.when(first_group < end_group)
    def _():
        fetch(first_group)

    acc[...] = jnp.zeros_like(acc)
    deg[...] = jnp.zeros_like(deg)

    def body(here, carry):
        side = here & 1

        @pl.when(here + 1 < end_group)
        def _():
            fetch(here + 1)

        pltpu.make_async_copy(w_ref.at[pl.ds(0, group)], held.at[side], sems.at[side]).wait()
        slot = lax.broadcasted_iota(jnp.int32, (TILE, TILE), 0).astype(F32).astype(BF)
        lane = lax.broadcasted_iota(jnp.int32, (TILE, TILE), 1)
        one = jnp.ones((TILE, TILE), BF)
        zero = jnp.zeros((TILE, TILE), BF)

        def diagonal(first, second):
            top = jnp.concatenate([first, zero], axis=1)
            bottom = jnp.concatenate([zero, second], axis=1)
            return jnp.concatenate([top, bottom], axis=0)

        def fields(pair, k):
            return unpack(word_ref[(here * group + pair) * 2 + k])

        def adjacency(pair):
            dst_hot, src_hot, count = [], [], None
            for k in range(2):
                block, src_tile, dst_tile, used = fields(pair, k)
                base = jnp.where(used > 0, dst_tile * TILE, 1 << 20)
                dst = (dst_ref[pl.ds(block, 1), :] - base).astype(F32).astype(BF)
                src = (src_ref[pl.ds(block, 1), :] - src_tile * TILE).astype(F32).astype(BF)
                dst_hot.append(jnp.where(slot == dst, one, zero))
                src_hot.append(jnp.where(slot == src, one, zero))
                column = jnp.sum(dst_hot[k].astype(F32), axis=1, keepdims=True)
                extra = jnp.where(lane == lax.rem(dst_tile, owners), column, 0.0)
                count = extra if count is None else count + extra
            found = lax.dot_general(
                jnp.concatenate(dst_hot, axis=1),
                diagonal(src_hot[0], src_hot[1]),
                (((1,), (1,)), ((), ())),
                preferred_element_type=F32,
            )
            return found.astype(BF), count

        def message(pair):
            src_tile = fields(pair, 0)[1]
            rows = pl.ds(pl.multiple_of(src_tile * TILE, TILE), TILE)
            tile = jnp.concatenate(
                [x0_ref[rows, :], x1_ref[rows, :], x2_ref[rows, :], x3_ref[rows, :]], axis=1
            )
            weight = jnp.concatenate([held[side, pair, 0], held[side, pair, 1]], axis=1)
            out = jnp.dot(tile, weight, preferred_element_type=F32).astype(BF)
            return diagonal(out[:, :TILE], out[:, TILE:])

        total = deg[...]
        for first in range(0, group, split):
            pairs = range(first, first + split)
            found = [adjacency(pair) for pair in pairs]
            messages = [message(pair) for pair in pairs]
            sums = [
                jnp.dot(f[0], m, preferred_element_type=F32) for f, m in zip(found, messages)
            ]
            for pair, both, part in zip(pairs, sums, found):
                total = total + part[1]
                for k in range(2):
                    dst = lax.rem(fields(pair, k)[2], owners)
                    acc[dst] = acc[dst] + both[:, k * TILE : (k + 1) * TILE]
        deg[...] = total
        return carry

    lax.fori_loop(first_group, end_group, body, 0)

    degree = deg[...].T[:owners]
    high = jnp.floor(degree * (1.0 / 256.0)) * 256.0
    low = degree - high
    line = lax.broadcasted_iota(jnp.int32, (owners, DEG_ROWS, TILE), 1)
    out_ref[:, :TILE, :] = acc[...].astype(BF)
    rows = jnp.where(line == 0, high[:, None, :], jnp.where(line == 1, low[:, None, :], 0.0))
    out_ref[:, TILE:, :] = rows.astype(BF)


def blocks_call(words, span, weights, edge_src, edge_dst, pieces, owners, name, group=16, split=16):
    _, _, model_dim, cols = weights.shape
    vmem = pl.BlockSpec(memory_space=pltpu.VMEM)
    smem = pl.BlockSpec(memory_space=pltpu.SMEM)
    return pl.pallas_call(
        functools.partial(blocks_kernel, group=group, owners=owners, split=split),
        out_shape=jax.ShapeDtypeStruct((owners, TILE + DEG_ROWS, cols), BF),
        in_specs=[smem, smem, vmem, vmem] + [vmem] * len(pieces) + [pl.BlockSpec(memory_space=pl.ANY)],
        out_specs=vmem,
        scratch_shapes=[
            pltpu.VMEM((owners, TILE, cols), F32),
            pltpu.VMEM((TILE, TILE), F32),
            pltpu.VMEM((2, group, 2, model_dim, cols), BF),
            pltpu.SemaphoreType.DMA((2,)),
        ],
        compiler_params=pltpu.CompilerParams(vmem_limit_bytes=VMEM_LIMIT),
        name=name,
    )(words, span, edge_src, edge_dst, *pieces, weights)


def arrange(src_tile, dst_tile, live, owners, src_tiles, group):
    blocks = src_tile.shape[0]
    keys = 2 * src_tiles
    slots = 2 * group * (-(-(blocks + keys) // (2 * group)) + 1)
    index = jnp.arange(blocks, dtype=jnp.int32)
    key_range = jnp.arange(keys, dtype=jnp.int32)
    active = index < live
    key = jnp.where(active, jnp.where(dst_tile < owners, src_tiles, 0) + src_tile, keys)
    count = jnp.sum((key[None, :] == key_range[:, None]).astype(jnp.int32), axis=1)
    pairs = (count + 1) >> 1
    start = jnp.sum(jnp.where(key_range[None, :] < key_range[:, None], pairs[None, :], 0), axis=1)
    mirror_pairs = jnp.sum(pairs[:src_tiles])
    hub_pairs = jnp.sum(pairs[src_tiles:])
    mirror_groups = (mirror_pairs + group - 1) // group
    hub_groups = (hub_pairs + group - 1) // group
    start = start + jnp.where(key_range >= src_tiles, mirror_groups * group - mirror_pairs, 0)
    before = (key[None, :] == key[:, None]) & (index[None, :] < index[:, None])
    rank = jnp.sum(before.astype(jnp.int32), axis=1)
    place = jnp.sum(jnp.where(key[:, None] == key_range[None, :], start[None, :], 0), axis=1)
    place = jnp.where(active, 2 * place + rank, -1)
    word = index | (src_tile << 9) | (dst_tile << 14) | (1 << 20)
    slot = jnp.arange(slots, dtype=jnp.int32)
    words = jnp.sum(jnp.where(place[None, :] == slot[:, None], word[None, :], 0), axis=1)
    zero = jnp.zeros((), jnp.int32)
    mirror_span = jnp.stack([zero, mirror_groups])
    hub_span = jnp.stack([mirror_groups, mirror_groups + hub_groups])
    return words, mirror_span, hub_span


def final_kernel(
    hub_ref,
    mirror_ref,
    master_ref,
    self_ref,
    x0_ref,
    x1_ref,
    x2_ref,
    x3_ref,
    mixed_ref,
    squares_ref,
    right,
    *,
    chunk,
):
    step = pl.program_id(0)
    owners = mirror_ref.shape[0]
    cols = mirror_ref.shape[2]
    slots = owners * TILE
    last_chunks = pl.num_programs(0)

    @pl.when(step == 0)
    def _():
        high = mirror_ref[:, TILE, :].astype(F32)
        low = mirror_ref[:, TILE + 1, :].astype(F32)
        pad = jnp.zeros((TILE - 2 * owners, TILE), F32)
        table = jnp.concatenate([high, low, pad], axis=0).T
        lane = lax.broadcasted_iota(jnp.int32, (TILE, TILE), 1)
        for p in range(owners):
            rows = slice(p * TILE, (p + 1) * TILE)
            right[rows, :cols] = mirror_ref[p, :TILE, :]
            keep = (lane == p) | (lane == p + owners)
            right[rows, cols:] = jnp.where(keep, table, 0.0).astype(BF)

    rows = pl.ds(pl.multiple_of(step * chunk, chunk), chunk)
    tile = jnp.concatenate(
        [x0_ref[rows, :], x1_ref[rows, :], x2_ref[rows, :], x3_ref[rows, :]], axis=1
    )
    own = jnp.dot(tile, self_ref[...], preferred_element_type=F32)
    entity = lax.broadcasted_iota(jnp.int32, (chunk, TILE), 0) + step * chunk
    hot = jnp.concatenate(
        [
            jnp.where(entity == master_ref[p : p + 1, :], 1.0, 0.0).astype(BF)
            for p in range(owners)
        ],
        axis=1,
    )
    sums = jnp.dot(hot, right[...], preferred_element_type=F32)
    degree = jnp.sum(sums[:, cols:], axis=1, keepdims=True)
    total = sums[:, :cols]
    scale = lax.rsqrt(jnp.maximum(degree, 1.0))
    mixed = own + total * scale
    mixed_ref[...] = mixed

    @pl.when(step == 0)
    def _():
        hub = jnp.sum(hub_ref[:, :TILE, :].astype(F32), axis=0)
        line = jnp.sum(
            hub_ref[:, TILE, :].astype(F32) + hub_ref[:, TILE + 1, :].astype(F32),
            axis=0,
            keepdims=True,
        )
        column = jnp.broadcast_to(line, (TILE, TILE)).T[:, :1]
        hub_scale = lax.rsqrt(jnp.maximum(column + degree[:TILE], 1.0))
        mixed_ref[:TILE, :] = own[:TILE] + (total[:TILE] + hub) * hub_scale

    value = mixed_ref[...]
    squares = jnp.sum(value * value, axis=1, keepdims=True)
    squares_ref[...] = jnp.broadcast_to(squares, (chunk, TILE)).T[:8, :]


def final(hub, mirror, master, self_weight, pieces):
    n_local, cols = pieces[0].shape
    owners = mirror.shape[0]
    chunk = 256
    whole = lambda shape: pl.BlockSpec(shape, lambda i: (0,) * len(shape))
    return pl.pallas_call(
        functools.partial(final_kernel, chunk=chunk),
        out_shape=(
            jax.ShapeDtypeStruct((n_local, cols), F32),
            jax.ShapeDtypeStruct((8, n_local), F32),
        ),
        grid=(n_local // chunk,),
        in_specs=[whole(hub.shape), whole(mirror.shape), whole(master.shape), whole(self_weight.shape)]
        + [whole(p.shape) for p in pieces],
        out_specs=(
            pl.BlockSpec((chunk, cols), lambda i: (i, 0)),
            pl.BlockSpec((8, chunk), lambda i: (0, i)),
        ),
        scratch_shapes=[pltpu.VMEM((owners * TILE, 2 * cols), BF)],
        compiler_params=pltpu.CompilerParams(vmem_limit_bytes=VMEM_LIMIT),
        name="final",
    )(hub, mirror, master, self_weight, *pieces)


def from_others(x, size):
    return [
        lax.ppermute(x, "feat", [((i + shift) % size, i) for i in range(size)])
        for shift in range(1, size)
    ]


def on_device(
    embeddings,
    self_weight,
    bases,
    basis_coef,
    out_gain,
    edge_src,
    edge_dst,
    block_rel,
    mirror_master_rows,
    block_count,
):
    owners = lax.axis_size("dom")
    feat_size = lax.axis_size("feat")
    feat = lax.axis_index("feat").astype(jnp.int32)
    blocks = edge_src.shape[0]
    n_local, cols = embeddings.shape
    n_bases, model_dim, _ = bases.shape
    relations = basis_coef.shape[0]

    pieces = [embeddings] + from_others(embeddings, feat_size)

    src_tile = edge_src[:, 0] // TILE
    dst_tile = edge_dst[:, 0] // TILE

    spread = 4
    relation = jnp.repeat(block_rel, spread)
    one_hot = (relation[:, None] == jnp.arange(relations)[None, :]).astype(BF)
    wide = jnp.concatenate([basis_coef] * spread, axis=1)
    lhs = jnp.dot(one_hot, wide, preferred_element_type=F32)
    line = lax.broadcasted_iota(jnp.int32, lhs.shape, 0) % spread
    group = lax.broadcasted_iota(jnp.int32, lhs.shape, 1) // n_bases
    lhs = jnp.where(line == group, lhs, 0.0).astype(BF)

    group_size = 16
    words, mirror_span, hub_span = arrange(
        src_tile, dst_tile, block_count[0], owners, n_local // TILE, group_size
    )
    weights = mix(feat.reshape(1), lhs, bases, blocks)
    edges = (edge_src, edge_dst)
    mirror_part = blocks_call(words, mirror_span, weights, *edges, pieces, owners, "mirror_blocks")
    mirror = lax.all_to_all(mirror_part, "dom", split_axis=0, concat_axis=0, tiled=True)
    weights, _ = lax.optimization_barrier((weights, mirror_part))
    hub_part = blocks_call(words, hub_span, weights, *edges, pieces, owners, "hub_blocks")
    hub = lax.all_to_all(hub_part, "dom", split_axis=0, concat_axis=0, tiled=True)

    turned = jnp.roll(self_weight, -feat * cols, axis=0)
    mixed, squares = final(hub, mirror, mirror_master_rows.reshape(owners, TILE), turned, pieces)
    line = squares[0].reshape(n_local // TILE, TILE)
    everyone = line
    for other in from_others(line, feat_size):
        everyone = everyone + other
    norm = lax.rsqrt(everyone.reshape(n_local) / model_dim + 1e-05)
    return (mixed * norm[:, None] * out_gain).astype(BF)


def solution(mesh):
    in_specs = (
        P("dom", "feat"),
        P(None, "feat"),
        P(None, None, "feat"),
        P(),
        P("feat"),
        P("dom", None),
        P("dom", None),
        P("dom"),
        P("dom"),
        P("dom"),
    )
    out_specs = P("dom", "feat")
    return jax.shard_map(
        on_device, mesh=mesh, in_specs=in_specs, out_specs=out_specs, check_vma=False
    )
```

```python
import functools

import jax
import jax.numpy as jnp
from jax import lax
from jax.experimental import pallas as pl
from jax.experimental.pallas import tpu as pltpu
from jax.sharding import PartitionSpec as P

TILE = 128
HUB_MIRRORS = 128
CAP = 128
DEG_ROWS = 16
VMEM_LIMIT = 56 * 1024 * 1024
BF = jnp.bfloat16
F32 = jnp.float32


def mix_kernel(feat_ref, lhs_ref, bases_ref, w_ref, spread, *, chunk):
    n_bases, depth, cols = bases_ref.shape
    spread[...] = bases_ref[...].astype(F32).reshape(n_bases * depth, cols)

    def rows_of(d):
        return spread[pl.ds(d, n_bases, stride=depth), :].astype(BF)

    rights = []
    for octet in range(depth // 8):
        halves = []
        for half in range(2):
            first = octet * 8 + half * 4
            halves.append(jnp.concatenate([rows_of(first + i) for i in range(4)], axis=0))
        rights.append(jnp.concatenate(halves, axis=1))
    pairs = chunk // 8
    low = lax.broadcasted_iota(jnp.int32, (pairs, 8, cols), 1) < 4

    def body(step, carry):
        row = pl.multiple_of(step * chunk, chunk)
        left = lhs_ref[pl.ds(row, chunk), :]
        evens, odds = [], []
        for right in rights:
            out = jnp.dot(left, right, preferred_element_type=F32)
            first = out[:, :cols].reshape(pairs, 8, cols)
            second = out[:, cols:].reshape(pairs, 8, cols)
            evens.append(jnp.where(low, first, pltpu.roll(second, 4, 1)))
            odds.append(jnp.where(low, pltpu.roll(first, 4, 1), second))
        pair = step * pairs
        w_ref[pl.ds(pair, pairs), 0] = jnp.concatenate(evens, axis=1).astype(BF)
        w_ref[pl.ds(pair, pairs), 1] = jnp.concatenate(odds, axis=1).astype(BF)
        return carry

    lax.fori_loop(0, lhs_ref.shape[0] // chunk, body, 0)


def mix(feat, lhs, bases, blocks):
    n_bases, model_dim, cols = bases.shape
    depth = 16
    steps = model_dim // depth
    per_part = cols // depth
    return pl.pallas_call(
        functools.partial(mix_kernel, chunk=2048),
        out_shape=jax.ShapeDtypeStruct((blocks // 2, 2, model_dim, cols), BF),
        grid_spec=pltpu.PrefetchScalarGridSpec(
            num_scalar_prefetch=1,
            grid=(steps,),
            in_specs=[
                pl.BlockSpec(lhs.shape, lambda i, f: (0, 0)),
                pl.BlockSpec(
                    (n_bases, depth, cols),
                    lambda i, f: (0, lax.rem(i + f[0] * per_part, steps), 0),
                ),
            ],
            out_specs=pl.BlockSpec((blocks // 2, 2, depth, cols), lambda i, f: (0, 0, i, 0)),
            scratch_shapes=[pltpu.VMEM((n_bases * depth, cols), F32)],
        ),
        compiler_params=pltpu.CompilerParams(vmem_limit_bytes=VMEM_LIMIT),
        name="mix",
    )(feat, lhs, bases)


def unpack(word):
    return word & 511, (word >> 9) & 31, (word >> 14) & 63, word >> 20


def blocks_kernel(*refs, group, owners, split, n_out):
    word_ref, span_ref, src_hbm, dst_hbm = refs[:4]
    piece_refs, w_ref = refs[4:8], refs[8]
    out_refs = refs[9 : 9 + n_out]
    acc, deg, held, src_ref, dst_ref, table, sems = refs[9 + n_out :]
    first_group, end_group = span_ref[0], span_ref[1]

    def fetch(at):
        side = at & 1
        for k in range(2 * group):
            block = word_ref[at * (2 * group) + k] & 511
            pltpu.make_async_copy(
                w_ref.at[block >> 1, block & 1], held.at[side, k // 2, k % 2], sems.at[side]
            ).start()

    @pl.when(first_group < end_group)
    def _():
        fetch(first_group)

    cols = table.shape[1] // len(piece_refs)
    loads = [
        pltpu.make_async_copy(src_hbm, src_ref, sems.at[2]),
        pltpu.make_async_copy(dst_hbm, dst_ref, sems.at[3]),
    ]
    for p, piece in enumerate(piece_refs):
        here = table.at[:, p * cols : (p + 1) * cols]
        loads.append(pltpu.make_async_copy(piece, here, sems.at[4 + p]))
    for load in loads:
        load.start()
    acc[...] = jnp.zeros_like(acc)
    deg[...] = jnp.zeros_like(deg)
    for load in loads:
        load.wait()

    def body(here, carry):
        side = here & 1

        @pl.when(here + 1 < end_group)
        def _():
            fetch(here + 1)

        pltpu.make_async_copy(w_ref.at[pl.ds(0, group)], held.at[side], sems.at[side]).wait()
        slot = lax.broadcasted_iota(jnp.int32, (TILE, TILE), 0).astype(F32).astype(BF)
        lane = lax.broadcasted_iota(jnp.int32, (TILE, TILE), 1)
        one = jnp.ones((TILE, TILE), BF)
        zero = jnp.zeros((TILE, TILE), BF)

        def diagonal(first, second):
            top = jnp.concatenate([first, zero], axis=1)
            bottom = jnp.concatenate([zero, second], axis=1)
            return jnp.concatenate([top, bottom], axis=0)

        def fields(pair, k):
            return unpack(word_ref[(here * group + pair) * 2 + k])

        def adjacency(pair):
            dst_hot, src_hot, count = [], [], None
            for k in range(2):
                block, src_tile, dst_tile, used = fields(pair, k)
                base = jnp.where(used > 0, dst_tile * TILE, 1 << 20)
                dst = (dst_ref[pl.ds(block, 1), :] - base).astype(F32).astype(BF)
                src = (src_ref[pl.ds(block, 1), :] - src_tile * TILE).astype(F32).astype(BF)
                dst_hot.append(jnp.where(slot == dst, one, zero))
                src_hot.append(jnp.where(slot == src, one, zero))
                column = jnp.sum(dst_hot[k].astype(F32), axis=1, keepdims=True)
                extra = jnp.where(lane == lax.rem(dst_tile, owners), column, 0.0)
                count = extra if count is None else count + extra
            found = lax.dot_general(
                jnp.concatenate(dst_hot, axis=1),
                diagonal(src_hot[0], src_hot[1]),
                (((1,), (1,)), ((), ())),
                preferred_element_type=F32,
            )
            return found.astype(BF), count

        def message(pair):
            src_tile = fields(pair, 0)[1]
            rows = pl.ds(pl.multiple_of(src_tile * TILE, TILE), TILE)
            tile = table[rows, :]
            weight = jnp.concatenate([held[side, pair, 0], held[side, pair, 1]], axis=1)
            out = jnp.dot(tile, weight, preferred_element_type=F32).astype(BF)
            return diagonal(out[:, :TILE], out[:, TILE:])

        total = deg[...]
        for first in range(0, group, split):
            pairs = range(first, first + split)
            found = [adjacency(pair) for pair in pairs]
            messages = [message(pair) for pair in pairs]
            sums = [
                jnp.dot(f[0], m, preferred_element_type=F32) for f, m in zip(found, messages)
            ]
            for pair, both, part in zip(pairs, sums, found):
                total = total + part[1]
                for k in range(2):
                    dst = lax.rem(fields(pair, k)[2], owners)
                    acc[dst] = acc[dst] + both[:, k * TILE : (k + 1) * TILE]
        deg[...] = total
        return carry

    lax.fori_loop(first_group, end_group, body, 0)

    deg[...] = deg[...].T
    line = lax.broadcasted_iota(jnp.int32, (DEG_ROWS, TILE), 0)
    core = span_ref[2]
    for part, out_ref in enumerate(out_refs):
        for i in range(owners // n_out):
            at = i if n_out == 1 else 2 * i + (core ^ part)
            degree = deg[pl.ds(at, 1), :]
            high = jnp.floor(degree * (1.0 / 256.0)) * 256.0
            low = degree - high
            out_ref[i, :TILE, :] = acc[at].astype(BF)
            rows = jnp.where(line == 0, high, jnp.where(line == 1, low, 0.0))
            out_ref[i, TILE:, :] = rows.astype(BF)


def blocks_call(
    words, span, weights, edge_src, edge_dst, pieces, owners, name, n_out, group=16, split=16
):
    _, _, model_dim, cols = weights.shape
    vmem = pl.BlockSpec(memory_space=pltpu.VMEM)
    smem = pl.BlockSpec(memory_space=pltpu.SMEM)
    anywhere = pl.BlockSpec(memory_space=pl.ANY)
    out = jax.ShapeDtypeStruct((owners // n_out, TILE + DEG_ROWS, cols), BF)
    pairs = 512 // 2 // n_out
    return pl.pallas_call(
        functools.partial(blocks_kernel, group=group, owners=owners, split=split, n_out=n_out),
        out_shape=(out,) * n_out,
        in_specs=[smem, smem] + [anywhere] * (3 + len(pieces)),
        out_specs=(vmem,) * n_out,
        scratch_shapes=[
            pltpu.VMEM((owners, TILE, cols), F32),
            pltpu.VMEM((TILE, TILE), F32),
            pltpu.VMEM((2, group, 2, model_dim, cols), BF),
            pltpu.VMEM(edge_src.shape, jnp.int32),
            pltpu.VMEM(edge_dst.shape, jnp.int32),
            pltpu.VMEM((pieces[0].shape[0], model_dim), BF),
            pltpu.SemaphoreType.DMA((4 + len(pieces),)),
        ],
        cost_estimate=pl.CostEstimate(
            flops=pairs * 2 * TILE * model_dim * cols * 4,
            bytes_accessed=pairs * 2 * model_dim * cols * 2,
            transcendentals=0,
        ),
        compiler_params=pltpu.CompilerParams(vmem_limit_bytes=VMEM_LIMIT),
        name=name,
    )(words, span, edge_src, edge_dst, *pieces, weights)


def arrange(src_tile, dst_tile, live, core, owners, src_tiles, group):
    blocks = src_tile.shape[0]
    keys = 2 * src_tiles
    slots = 2 * group * (-(-(blocks + keys) // (2 * group)) + 1)
    index = jnp.arange(blocks, dtype=jnp.int32)
    key_range = jnp.arange(keys, dtype=jnp.int32)
    active = index < live
    key = jnp.where(active, jnp.where(dst_tile < owners, src_tiles, 0) + src_tile, keys)
    count = jnp.sum((key[None, :] == key_range[:, None]).astype(jnp.int32), axis=1)
    pairs = (count + 1) >> 1
    start = jnp.sum(jnp.where(key_range[None, :] < key_range[:, None], pairs[None, :], 0), axis=1)
    mirror_pairs = jnp.sum(pairs[:src_tiles])
    hub_pairs = jnp.sum(pairs[src_tiles:])
    mirror_groups = (mirror_pairs + group - 1) // group
    hub_groups = (hub_pairs + group - 1) // group
    start = start + jnp.where(key_range >= src_tiles, mirror_groups * group - mirror_pairs, 0)
    before = (key[None, :] == key[:, None]) & (index[None, :] < index[:, None])
    rank = jnp.sum(before.astype(jnp.int32), axis=1)
    place = jnp.sum(jnp.where(key[:, None] == key_range[None, :], start[None, :], 0), axis=1)
    place = jnp.where(active, 2 * place + rank, -1)
    word = index | (src_tile << 9) | (dst_tile << 14) | (1 << 20)
    slot = jnp.arange(slots, dtype=jnp.int32)
    words = jnp.sum(jnp.where(place[None, :] == slot[:, None], word[None, :], 0), axis=1)
    zero = jnp.zeros((), jnp.int32)
    mirror_span = jnp.stack([zero, mirror_groups, core])
    hub_span = jnp.stack([mirror_groups, mirror_groups + hub_groups, core])
    return words, mirror_span, hub_span


def square_lines(value):
    squares = jnp.sum(value * value, axis=1, keepdims=True)
    line = jnp.broadcast_to(squares, value.shape).T[:1, :]
    pieces = [line[:, i : i + TILE] for i in range(0, value.shape[0], TILE)]
    return jnp.concatenate(pieces, axis=0)


def mirror_kernel(
    feat_ref,
    mirror_ref,
    master_ref,
    self_ref,
    x0_ref,
    x1_ref,
    x2_ref,
    x3_ref,
    mixed_ref,
    squares_ref,
    right,
    turned,
    *,
    chunk,
    reach,
):
    step = pl.program_id(0)
    owners = mirror_ref.shape[0]
    cols = mirror_ref.shape[2]

    @pl.when(step == 0)
    def _():
        for p in range(4):
            at = pl.multiple_of(lax.rem(feat_ref[0] + p, 4) * cols, cols)
            turned[p * cols : (p + 1) * cols, :] = self_ref[pl.ds(at, cols), :]
        high = mirror_ref[:, TILE, :].astype(F32)
        low = mirror_ref[:, TILE + 1, :].astype(F32)
        pad = jnp.zeros((TILE - 2 * owners, TILE), F32)
        table = jnp.concatenate([high, low, pad], axis=0).T
        lane = lax.broadcasted_iota(jnp.int32, (TILE, TILE), 1)
        for p in range(owners):
            rows = slice(p * TILE, (p + 1) * TILE)
            right[rows, :cols] = mirror_ref[p, :TILE, :]
            keep = (lane == p) | (lane == p + owners)
            right[rows, cols:] = jnp.where(keep, table, 0.0).astype(BF)

    rows = pl.ds(pl.multiple_of(step * chunk, chunk), chunk)
    tile = jnp.concatenate(
        [x0_ref[rows, :], x1_ref[rows, :], x2_ref[rows, :], x3_ref[rows, :]], axis=1
    )
    own = jnp.dot(tile, turned[...], preferred_element_type=F32)

    @pl.when(step * chunk < reach)
    def _():
        local = lax.broadcasted_iota(jnp.int32, (TILE, TILE), 0).astype(F32).astype(BF)
        one = jnp.ones((TILE, TILE), BF)
        zero = jnp.zeros((TILE, TILE), BF)
        columns = []
        for p in range(owners):
            column = []
            for first in range(0, chunk, TILE):
                target = master_ref[p : p + 1, :] - (step * chunk + first)
                column.append(jnp.where(local == target.astype(F32).astype(BF), one, zero))
            columns.append(jnp.concatenate(column, axis=0))
        sums = jnp.dot(jnp.concatenate(columns, axis=1), right[...], preferred_element_type=F32)
        degree = jnp.sum(sums[:, cols:], axis=1, keepdims=True)
        mixed = own + sums[:, :cols] * lax.rsqrt(jnp.maximum(degree, 1.0))
        mixed_ref[...] = mixed
        squares_ref[0] = square_lines(mixed)

    @pl.when(step * chunk >= reach)
    def _():
        mixed_ref[...] = own
        squares_ref[0] = square_lines(own)


def mirror_final(feat, mirror, master, self_weight, pieces):
    n_local, cols = pieces[0].shape
    owners = mirror.shape[0]
    chunk = 512
    whole = lambda shape: pl.BlockSpec(shape, lambda i, *_: (0,) * len(shape))
    return pl.pallas_call(
        functools.partial(mirror_kernel, chunk=chunk, reach=n_local - n_local // 4),
        out_shape=(
            jax.ShapeDtypeStruct((n_local, cols), F32),
            jax.ShapeDtypeStruct((n_local // chunk, chunk // TILE, TILE), F32),
        ),
        grid_spec=pltpu.PrefetchScalarGridSpec(
            num_scalar_prefetch=1,
            grid=(n_local // chunk,),
            in_specs=[whole(mirror.shape), whole(master.shape), whole(self_weight.shape)]
            + [whole(p.shape) for p in pieces],
            out_specs=(
                pl.BlockSpec((chunk, cols), lambda i, *_: (i, 0)),
                pl.BlockSpec((1, chunk // TILE, TILE), lambda i, *_: (i, 0, 0)),
            ),
            scratch_shapes=[
                pltpu.VMEM((owners * TILE, 2 * cols), BF),
                pltpu.VMEM(self_weight.shape, BF),
            ],
        ),
        cost_estimate=pl.CostEstimate(
            flops=n_local * n_local * 4 * cols, bytes_accessed=8 << 20, transcendentals=0
        ),
        compiler_params=pltpu.CompilerParams(vmem_limit_bytes=VMEM_LIMIT),
        name="mirror_final",
    )(feat, mirror, master, self_weight, *pieces)


def hub_kernel(hub_ref, mixed_ref, squares_ref, out_ref, lines_ref):
    hub = jnp.sum(hub_ref[:, :TILE, :].astype(F32), axis=0)
    counts = hub_ref[:, TILE : TILE + DEG_ROWS, :].astype(F32)
    line = jnp.sum(jnp.sum(counts, axis=0), axis=0, keepdims=True)
    column = jnp.broadcast_to(line, (TILE, TILE)).T[:, :1]
    mixed = mixed_ref[...] + hub * lax.rsqrt(jnp.maximum(column, 1.0))
    out_ref[...] = mixed
    lines_ref[...] = squares_ref[...]
    lines_ref[0, :1, :] = square_lines(mixed)


def hub_final(hub, mixed, squares):
    cols = mixed.shape[1]
    hub_block = pl.BlockSpec(hub.shape, lambda i: (0, 0, 0))
    mixed_block = pl.BlockSpec((HUB_MIRRORS, cols), lambda i: (0, 0))
    line_block = pl.BlockSpec((1,) + squares.shape[1:], lambda i: (0, 0, 0))
    return pl.pallas_call(
        hub_kernel,
        out_shape=(
            jax.ShapeDtypeStruct(mixed.shape, mixed.dtype),
            jax.ShapeDtypeStruct(squares.shape, squares.dtype),
        ),
        grid=(1,),
        in_specs=[hub_block, mixed_block, line_block],
        out_specs=(mixed_block, line_block),
        input_output_aliases={1: 0, 2: 1},
        name="hub_final",
    )(hub, mixed, squares)


def from_others(x, size):
    return [
        lax.ppermute(x, "feat", [((i + shift) % size, i) for i in range(size)])
        for shift in range(1, size)
    ]


def on_device(
    embeddings,
    self_weight,
    bases,
    basis_coef,
    out_gain,
    edge_src,
    edge_dst,
    block_rel,
    mirror_master_rows,
    block_count,
):
    owners = lax.axis_size("dom")
    feat_size = lax.axis_size("feat")
    feat = lax.axis_index("feat").astype(jnp.int32)
    blocks = edge_src.shape[0]
    n_local, cols = embeddings.shape
    n_bases, model_dim, _ = bases.shape
    relations = basis_coef.shape[0]

    pieces = [embeddings] + from_others(embeddings, feat_size)

    src_tile = edge_src[:, 0] // TILE
    dst_tile = edge_dst[:, 0] // TILE

    spread = 4
    relation = jnp.repeat(block_rel, spread)
    one_hot = (relation[:, None] == jnp.arange(relations)[None, :]).astype(BF)
    wide = jnp.concatenate([basis_coef] * spread, axis=1)
    lhs = jnp.dot(one_hot, wide, preferred_element_type=F32)
    line = lax.broadcasted_iota(jnp.int32, lhs.shape, 0) % spread
    group = lax.broadcasted_iota(jnp.int32, lhs.shape, 1) // n_bases
    lhs = jnp.where(line == group, lhs, 0.0).astype(BF)

    group_size = 16
    device = lax.axis_index("dom").astype(jnp.int32)
    words, mirror_span, hub_span = arrange(
        src_tile, dst_tile, block_count[0], device & 1, owners, n_local // TILE, group_size
    )
    weights = mix(feat.reshape(1), lhs, bases, blocks)
    edges = (edge_src, edge_dst)
    (mirror_part,) = blocks_call(
        words, mirror_span, weights, *edges, pieces, owners, "mirror_blocks", 1
    )
    mirror = lax.all_to_all(mirror_part, "dom", split_axis=0, concat_axis=0, tiled=True)
    weights, _ = lax.optimization_barrier((weights, mirror_part))
    kept, sent = blocks_call(words, hub_span, weights, *edges, pieces, owners, "hub_blocks", 2)
    came = lax.ppermute(sent, "dom", [(i, i ^ 1) for i in range(owners)])
    hub_part = (kept.astype(F32) + came.astype(F32)).astype(BF)
    hub_part, mirror = lax.optimization_barrier((hub_part, mirror))
    hub = lax.all_to_all(
        hub_part,
        "dom",
        split_axis=0,
        concat_axis=0,
        tiled=True,
        axis_index_groups=[list(range(c, owners, 2)) for c in range(2)],
    )

    mixed, squares = mirror_final(
        feat.reshape(1), mirror, mirror_master_rows.reshape(owners, TILE), self_weight, pieces
    )
    mixed, squares = hub_final(hub, mixed, squares)
    line = squares.reshape(n_local // TILE, TILE)
    everyone = line
    for other in from_others(line, feat_size):
        everyone = everyone + other
    norm = lax.rsqrt(everyone.reshape(n_local) / model_dim + 1e-05)
    return (mixed * norm[:, None] * out_gain).astype(BF)


def solution(mesh):
    in_specs = (
        P("dom", "feat"),
        P(None, "feat"),
        P(None, None, "feat"),
        P(),
        P("feat"),
        P("dom", None),
        P("dom", None),
        P("dom"),
        P("dom"),
        P("dom"),
    )
    out_specs = P("dom", "feat")
    return jax.shard_map(
        on_device, mesh=mesh, in_specs=in_specs, out_specs=out_specs, check_vma=False
    )
```

```python
import functools

import jax
import jax.numpy as jnp
from jax import lax
from jax.experimental import pallas as pl
from jax.experimental.pallas import tpu as pltpu
from jax.sharding import PartitionSpec as P

TILE = 128
HUB_MIRRORS = 128
CAP = 128
DEG_ROWS = 16
VMEM_LIMIT = 56 * 1024 * 1024
BF = jnp.bfloat16
F32 = jnp.float32
HOT = jnp.float8_e4m3fn


def prepare_kernel(
    live_ref, src_ref, dst_ref, rel_ref, coef_ref, words_ref, lhs_ref, spread, *, owners, src_tiles, group
):
    blocks = src_ref.shape[0]
    relations, n_bases = coef_ref.shape
    live = live_ref[0]
    src_tile = src_ref[:, :1] >> 7
    dst_tile = dst_ref[:, :1] >> 7
    index = lax.broadcasted_iota(jnp.int32, (blocks, 1), 0)
    active = index < live
    key = jnp.where(dst_tile < owners, src_tiles, 0) + src_tile
    key = jnp.where(active, key, TILE - 1)
    key_wide = jnp.broadcast_to(key, (blocks, TILE))
    key_row = key_wide.astype(F32).T[:1, :]
    lane = lax.broadcasted_iota(jnp.int32, (1, TILE), 1)
    same_key = key_wide == lane
    count = jnp.sum(same_key.astype(F32), axis=0, keepdims=True)
    count = jnp.where(lane < 2 * src_tiles, count, 0.0).astype(jnp.int32)
    pairs = (count + 1) >> 1
    earlier = lax.broadcasted_iota(jnp.int32, (TILE, TILE), 0) < lax.broadcasted_iota(
        jnp.int32, (TILE, TILE), 1
    )
    pairs_wide = jnp.broadcast_to(pairs, (8, TILE)).astype(F32).astype(BF)
    start = jnp.dot(
        pairs_wide, jnp.where(earlier, 1.0, 0.0).astype(BF), preferred_element_type=F32
    )[:1].astype(jnp.int32)
    zero = jnp.zeros_like(pairs)
    mirror_pairs = jnp.sum(
        jnp.where(lane < src_tiles, pairs, zero).astype(F32), axis=1, keepdims=True
    ).astype(jnp.int32)
    hub_pairs = jnp.sum(
        jnp.where(lane >= src_tiles, pairs, zero).astype(F32), axis=1, keepdims=True
    ).astype(jnp.int32)
    shift = group.bit_length() - 1
    mirror_groups = (mirror_pairs + group - 1) >> shift
    hub_groups = (hub_pairs + group - 1) >> shift
    start = start + jnp.where(lane >= src_tiles, mirror_groups * group - mirror_pairs, 0)
    other = lax.broadcasted_iota(jnp.int32, (1, blocks), 1)
    before = (key.astype(F32) == key_row) & (other < index)
    rank = jnp.sum(before.astype(F32), axis=1, keepdims=True).astype(jnp.int32)
    first = jnp.sum(
        jnp.where(same_key, start, 0).astype(F32), axis=1, keepdims=True
    ).astype(jnp.int32)
    place = jnp.where(active, 2 * first + rank, -1)
    word = index | (src_tile << 9) | (dst_tile << 14) | (1 << 20)
    slots = words_ref.shape[1] - TILE
    slot = lax.broadcasted_iota(jnp.int32, (1, slots), 1)
    words_ref[:, :slots] = jnp.sum(jnp.where(place == slot, word, 0), axis=0, keepdims=True)
    words_ref[:, slots:] = jnp.where(
        lane == 0, mirror_groups, jnp.where(lane == 1, mirror_groups + hub_groups, 0)
    )

    rel_wide = jnp.broadcast_to(rel_ref[...].astype(F32), (TILE, blocks)).T[:, :1]
    relation = rel_wide.astype(jnp.int32)
    span = lax.broadcasted_iota(jnp.int32, (1, relations), 1)
    one_hot = jnp.where(relation == span, 1.0, 0.0).astype(BF)
    mixing = jnp.dot(one_hot, coef_ref[...], preferred_element_type=F32)
    copies = lhs_ref.shape[1] // n_bases
    blank = jnp.zeros_like(mixing)
    for i in range(copies):
        row = jnp.concatenate([mixing if k == i else blank for k in range(copies)], axis=1)
        for half in range(copies * n_bases // TILE):
            spread[half, pl.ds(i, blocks, stride=copies), :] = row[:, half * TILE : (half + 1) * TILE]
    for half in range(copies * n_bases // TILE):
        lhs_ref[:, half * TILE : (half + 1) * TILE] = spread[half].astype(BF)


def prepare(live, edge_src, edge_dst, block_rel, basis_coef, owners, src_tiles, group):
    blocks = edge_src.shape[0]
    n_bases = basis_coef.shape[1]
    slots = 2 * group * (-(-(blocks + 2 * src_tiles) // (2 * group)) + 1)
    slots = -(-slots // TILE) * TILE
    vmem = pl.BlockSpec(memory_space=pltpu.VMEM)
    return pl.pallas_call(
        functools.partial(prepare_kernel, owners=owners, src_tiles=src_tiles, group=group),
        out_shape=(
            jax.ShapeDtypeStruct((1, slots + TILE), jnp.int32),
            jax.ShapeDtypeStruct((4 * blocks, 4 * n_bases), BF),
        ),
        in_specs=[pl.BlockSpec(memory_space=pltpu.SMEM)] + [vmem] * 4,
        out_specs=(vmem, vmem),
        scratch_shapes=[pltpu.VMEM((4 * n_bases // TILE, 4 * blocks, TILE), F32)],
        compiler_params=pltpu.CompilerParams(vmem_limit_bytes=VMEM_LIMIT),
        name="prepare",
    )(live, edge_src, edge_dst, block_rel.reshape(1, blocks), basis_coef)


def mix_kernel(feat_ref, lhs_ref, bases_ref, w_ref, spread, rights, *, chunk):
    n_bases, depth, cols = bases_ref.shape
    side = pl.program_id(0) & 1
    spread[...] = bases_ref[...].astype(F32).reshape(n_bases * depth, cols)
    for d in range(depth):
        octet, half, row = d // 8, d % 8 // 4, d % 4
        rows = slice(row * n_bases, (row + 1) * n_bases)
        rights[side, octet, rows, half * cols : (half + 1) * cols] = spread[
            pl.ds(d, n_bases, stride=depth), :
        ].astype(BF)
    pairs = chunk // 8
    low = lax.broadcasted_iota(jnp.int32, (pairs, 8, cols), 1) < 4
    for row in range(0, lhs_ref.shape[0], chunk):
        left = lhs_ref[row : row + chunk, :]
        pair = row // 8
        for first_octet in range(0, depth // 8, 2):
            evens, odds = [], []
            for octet in (first_octet, first_octet + 1):
                out = jnp.dot(left, rights[1 - side, octet], preferred_element_type=F32)
                first = out[:, :cols].reshape(pairs, 8, cols)
                second = out[:, cols:].reshape(pairs, 8, cols)
                evens.append(jnp.where(low, first, pltpu.roll(second, 4, 1)))
                odds.append(jnp.where(low, pltpu.roll(first, 4, 1), second))
            at = slice(first_octet * 8, first_octet * 8 + 16)
            w_ref[pair : pair + pairs, 0, at] = jnp.concatenate(evens, axis=1).astype(BF)
            w_ref[pair : pair + pairs, 1, at] = jnp.concatenate(odds, axis=1).astype(BF)


def mix(feat, lhs, bases, blocks):
    n_bases, model_dim, cols = bases.shape
    depth = 32
    steps = model_dim // depth
    per_part = cols // depth

    def bases_at(i, f):
        return (0, lax.rem(jnp.minimum(i, steps - 1) + f[0] * per_part, steps), 0)

    return pl.pallas_call(
        functools.partial(mix_kernel, chunk=512),
        out_shape=jax.ShapeDtypeStruct((blocks // 2, 2, model_dim, cols), BF),
        grid_spec=pltpu.PrefetchScalarGridSpec(
            num_scalar_prefetch=1,
            grid=(steps + 1,),
            in_specs=[
                pl.BlockSpec(lhs.shape, lambda i, f: (0, 0)),
                pl.BlockSpec((n_bases, depth, cols), bases_at),
            ],
            out_specs=pl.BlockSpec(
                (blocks // 2, 2, depth, cols), lambda i, f: (0, 0, jnp.maximum(i - 1, 0), 0)
            ),
            scratch_shapes=[
                pltpu.VMEM((n_bases * depth, cols), F32),
                pltpu.VMEM((2, depth // 8, 4 * n_bases, 2 * cols), BF),
            ],
        ),
        cost_estimate=pl.CostEstimate(
            flops=8 * blocks * n_bases * model_dim * cols,
            bytes_accessed=blocks * model_dim * cols * 2,
            transcendentals=0,
        ),
        compiler_params=pltpu.CompilerParams(vmem_limit_bytes=VMEM_LIMIT),
        name="mix",
    )(feat, lhs, bases)


def unpack(word):
    return word & 511, (word >> 9) & 31, (word >> 14) & 63, word >> 20


def blocks_kernel(*refs, group, owners, split, hubs):
    word_ref, src_ref, dst_ref = refs[:3]
    piece_refs, w_ref, out_ref = refs[3:7], refs[7], refs[8]
    acc, deg, held, table, sems = refs[9:]
    spans = word_ref.shape[1] - TILE
    first_group = word_ref[0, spans] if hubs else 0
    end_group = word_ref[0, spans + int(hubs)]

    def fetch(at):
        side = at & 1
        for k in range(2 * group):
            block = word_ref[0, at * (2 * group) + k] & 511
            pltpu.make_async_copy(
                w_ref.at[block >> 1, block & 1], held.at[side, k // 2, k % 2], sems.at[side]
            ).start()

    @pl.when(first_group < end_group)
    def _():
        fetch(first_group)

    cols = table.shape[1] // len(piece_refs)
    loads = []
    for p, piece in enumerate(piece_refs):
        here = table.at[:, p * cols : (p + 1) * cols]
        loads.append(pltpu.make_async_copy(piece, here, sems.at[2 + p]))
    for load in loads:
        load.start()
    acc[...] = jnp.zeros_like(acc)
    deg[...] = jnp.zeros_like(deg)
    for load in loads:
        load.wait()

    def body(here, carry):
        side = here & 1

        @pl.when(here + 1 < end_group)
        def _():
            fetch(here + 1)

        pltpu.make_async_copy(w_ref.at[pl.ds(0, group)], held.at[side], sems.at[side]).wait()
        slot = lax.broadcasted_iota(jnp.int32, (TILE, TILE), 0).astype(F32).astype(BF)
        lane = lax.broadcasted_iota(jnp.int32, (TILE, TILE), 1)
        one = jnp.ones((TILE, TILE), BF)
        zero = jnp.zeros((TILE, TILE), BF)

        def diagonal(first, second):
            top = jnp.concatenate([first, zero], axis=1)
            bottom = jnp.concatenate([zero, second], axis=1)
            return jnp.concatenate([top, bottom], axis=0)

        def fields(pair, k):
            return unpack(word_ref[0, (here * group + pair) * 2 + k])

        def adjacency(pair):
            dst_hot, src_hot, count = [], [], None
            for k in range(2):
                block, src_tile, dst_tile, used = fields(pair, k)
                base = jnp.where(used > 0, dst_tile * TILE, 1 << 20)
                dst = (dst_ref[pl.ds(block, 1), :] - base).astype(F32).astype(BF)
                src = (src_ref[pl.ds(block, 1), :] - src_tile * TILE).astype(F32).astype(BF)
                dst_hot.append(jnp.where(slot == dst, one, zero))
                src_hot.append(jnp.where(slot == src, one, zero))
                column = jnp.sum(dst_hot[k].astype(F32), axis=1, keepdims=True)
                extra = jnp.where(lane == lax.rem(dst_tile, owners), column, 0.0)
                count = extra if count is None else count + extra
            found = lax.dot_general(
                jnp.concatenate(dst_hot, axis=1).astype(HOT),
                diagonal(src_hot[0], src_hot[1]).astype(HOT),
                (((1,), (1,)), ((), ())),
                preferred_element_type=F32,
            )
            return found.astype(BF), count

        def message(pair):
            src_tile = fields(pair, 0)[1]
            rows = pl.ds(pl.multiple_of(src_tile * TILE, TILE), TILE)
            tile = table[rows, :]
            weight = jnp.concatenate([held[side, pair, 0], held[side, pair, 1]], axis=1)
            out = jnp.dot(tile, weight, preferred_element_type=F32).astype(BF)
            return diagonal(out[:, :TILE], out[:, TILE:])

        total = deg[...]
        for first in range(0, group, split):
            pairs = range(first, first + split)
            found = [adjacency(pair) for pair in pairs]
            messages = [message(pair) for pair in pairs]
            sums = [
                jnp.dot(f[0], m, preferred_element_type=F32) for f, m in zip(found, messages)
            ]
            for pair, both, part in zip(pairs, sums, found):
                total = total + part[1]
                for k in range(2):
                    dst = lax.rem(fields(pair, k)[2], owners)
                    acc[dst] = acc[dst] + both[:, k * TILE : (k + 1) * TILE]
        deg[...] = total
        return carry

    lax.fori_loop(first_group, end_group, body, 0)

    deg[...] = deg[...].T
    line = lax.broadcasted_iota(jnp.int32, (DEG_ROWS, TILE), 0)
    for at in range(owners):
        degree = deg[at : at + 1, :]
        high = jnp.floor(degree * (1.0 / 256.0)) * 256.0
        low = degree - high
        out_ref[at, :TILE, :] = acc[at].astype(BF)
        rows = jnp.where(line == 0, high, jnp.where(line == 1, low, 0.0))
        out_ref[at, TILE:, :] = rows.astype(BF)


def blocks_call(words, weights, edge_src, edge_dst, pieces, owners, hubs, group=16, split=16):
    pair_count, _, model_dim, cols = weights.shape
    vmem = pl.BlockSpec(memory_space=pltpu.VMEM)
    smem = pl.BlockSpec(memory_space=pltpu.SMEM)
    anywhere = pl.BlockSpec(memory_space=pl.ANY)
    return pl.pallas_call(
        functools.partial(blocks_kernel, group=group, owners=owners, split=split, hubs=hubs),
        out_shape=jax.ShapeDtypeStruct((owners, TILE + DEG_ROWS, cols), BF),
        in_specs=[smem, vmem, vmem] + [anywhere] * (1 + len(pieces)),
        out_specs=vmem,
        scratch_shapes=[
            pltpu.VMEM((owners, TILE, cols), F32),
            pltpu.VMEM((TILE, TILE), F32),
            pltpu.VMEM((2, group, 2, model_dim, cols), BF),
            pltpu.VMEM((pieces[0].shape[0], model_dim), BF),
            pltpu.SemaphoreType.DMA((2 + len(pieces),)),
        ],
        cost_estimate=pl.CostEstimate(
            flops=pair_count * 4 * TILE * model_dim * cols,
            bytes_accessed=pair_count * model_dim * cols * 2,
            transcendentals=0,
        ),
        compiler_params=pltpu.CompilerParams(vmem_limit_bytes=VMEM_LIMIT),
        name="hub_blocks" if hubs else "mirror_blocks",
    )(words, edge_src, edge_dst, *pieces, weights)


def square_lines(value):
    squares = jnp.sum(value * value, axis=1, keepdims=True)
    line = jnp.broadcast_to(squares, value.shape).T[:1, :]
    pieces = [line[:, i : i + TILE] for i in range(0, value.shape[0], TILE)]
    return jnp.concatenate(pieces, axis=0)


def mirror_kernel(
    feat_ref,
    mirror_ref,
    master_ref,
    self_ref,
    x0_ref,
    x1_ref,
    x2_ref,
    x3_ref,
    mixed_ref,
    squares_ref,
    right,
    turned,
    *,
    chunk,
    reach,
):
    step = pl.program_id(0)
    owners = mirror_ref.shape[0]
    cols = mirror_ref.shape[2]

    @pl.when(step == 0)
    def _():
        for p in range(4):
            at = pl.multiple_of(lax.rem(feat_ref[0] + p, 4) * cols, cols)
            turned[p * cols : (p + 1) * cols, :] = self_ref[pl.ds(at, cols), :]
        high = mirror_ref[:, TILE, :].astype(F32)
        low = mirror_ref[:, TILE + 1, :].astype(F32)
        pad = jnp.zeros((TILE - 2 * owners, TILE), F32)
        table = jnp.concatenate([high, low, pad], axis=0).T
        lane = lax.broadcasted_iota(jnp.int32, (TILE, TILE), 1)
        for p in range(owners):
            rows = slice(p * TILE, (p + 1) * TILE)
            right[rows, :cols] = mirror_ref[p, :TILE, :]
            keep = (lane == p) | (lane == p + owners)
            right[rows, cols:] = jnp.where(keep, table, 0.0).astype(BF)

    rows = pl.ds(pl.multiple_of(step * chunk, chunk), chunk)
    tile = jnp.concatenate(
        [x0_ref[rows, :], x1_ref[rows, :], x2_ref[rows, :], x3_ref[rows, :]], axis=1
    )
    own = jnp.dot(tile, turned[...], preferred_element_type=F32)

    @pl.when(step * chunk < reach)
    def _():
        local = lax.broadcasted_iota(jnp.int32, (TILE, TILE), 0).astype(F32).astype(BF)
        one = jnp.ones((TILE, TILE), BF)
        zero = jnp.zeros((TILE, TILE), BF)
        columns = []
        for p in range(owners):
            column = []
            for first in range(0, chunk, TILE):
                target = master_ref[p : p + 1, :] - (step * chunk + first)
                column.append(jnp.where(local == target.astype(F32).astype(BF), one, zero))
            columns.append(jnp.concatenate(column, axis=0))
        sums = jnp.dot(jnp.concatenate(columns, axis=1), right[...], preferred_element_type=F32)
        degree = jnp.sum(sums[:, cols:], axis=1, keepdims=True)
        mixed = own + sums[:, :cols] * lax.rsqrt(jnp.maximum(degree, 1.0))
        mixed_ref[...] = mixed
        squares_ref[0] = square_lines(mixed)

    @pl.when(step * chunk >= reach)
    def _():
        mixed_ref[...] = own
        squares_ref[0] = square_lines(own)


def mirror_final(feat, mirror, master, self_weight, pieces):
    n_local, cols = pieces[0].shape
    owners = mirror.shape[0]
    chunk = 1024
    whole = lambda shape: pl.BlockSpec(shape, lambda i, *_: (0,) * len(shape))
    return pl.pallas_call(
        functools.partial(mirror_kernel, chunk=chunk, reach=n_local - n_local // 4),
        out_shape=(
            jax.ShapeDtypeStruct((n_local, cols), F32),
            jax.ShapeDtypeStruct((n_local // chunk, chunk // TILE, TILE), F32),
        ),
        grid_spec=pltpu.PrefetchScalarGridSpec(
            num_scalar_prefetch=1,
            grid=(n_local // chunk,),
            in_specs=[whole(mirror.shape), whole(master.shape), whole(self_weight.shape)]
            + [whole(p.shape) for p in pieces],
            out_specs=(
                pl.BlockSpec((chunk, cols), lambda i, *_: (i, 0)),
                pl.BlockSpec((1, chunk // TILE, TILE), lambda i, *_: (i, 0, 0)),
            ),
            scratch_shapes=[
                pltpu.VMEM((owners * TILE, 2 * cols), BF),
                pltpu.VMEM(self_weight.shape, BF),
            ],
        ),
        cost_estimate=pl.CostEstimate(
            flops=n_local * n_local * 4 * cols, bytes_accessed=8 << 20, transcendentals=0
        ),
        compiler_params=pltpu.CompilerParams(vmem_limit_bytes=VMEM_LIMIT),
        name="mirror_final",
    )(feat, mirror, master, self_weight, *pieces)


def hub_kernel(hub_ref, mixed_ref, squares_ref, out_ref, lines_ref):
    hub = jnp.sum(hub_ref[:, :TILE, :].astype(F32), axis=0)
    counts = hub_ref[:, TILE : TILE + DEG_ROWS, :].astype(F32)
    line = jnp.sum(jnp.sum(counts, axis=0), axis=0, keepdims=True)
    column = jnp.broadcast_to(line, (TILE, TILE)).T[:, :1]
    mixed = mixed_ref[...] + hub * lax.rsqrt(jnp.maximum(column, 1.0))
    out_ref[...] = mixed
    lines_ref[...] = squares_ref[...]
    lines_ref[0, :1, :] = square_lines(mixed)


def hub_final(hub, mixed, squares):
    cols = mixed.shape[1]
    hub_block = pl.BlockSpec(hub.shape, lambda i: (0, 0, 0))
    mixed_block = pl.BlockSpec((HUB_MIRRORS, cols), lambda i: (0, 0))
    line_block = pl.BlockSpec((1,) + squares.shape[1:], lambda i: (0, 0, 0))
    return pl.pallas_call(
        hub_kernel,
        out_shape=(
            jax.ShapeDtypeStruct(mixed.shape, mixed.dtype),
            jax.ShapeDtypeStruct(squares.shape, squares.dtype),
        ),
        grid=(1,),
        in_specs=[hub_block, mixed_block, line_block],
        out_specs=(mixed_block, line_block),
        input_output_aliases={1: 0, 2: 1},
        name="hub_final",
    )(hub, mixed, squares)


def from_others(x, size):
    return [
        lax.ppermute(x, "feat", [((i + shift) % size, i) for i in range(size)])
        for shift in range(1, size)
    ]


def on_device(
    embeddings,
    self_weight,
    bases,
    basis_coef,
    out_gain,
    edge_src,
    edge_dst,
    block_rel,
    mirror_master_rows,
    block_count,
):
    owners = lax.axis_size("dom")
    feat_size = lax.axis_size("feat")
    feat = lax.axis_index("feat").astype(jnp.int32)
    blocks = edge_src.shape[0]
    n_local, cols = embeddings.shape
    model_dim = bases.shape[1]
    pieces = [embeddings] + from_others(embeddings, feat_size)
    words, lhs = prepare(
        block_count, edge_src, edge_dst, block_rel, basis_coef, owners, n_local // TILE, 16
    )
    weights = mix(feat.reshape(1), lhs, bases, blocks)
    edges = (edge_src, edge_dst)
    mirror_part = blocks_call(words, weights, *edges, pieces, owners, False)
    mirror = lax.all_to_all(mirror_part, "dom", split_axis=0, concat_axis=0, tiled=True)
    weights, _ = lax.optimization_barrier((weights, mirror_part))
    hub_part = blocks_call(words, weights, *edges, pieces, owners, True)
    hub_part, mirror = lax.optimization_barrier((hub_part, mirror))
    hub = lax.all_to_all(hub_part, "dom", split_axis=0, concat_axis=0, tiled=True)

    mixed, squares = mirror_final(
        feat.reshape(1), mirror, mirror_master_rows.reshape(owners, TILE), self_weight, pieces
    )
    mixed, squares = hub_final(hub, mixed, squares)
    line = squares.reshape(n_local // TILE, TILE)
    everyone = line
    for other in from_others(line, feat_size):
        everyone = everyone + other
    norm = lax.rsqrt(everyone.reshape(n_local) / model_dim + 1e-05)
    return (mixed * norm[:, None] * out_gain).astype(BF)


def solution(mesh):
    in_specs = (
        P("dom", "feat"),
        P(None, "feat"),
        P(None, None, "feat"),
        P(),
        P("feat"),
        P("dom", None),
        P("dom", None),
        P("dom"),
        P("dom"),
        P("dom"),
    )
    out_specs = P("dom", "feat")
    return jax.shard_map(
        on_device, mesh=mesh, in_specs=in_specs, out_specs=out_specs, check_vma=False
    )
```

```python
import functools

import jax
import jax.numpy as jnp
from jax import lax
from jax.experimental import pallas as pl
from jax.experimental.pallas import tpu as pltpu
from jax.sharding import PartitionSpec as P

TILE = 128
HUB_MIRRORS = 128
CAP = 128
DEG_ROWS = 16
VMEM_LIMIT = 44 * 1024 * 1024
BF = jnp.bfloat16
F32 = jnp.float32
HOT = jnp.float8_e4m3fn


def prepare_kernel(
    live_ref, src_ref, dst_ref, rel_ref, coef_ref, words_ref, lhs_ref, spread, *, owners, src_tiles, group
):
    blocks = src_ref.shape[0]
    n_bases, relations = coef_ref.shape
    live = live_ref[0]
    src_tile = src_ref[:, :1] >> 7
    dst_tile = dst_ref[:, :1] >> 7
    index = lax.broadcasted_iota(jnp.int32, (blocks, 1), 0)
    active = index < live
    key = jnp.where(dst_tile < owners, src_tiles, 0) + src_tile
    key = jnp.where(active, key, TILE - 1)
    key_wide = jnp.broadcast_to(key, (blocks, TILE))
    key_row = key_wide.astype(F32).T[:1, :]
    lane = lax.broadcasted_iota(jnp.int32, (1, TILE), 1)
    same_key = key_wide == lane
    count = jnp.sum(same_key.astype(F32), axis=0, keepdims=True)
    count = jnp.where(lane < 2 * src_tiles, count, 0.0).astype(jnp.int32)
    pairs = (count + 1) >> 1
    earlier = lax.broadcasted_iota(jnp.int32, (TILE, TILE), 0) < lax.broadcasted_iota(
        jnp.int32, (TILE, TILE), 1
    )
    pairs_wide = jnp.broadcast_to(pairs, (8, TILE)).astype(F32).astype(BF)
    start = jnp.dot(
        pairs_wide, jnp.where(earlier, 1.0, 0.0).astype(BF), preferred_element_type=F32
    )[:1].astype(jnp.int32)
    zero = jnp.zeros_like(pairs)
    mirror_pairs = jnp.sum(
        jnp.where(lane < src_tiles, pairs, zero).astype(F32), axis=1, keepdims=True
    ).astype(jnp.int32)
    hub_pairs = jnp.sum(
        jnp.where(lane >= src_tiles, pairs, zero).astype(F32), axis=1, keepdims=True
    ).astype(jnp.int32)
    shift = group.bit_length() - 1
    mirror_groups = (mirror_pairs + group - 1) >> shift
    hub_groups = (hub_pairs + group - 1) >> shift
    start = start + jnp.where(lane >= src_tiles, mirror_groups * group - mirror_pairs, 0)
    other = lax.broadcasted_iota(jnp.int32, (1, blocks), 1)
    before = (key.astype(F32) == key_row) & (other < index)
    rank = jnp.sum(before.astype(F32), axis=1, keepdims=True).astype(jnp.int32)
    first = jnp.sum(
        jnp.where(same_key, start, 0).astype(F32), axis=1, keepdims=True
    ).astype(jnp.int32)
    place = jnp.where(active, 2 * first + rank, -1)
    word = index | (src_tile << 9) | (dst_tile << 14) | (1 << 20)
    slots = words_ref.shape[1] - TILE
    slot = lax.broadcasted_iota(jnp.int32, (1, slots), 1)
    words_ref[:, :slots] = jnp.sum(jnp.where(place == slot, word, 0), axis=0, keepdims=True)
    words_ref[:, slots:] = jnp.where(
        lane == 0, mirror_groups, jnp.where(lane == 1, mirror_groups + hub_groups, 0)
    )

    rel_wide = jnp.broadcast_to(rel_ref[...].astype(F32), (TILE, blocks)).T[:, :1]
    relation = rel_wide.astype(jnp.int32)
    span = lax.broadcasted_iota(jnp.int32, (1, relations), 1)
    one_hot = jnp.where(relation == span, 1.0, 0.0).astype(BF)
    mixing = lax.dot_general(
        one_hot, coef_ref[...], (((1,), (1,)), ((), ())), preferred_element_type=F32
    )
    copies = lhs_ref.shape[1] // n_bases
    blank = jnp.zeros_like(mixing)
    for i in range(copies):
        row = jnp.concatenate([mixing if k == i else blank for k in range(copies)], axis=1)
        for half in range(copies * n_bases // TILE):
            spread[half, pl.ds(i, blocks, stride=copies), :] = row[:, half * TILE : (half + 1) * TILE]
    for half in range(copies * n_bases // TILE):
        lhs_ref[:, half * TILE : (half + 1) * TILE] = spread[half].astype(BF)


def prepare(live, edge_src, edge_dst, block_rel, basis_coef, owners, src_tiles, group):
    blocks = edge_src.shape[0]
    n_bases = basis_coef.shape[1]
    slots = 2 * group * (-(-(blocks + 2 * src_tiles) // (2 * group)) + 1)
    slots = -(-slots // TILE) * TILE
    vmem = pl.BlockSpec(memory_space=pltpu.VMEM)
    return pl.pallas_call(
        functools.partial(prepare_kernel, owners=owners, src_tiles=src_tiles, group=group),
        out_shape=(
            jax.ShapeDtypeStruct((1, slots + TILE), jnp.int32),
            jax.ShapeDtypeStruct((4 * blocks, 4 * n_bases), BF),
        ),
        in_specs=[pl.BlockSpec(memory_space=pltpu.SMEM)] + [vmem] * 4,
        out_specs=(vmem, vmem),
        scratch_shapes=[pltpu.VMEM((4 * n_bases // TILE, 4 * blocks, TILE), F32)],
        compiler_params=pltpu.CompilerParams(vmem_limit_bytes=VMEM_LIMIT),
        name="prepare",
    )(live, edge_src, edge_dst, block_rel.reshape(1, blocks), basis_coef.T)


def mix_kernel(feat_ref, lhs_ref, bases_ref, *rest, chunk):
    w_ref, spread, rights = rest[-3:]
    n_bases, depth, cols = bases_ref.shape
    step = pl.program_id(0)
    side = step & 1

    def turn():
        spread[...] = bases_ref[...].astype(F32).reshape(n_bases * depth, cols)
        for d in range(depth):
            octet, half, row = d // 8, d % 8 // 4, d % 4
            rows = slice(row * n_bases, (row + 1) * n_bases)
            rights[side, octet, rows, half * cols : (half + 1) * cols] = spread[
                pl.ds(d, n_bases, stride=depth), :
            ].astype(BF)

    @pl.when(step == 0)
    def _():
        turn()

    @pl.when(step > 0)
    def _():
        turn()
        pairs = chunk // 8
        low = lax.broadcasted_iota(jnp.int32, (pairs, 8, cols), 1) < 4
        for row in range(0, lhs_ref.shape[0], chunk):
            left = lhs_ref[row : row + chunk, :]
            pair = row // 8
            for first_octet in range(0, depth // 8, 2):
                evens, odds = [], []
                for octet in (first_octet, first_octet + 1):
                    out = jnp.dot(left, rights[1 - side, octet], preferred_element_type=F32)
                    first = out[:, :cols].reshape(pairs, 8, cols)
                    second = out[:, cols:].reshape(pairs, 8, cols)
                    evens.append(jnp.where(low, first, pltpu.roll(second, 4, 1)))
                    odds.append(jnp.where(low, pltpu.roll(first, 4, 1), second))
                at = slice(first_octet * 8, first_octet * 8 + 16)
                w_ref[pair : pair + pairs, 0, at] = jnp.concatenate(evens, axis=1).astype(BF)
                w_ref[pair : pair + pairs, 1, at] = jnp.concatenate(odds, axis=1).astype(BF)


def mix(feat, lhs, bases, blocks, begin=0, end=None, earlier=None):
    n_bases, model_dim, cols = bases.shape
    depth = 32
    steps = model_dim // depth
    end = steps if end is None else end
    per_part = cols // depth

    def bases_at(i, f):
        return (0, lax.rem(jnp.minimum(i + begin, end - 1) + f[0] * per_part, steps), 0)

    more = [] if earlier is None else [earlier]
    return pl.pallas_call(
        functools.partial(mix_kernel, chunk=512),
        out_shape=jax.ShapeDtypeStruct((blocks // 2, 2, model_dim, cols), BF),
        grid_spec=pltpu.PrefetchScalarGridSpec(
            num_scalar_prefetch=1,
            grid=(end - begin + 1,),
            in_specs=[
                pl.BlockSpec(lhs.shape, lambda i, f: (0, 0)),
                pl.BlockSpec((n_bases, depth, cols), bases_at),
            ]
            + [pl.BlockSpec(memory_space=pl.ANY)] * len(more),
            out_specs=pl.BlockSpec(
                (blocks // 2, 2, depth, cols),
                lambda i, f: (0, 0, jnp.maximum(i - 1, 0) + begin, 0),
            ),
            scratch_shapes=[
                pltpu.VMEM((n_bases * depth, cols), F32),
                pltpu.VMEM((2, depth // 8, 4 * n_bases, 2 * cols), BF),
            ],
        ),
        input_output_aliases={3: 0} if more else {},
        cost_estimate=pl.CostEstimate(
            flops=8 * blocks * n_bases * depth * (end - begin) * cols,
            bytes_accessed=blocks * depth * (end - begin) * cols * 2,
            transcendentals=0,
        ),
        compiler_params=pltpu.CompilerParams(vmem_limit_bytes=VMEM_LIMIT),
        name="mix" if earlier is None else "mix_rest",
    )(feat, lhs, in_hbm(bases), *more)


def in_vmem(x):
    return pltpu.with_memory_space_constraint(x, pltpu.VMEM)


def in_hbm(x):
    return pltpu.with_memory_space_constraint(x, pltpu.HBM)


def joins(joined, halves, sems, first_sem):
    rows = halves[0].shape[0]
    return [
        pltpu.make_async_copy(half, joined.at[pl.ds(i * rows, rows)], sems.at[first_sem + i])
        for i, half in enumerate(halves)
    ]


def unpack(word):
    return word & 511, (word >> 9) & 31, (word >> 14) & 63, word >> 20


def blocks_kernel(*refs, group, owners, split, hubs):
    word_ref, src_ref, dst_ref = refs[:3]
    pieces, halves = refs[3:6], refs[6:8]
    w_ref, out_ref, acc, deg, held, joined, sems = refs[8:]
    spans = word_ref.shape[1] - TILE
    first_group = word_ref[0, spans] if hubs else 0
    end_group = word_ref[0, spans + int(hubs)]

    def fetch(at):
        side = at & 1
        for k in range(2 * group):
            block = word_ref[0, at * (2 * group) + k] & 511
            pltpu.make_async_copy(
                w_ref.at[block >> 1, block & 1], held.at[side, k // 2, k % 2], sems.at[side]
            ).start()

    @pl.when(first_group < end_group)
    def _():
        fetch(first_group)

    loads = joins(joined, halves, sems, 2)
    for load in loads:
        load.start()
    acc[...] = jnp.zeros_like(acc)
    deg[...] = jnp.zeros_like(deg)
    for load in loads:
        load.wait()

    def body(here, carry):
        side = here & 1

        @pl.when(here + 1 < end_group)
        def _():
            fetch(here + 1)

        pltpu.make_async_copy(w_ref.at[pl.ds(0, group)], held.at[side], sems.at[side]).wait()
        slot = lax.broadcasted_iota(jnp.int32, (TILE, TILE), 0).astype(F32).astype(BF)
        lane = lax.broadcasted_iota(jnp.int32, (TILE, TILE), 1)
        one = jnp.ones((TILE, TILE), BF)
        zero = jnp.zeros((TILE, TILE), BF)

        def diagonal(first, second):
            top = jnp.concatenate([first, zero], axis=1)
            bottom = jnp.concatenate([zero, second], axis=1)
            return jnp.concatenate([top, bottom], axis=0)

        def fields(pair, k):
            return unpack(word_ref[0, (here * group + pair) * 2 + k])

        def adjacency(pair):
            dst_hot, src_hot, count = [], [], None
            for k in range(2):
                block, src_tile, dst_tile, used = fields(pair, k)
                base = jnp.where(used > 0, dst_tile * TILE, 1 << 20)
                dst = (dst_ref[pl.ds(block, 1), :] - base).astype(F32).astype(BF)
                src = (src_ref[pl.ds(block, 1), :] - src_tile * TILE).astype(F32).astype(BF)
                dst_hot.append(jnp.where(slot == dst, one, zero))
                src_hot.append(jnp.where(slot == src, one, zero))
                column = jnp.sum(dst_hot[k].astype(F32), axis=1, keepdims=True)
                extra = jnp.where(lane == lax.rem(dst_tile, owners), column, 0.0)
                count = extra if count is None else count + extra
            found = lax.dot_general(
                jnp.concatenate(dst_hot, axis=1).astype(HOT),
                diagonal(src_hot[0], src_hot[1]).astype(HOT),
                (((1,), (1,)), ((), ())),
                preferred_element_type=F32,
            )
            return found.astype(BF), count

        def message(pair):
            src_tile = fields(pair, 0)[1]
            rows = pl.ds(pl.multiple_of(src_tile * TILE, TILE), TILE)
            tile = jnp.concatenate(
                [pieces[0][rows, :], pieces[1][rows, :], joined[rows, :], pieces[2][rows, :]],
                axis=1,
            )
            weight = jnp.concatenate([held[side, pair, 0], held[side, pair, 1]], axis=1)
            out = jnp.dot(tile, weight, preferred_element_type=F32).astype(BF)
            return diagonal(out[:, :TILE], out[:, TILE:])

        total = deg[...]
        for first in range(0, group, split):
            pairs = range(first, first + split)
            found = [adjacency(pair) for pair in pairs]
            messages = [message(pair) for pair in pairs]
            sums = [
                jnp.dot(f[0], m, preferred_element_type=F32) for f, m in zip(found, messages)
            ]
            for pair, both, part in zip(pairs, sums, found):
                total = total + part[1]
                for k in range(2):
                    dst = lax.rem(fields(pair, k)[2], owners)
                    acc[dst] = acc[dst] + both[:, k * TILE : (k + 1) * TILE]
        deg[...] = total
        return carry

    lax.fori_loop(first_group, end_group, body, 0)

    deg[...] = deg[...].T
    line = lax.broadcasted_iota(jnp.int32, (DEG_ROWS, TILE), 0)
    for at in range(owners):
        degree = deg[at : at + 1, :]
        high = jnp.floor(degree * (1.0 / 256.0)) * 256.0
        low = degree - high
        out_ref[at, :TILE, :] = acc[at].astype(BF)
        rows = jnp.where(line == 0, high, jnp.where(line == 1, low, 0.0))
        out_ref[at, TILE:, :] = rows.astype(BF)


def blocks_call(words, weights, edge_src, edge_dst, pieces, owners, hubs, group=16, split=16):
    pair_count, _, model_dim, cols = weights.shape
    vmem = pl.BlockSpec(memory_space=pltpu.VMEM)
    smem = pl.BlockSpec(memory_space=pltpu.SMEM)
    anywhere = pl.BlockSpec(memory_space=pl.ANY)
    return pl.pallas_call(
        functools.partial(blocks_kernel, group=group, owners=owners, split=split, hubs=hubs),
        out_shape=jax.ShapeDtypeStruct((owners, TILE + DEG_ROWS, cols), BF),
        in_specs=[smem, vmem, vmem] + [vmem] * 3 + [anywhere] * 3,
        out_specs=vmem,
        scratch_shapes=[
            pltpu.VMEM((owners, TILE, cols), F32),
            pltpu.VMEM((TILE, TILE), F32),
            pltpu.VMEM((2, group, 2, model_dim, cols), BF),
            pltpu.VMEM(pieces[0].shape, BF),
            pltpu.SemaphoreType.DMA((4,)),
        ],
        cost_estimate=pl.CostEstimate(
            flops=pair_count * 4 * TILE * model_dim * cols,
            bytes_accessed=pair_count * model_dim * cols * 2,
            transcendentals=0,
        ),
        compiler_params=pltpu.CompilerParams(vmem_limit_bytes=VMEM_LIMIT),
        name="hub_blocks" if hubs else "mirror_blocks",
    )(words, edge_src, edge_dst, *pieces, weights)


def square_lines(value):
    squares = jnp.sum(value * value, axis=1, keepdims=True)
    line = jnp.broadcast_to(squares, value.shape).T[:1, :]
    pieces = [line[:, i : i + TILE] for i in range(0, value.shape[0], TILE)]
    return jnp.concatenate(pieces, axis=0)


def mirror_kernel(
    feat_ref,
    mirror_ref,
    master_ref,
    self_ref,
    x0_ref,
    x1_ref,
    x3_ref,
    first_ref,
    second_ref,
    mixed_ref,
    squares_ref,
    right,
    turned,
    x2_ref,
    sems,
    *,
    chunk,
    reach,
):
    step = pl.program_id(0)
    owners = mirror_ref.shape[0]
    cols = mirror_ref.shape[2]

    @pl.when(step == 0)
    def _():
        loads = joins(x2_ref, (first_ref, second_ref), sems, 0)
        for load in loads:
            load.start()
        for p in range(4):
            at = pl.multiple_of(lax.rem(feat_ref[0] + p, 4) * cols, cols)
            turned[p * cols : (p + 1) * cols, :] = self_ref[pl.ds(at, cols), :]
        high = mirror_ref[:, TILE, :].astype(F32)
        low = mirror_ref[:, TILE + 1, :].astype(F32)
        pad = jnp.zeros((TILE - 2 * owners, TILE), F32)
        table = jnp.concatenate([high, low, pad], axis=0).T
        lane = lax.broadcasted_iota(jnp.int32, (TILE, TILE), 1)
        for p in range(owners):
            rows = slice(p * TILE, (p + 1) * TILE)
            right[rows, :cols] = mirror_ref[p, :TILE, :]
            keep = (lane == p) | (lane == p + owners)
            right[rows, cols:] = jnp.where(keep, table, 0.0).astype(BF)
        for load in loads:
            load.wait()

    rows = pl.ds(pl.multiple_of(step * chunk, chunk), chunk)
    tile = jnp.concatenate(
        [x0_ref[rows, :], x1_ref[rows, :], x2_ref[rows, :], x3_ref[rows, :]], axis=1
    )
    own = jnp.dot(tile, turned[...], preferred_element_type=F32)

    @pl.when(step * chunk < reach)
    def _():
        local = lax.broadcasted_iota(jnp.int32, (TILE, TILE), 0).astype(F32).astype(BF)
        one = jnp.ones((TILE, TILE), BF)
        zero = jnp.zeros((TILE, TILE), BF)
        columns = []
        for p in range(owners):
            column = []
            for first in range(0, chunk, TILE):
                target = master_ref[p : p + 1, :] - (step * chunk + first)
                column.append(jnp.where(local == target.astype(F32).astype(BF), one, zero))
            columns.append(jnp.concatenate(column, axis=0))
        sums = jnp.dot(jnp.concatenate(columns, axis=1), right[...], preferred_element_type=F32)
        degree = jnp.sum(sums[:, cols:], axis=1, keepdims=True)
        mixed = own + sums[:, :cols] * lax.rsqrt(jnp.maximum(degree, 1.0))
        mixed_ref[...] = mixed
        squares_ref[...] = square_lines(mixed)

    @pl.when(step * chunk >= reach)
    def _():
        mixed_ref[...] = own
        squares_ref[...] = square_lines(own)


def mirror_final(feat, mirror, master, self_weight, pieces):
    n_local, cols = pieces[0].shape
    owners = mirror.shape[0]
    chunk = 1024
    whole = lambda shape: pl.BlockSpec(shape, lambda i, *_: (0,) * len(shape))
    return pl.pallas_call(
        functools.partial(mirror_kernel, chunk=chunk, reach=n_local - n_local // 4),
        out_shape=(
            jax.ShapeDtypeStruct((n_local, cols), F32),
            jax.ShapeDtypeStruct((n_local // TILE, TILE), F32),
        ),
        grid_spec=pltpu.PrefetchScalarGridSpec(
            num_scalar_prefetch=1,
            grid=(n_local // chunk,),
            in_specs=[whole(mirror.shape), whole(master.shape), whole(self_weight.shape)]
            + [whole(p.shape) for p in pieces[:3]]
            + [pl.BlockSpec(memory_space=pl.ANY)] * 2,
            out_specs=(
                pl.BlockSpec((chunk, cols), lambda i, *_: (i, 0)),
                pl.BlockSpec((chunk // TILE, TILE), lambda i, *_: (i, 0)),
            ),
            scratch_shapes=[
                pltpu.VMEM((owners * TILE, 2 * cols), BF),
                pltpu.VMEM(self_weight.shape, BF),
                pltpu.VMEM(pieces[0].shape, BF),
                pltpu.SemaphoreType.DMA((2,)),
            ],
        ),
        cost_estimate=pl.CostEstimate(
            flops=n_local * n_local * 4 * cols, bytes_accessed=8 << 20, transcendentals=0
        ),
        compiler_params=pltpu.CompilerParams(vmem_limit_bytes=VMEM_LIMIT),
        name="mirror_final",
    )(feat, mirror, master, self_weight, *pieces)


def hub_kernel(hub_ref, mixed_ref, squares_ref, out_ref, lines_ref):
    hub = jnp.sum(hub_ref[:, :TILE, :].astype(F32), axis=0)
    counts = hub_ref[:, TILE : TILE + DEG_ROWS, :].astype(F32)
    line = jnp.sum(jnp.sum(counts, axis=0), axis=0, keepdims=True)
    column = jnp.broadcast_to(line, (TILE, TILE)).T[:, :1]
    mixed = mixed_ref[:HUB_MIRRORS, :] + hub * lax.rsqrt(jnp.maximum(column, 1.0))
    out_ref[...] = mixed
    lines_ref[...] = squares_ref[...]
    lines_ref[:1, :] = square_lines(mixed)


def hub_final(hub, mixed, squares):
    vmem = pl.BlockSpec(memory_space=pltpu.VMEM)
    return pl.pallas_call(
        hub_kernel,
        out_shape=(
            jax.ShapeDtypeStruct((HUB_MIRRORS, mixed.shape[1]), F32),
            jax.ShapeDtypeStruct(squares.shape, F32),
        ),
        in_specs=[vmem] * 3,
        out_specs=(vmem, vmem),
        compiler_params=pltpu.CompilerParams(vmem_limit_bytes=VMEM_LIMIT),
        name="hub_final",
    )(hub, in_vmem(mixed), in_vmem(squares))


def scale_kernel(mixed_ref, hub_ref, a_ref, b_ref, c_ref, d_ref, gain_ref, out_ref, *, model_dim):
    lines = a_ref[...] + b_ref[...] + c_ref[...] + d_ref[...]
    norm = lax.rsqrt(lines / model_dim + 1e-05)
    gain = gain_ref[...]
    tiles, width = norm.shape
    for i in range(tiles):
        rows = slice(i * width, (i + 1) * width)
        value = hub_ref[...] if i == 0 else mixed_ref[rows, :]
        column = jnp.broadcast_to(norm[i : i + 1, :], (width, width)).T
        out_ref[rows, :] = (value * column * gain).astype(BF)


def scale(mixed, hub_mixed, lines, gain, model_dim):
    vmem = pl.BlockSpec(memory_space=pltpu.VMEM)
    return pl.pallas_call(
        functools.partial(scale_kernel, model_dim=model_dim),
        out_shape=jax.ShapeDtypeStruct(mixed.shape, BF),
        in_specs=[vmem] * 7,
        out_specs=vmem,
        compiler_params=pltpu.CompilerParams(vmem_limit_bytes=VMEM_LIMIT),
        name="scale",
    )(in_vmem(mixed), in_vmem(hub_mixed), *[in_vmem(x) for x in lines], gain)


def from_others(x, size):
    return [
        lax.ppermute(x, "feat", [((i + shift) % size, i) for i in range(size)])
        for shift in range(1, size)
    ]


def on_device(
    embeddings,
    self_weight,
    bases,
    basis_coef,
    out_gain,
    edge_src,
    edge_dst,
    block_rel,
    mirror_master_rows,
    block_count,
):
    owners = lax.axis_size("dom")
    feat_size = lax.axis_size("feat")
    feat = lax.axis_index("feat").astype(jnp.int32)
    blocks = edge_src.shape[0]
    n_local, cols = embeddings.shape
    model_dim = bases.shape[1]
    feat_at = feat.reshape(1)
    ahead = [((i + 1) % feat_size, i) for i in range(feat_size)]
    behind = [(i, (i + 1) % feat_size) for i in range(feat_size)]
    after = lax.ppermute(embeddings, "feat", ahead)
    before = lax.ppermute(embeddings, "feat", behind)

    words, lhs = prepare(
        block_count, edge_src, edge_dst, block_rel, basis_coef, owners, n_local // TILE, 16
    )
    steps = 10
    weights = mix(feat_at, lhs, bases, blocks, 0, steps)
    weights, after, before = lax.optimization_barrier((weights, after, before))
    half = n_local // 2
    halves = [
        lax.ppermute(after[:half], "feat", ahead),
        lax.ppermute(before[half:], "feat", behind),
    ]
    weights = mix(feat_at, lhs, bases, blocks, steps, None, weights)
    pieces = [in_vmem(x) for x in (embeddings, after, before)] + [in_hbm(x) for x in halves]
    edges = (edge_src, edge_dst)
    mirror_part = blocks_call(words, weights, *edges, pieces, owners, False)
    mirror = lax.all_to_all(mirror_part, "dom", split_axis=0, concat_axis=0, tiled=True)
    weights, _ = lax.optimization_barrier((weights, mirror_part))
    hub_part = blocks_call(words, weights, *edges, pieces, owners, True)
    hub_part, mirror = lax.optimization_barrier((hub_part, mirror))
    hub = lax.all_to_all(hub_part, "dom", split_axis=0, concat_axis=0, tiled=True)

    mixed, squares = mirror_final(
        feat.reshape(1), mirror, mirror_master_rows.reshape(owners, TILE), self_weight, pieces
    )
    hub_mixed, line = hub_final(hub, mixed, squares)
    lines = [line] + from_others(line, feat_size)
    return scale(mixed, hub_mixed, lines, out_gain.reshape(1, cols), model_dim)


def solution(mesh):
    in_specs = (
        P("dom", "feat"),
        P(None, "feat"),
        P(None, None, "feat"),
        P(),
        P("feat"),
        P("dom", None),
        P("dom", None),
        P("dom"),
        P("dom"),
        P("dom"),
    )
    out_specs = P("dom", "feat")
    return jax.shard_map(
        on_device, mesh=mesh, in_specs=in_specs, out_specs=out_specs, check_vma=False
    )
```

```python
import functools

import jax
import jax.numpy as jnp
from jax import lax
from jax.experimental import pallas as pl
from jax.experimental.pallas import tpu as pltpu
from jax.sharding import PartitionSpec as P

TILE = 128
HUB_MIRRORS = 128
CAP = 128
DEG_ROWS = 16
VMEM_LIMIT = 44 * 1024 * 1024
BF = jnp.bfloat16
F32 = jnp.float32
HOT = jnp.float8_e4m3fn


def prepare_kernel(
    live_ref,
    src_hbm,
    dst_hbm,
    rel_hbm,
    coef_hbm,
    words_ref,
    lhs_ref,
    spread,
    src_ref,
    dst_ref,
    rel_ref,
    coef_ref,
    sems,
    *,
    owners,
    src_tiles,
    group,
):
    loads = [
        pltpu.make_async_copy(a, b, sems.at[i])
        for i, (a, b) in enumerate(
            [(src_hbm, src_ref), (dst_hbm, dst_ref), (rel_hbm, rel_ref), (coef_hbm, coef_ref)]
        )
    ]
    for load in loads:
        load.start()
    for load in loads:
        load.wait()
    blocks = src_ref.shape[0]
    n_bases, relations = coef_ref.shape
    live = live_ref[0]
    src_tile = src_ref[:, :1] >> 7
    dst_tile = dst_ref[:, :1] >> 7
    index = lax.broadcasted_iota(jnp.int32, (blocks, 1), 0)
    active = index < live
    key = jnp.where(dst_tile < owners, src_tiles, 0) + src_tile
    key = jnp.where(active, key, TILE - 1)
    key_wide = jnp.broadcast_to(key, (blocks, TILE))
    key_row = key_wide.astype(F32).T[:1, :]
    lane = lax.broadcasted_iota(jnp.int32, (1, TILE), 1)
    same_key = key_wide == lane
    count = jnp.sum(same_key.astype(F32), axis=0, keepdims=True)
    count = jnp.where(lane < 2 * src_tiles, count, 0.0).astype(jnp.int32)
    pairs = (count + 1) >> 1
    earlier = lax.broadcasted_iota(jnp.int32, (TILE, TILE), 0) < lax.broadcasted_iota(
        jnp.int32, (TILE, TILE), 1
    )
    pairs_wide = jnp.broadcast_to(pairs, (8, TILE)).astype(F32).astype(BF)
    start = jnp.dot(
        pairs_wide, jnp.where(earlier, 1.0, 0.0).astype(BF), preferred_element_type=F32
    )[:1].astype(jnp.int32)
    zero = jnp.zeros_like(pairs)
    mirror_pairs = jnp.sum(
        jnp.where(lane < src_tiles, pairs, zero).astype(F32), axis=1, keepdims=True
    ).astype(jnp.int32)
    hub_pairs = jnp.sum(
        jnp.where(lane >= src_tiles, pairs, zero).astype(F32), axis=1, keepdims=True
    ).astype(jnp.int32)
    shift = group.bit_length() - 1
    mirror_groups = (mirror_pairs + group - 1) >> shift
    hub_groups = (hub_pairs + group - 1) >> shift
    start = start + jnp.where(lane >= src_tiles, mirror_groups * group - mirror_pairs, 0)
    other = lax.broadcasted_iota(jnp.int32, (1, blocks), 1)
    before = (key.astype(F32) == key_row) & (other < index)
    rank = jnp.sum(before.astype(F32), axis=1, keepdims=True).astype(jnp.int32)
    first = jnp.sum(
        jnp.where(same_key, start, 0).astype(F32), axis=1, keepdims=True
    ).astype(jnp.int32)
    place = jnp.where(active, 2 * first + rank, -1)
    word = index | (src_tile << 9) | (dst_tile << 14) | (1 << 20)
    slots = words_ref.shape[1] - TILE
    slot = lax.broadcasted_iota(jnp.int32, (1, slots), 1)
    words_ref[:, :slots] = jnp.sum(jnp.where(place == slot, word, 0), axis=0, keepdims=True)
    words_ref[:, slots:] = jnp.where(
        lane == 0, mirror_groups, jnp.where(lane == 1, mirror_groups + hub_groups, 0)
    )

    rel_wide = jnp.broadcast_to(rel_ref[...].astype(F32), (TILE, blocks)).T[:, :1]
    relation = rel_wide.astype(jnp.int32)
    span = lax.broadcasted_iota(jnp.int32, (1, relations), 1)
    one_hot = jnp.where(relation == span, 1.0, 0.0).astype(BF)
    mixing = lax.dot_general(
        one_hot, coef_ref[...], (((1,), (1,)), ((), ())), preferred_element_type=F32
    )
    copies = lhs_ref.shape[1] // n_bases
    blank = jnp.zeros_like(mixing)
    for i in range(copies):
        row = jnp.concatenate([mixing if k == i else blank for k in range(copies)], axis=1)
        for half in range(copies * n_bases // TILE):
            spread[half, pl.ds(i, blocks, stride=copies), :] = row[:, half * TILE : (half + 1) * TILE]
    for half in range(copies * n_bases // TILE):
        lhs_ref[:, half * TILE : (half + 1) * TILE] = spread[half].astype(BF)


def prepare(live, edge_src, edge_dst, block_rel, basis_coef, owners, src_tiles, group):
    blocks = edge_src.shape[0]
    n_bases = basis_coef.shape[1]
    slots = 2 * group * (-(-(blocks + 2 * src_tiles) // (2 * group)) + 1)
    slots = -(-slots // TILE) * TILE
    vmem = pl.BlockSpec(memory_space=pltpu.VMEM)
    return pl.pallas_call(
        functools.partial(prepare_kernel, owners=owners, src_tiles=src_tiles, group=group),
        out_shape=(
            jax.ShapeDtypeStruct((1, slots + TILE), jnp.int32),
            jax.ShapeDtypeStruct((4 * blocks, 4 * n_bases), BF),
        ),
        in_specs=[pl.BlockSpec(memory_space=pltpu.SMEM)] + [pl.BlockSpec(memory_space=pl.ANY)] * 4,
        out_specs=(vmem, vmem),
        scratch_shapes=[
            pltpu.VMEM((4 * n_bases // TILE, 4 * blocks, TILE), F32),
            pltpu.VMEM(edge_src.shape, jnp.int32),
            pltpu.VMEM(edge_dst.shape, jnp.int32),
            pltpu.VMEM((1, blocks), jnp.int32),
            pltpu.VMEM(basis_coef.shape[::-1], BF),
            pltpu.SemaphoreType.DMA((4,)),
        ],
        compiler_params=pltpu.CompilerParams(vmem_limit_bytes=VMEM_LIMIT),
        name="prepare",
    )(
        live,
        in_hbm(edge_src),
        in_hbm(edge_dst),
        in_hbm(block_rel.reshape(1, blocks)),
        in_hbm(basis_coef.T),
    )


def mix_kernel(feat_ref, lhs_ref, bases_ref, *rest, chunk):
    w_ref, spread, rights = rest[-3:]
    n_bases, depth, cols = bases_ref.shape
    step = pl.program_id(0)
    side = step & 1

    def turn():
        spread[:, :depth, :] = bases_ref[...].astype(F32)
        pitch = spread.shape[1]
        flat = spread.reshape(n_bases * pitch, cols)
        for d in range(depth):
            octet, half, row = d // 8, d % 8 // 4, d % 4
            rows = slice(row * n_bases, (row + 1) * n_bases)
            rights[side, octet, rows, half * cols : (half + 1) * cols] = flat[
                pl.ds(d, n_bases, stride=pitch), :
            ].astype(BF)

    @pl.when(step == 0)
    def _():
        turn()

    @pl.when(step > 0)
    def _():
        turn()
        pairs = chunk // 8
        low = lax.broadcasted_iota(jnp.int32, (pairs, 8, cols), 1) < 4
        for row in range(0, lhs_ref.shape[0], chunk):
            left = lhs_ref[row : row + chunk, :]
            pair = row // 8
            for first_octet in range(0, depth // 8, 2):
                evens, odds = [], []
                for octet in (first_octet, first_octet + 1):
                    out = jnp.dot(left, rights[1 - side, octet], preferred_element_type=F32)
                    first = out[:, :cols].reshape(pairs, 8, cols)
                    second = out[:, cols:].reshape(pairs, 8, cols)
                    evens.append(jnp.where(low, first, pltpu.roll(second, 4, 1)))
                    odds.append(jnp.where(low, pltpu.roll(first, 4, 1), second))
                at = slice(first_octet * 8, first_octet * 8 + 16)
                w_ref[pair : pair + pairs, 0, at] = jnp.concatenate(evens, axis=1).astype(BF)
                w_ref[pair : pair + pairs, 1, at] = jnp.concatenate(odds, axis=1).astype(BF)


def mix(feat, lhs, bases, blocks, begin=0, end=None, earlier=None):
    n_bases, model_dim, cols = bases.shape
    depth = 32
    steps = model_dim // depth
    end = steps if end is None else end
    per_part = cols // depth

    def bases_at(i, f):
        return (0, lax.rem(jnp.minimum(i + begin, end - 1) + f[0] * per_part, steps), 0)

    more = [] if earlier is None else [earlier]
    return pl.pallas_call(
        functools.partial(mix_kernel, chunk=512),
        out_shape=jax.ShapeDtypeStruct((blocks // 2, 2, model_dim, cols), BF),
        grid_spec=pltpu.PrefetchScalarGridSpec(
            num_scalar_prefetch=1,
            grid=(end - begin + 1,),
            in_specs=[
                pl.BlockSpec(lhs.shape, lambda i, f: (0, 0)),
                pl.BlockSpec((n_bases, depth, cols), bases_at),
            ]
            + [pl.BlockSpec(memory_space=pl.ANY)] * len(more),
            out_specs=pl.BlockSpec(
                (blocks // 2, 2, depth, cols),
                lambda i, f: (0, 0, jnp.maximum(i - 1, 0) + begin, 0),
            ),
            scratch_shapes=[
                pltpu.VMEM((n_bases, depth + 8, cols), F32),
                pltpu.VMEM((2, depth // 8, 4 * n_bases, 2 * cols), BF),
            ],
        ),
        input_output_aliases={3: 0} if more else {},
        cost_estimate=pl.CostEstimate(
            flops=8 * blocks * n_bases * depth * (end - begin) * cols,
            bytes_accessed=blocks * depth * (end - begin) * cols * 2,
            transcendentals=0,
        ),
        compiler_params=pltpu.CompilerParams(vmem_limit_bytes=VMEM_LIMIT),
        name="mix" if earlier is None else "mix_rest",
    )(feat, lhs, in_hbm(bases), *more)


def in_vmem(x):
    return pltpu.with_memory_space_constraint(x, pltpu.VMEM)


def in_hbm(x):
    return pltpu.with_memory_space_constraint(x, pltpu.HBM)


def joins(joined, halves, sems, first_sem):
    rows = halves[0].shape[0]
    return [
        pltpu.make_async_copy(half, joined.at[pl.ds(i * rows, rows)], sems.at[first_sem + i])
        for i, half in enumerate(halves)
    ]


def unpack(word):
    return word & 511, (word >> 9) & 31, (word >> 14) & 63, word >> 20


def blocks_kernel(*refs, group, owners, split, hubs):
    word_ref, src_hbm, dst_hbm = refs[:3]
    pieces, halves = refs[3:6], refs[6:8]
    w_ref, out_ref, acc, deg, held, joined, src_ref, dst_ref, sems = refs[8:]
    spans = word_ref.shape[1] - TILE
    first_group = word_ref[0, spans] if hubs else 0
    end_group = word_ref[0, spans + int(hubs)]

    def fetch(at):
        side = at & 1
        for k in range(2 * group):
            block = word_ref[0, at * (2 * group) + k] & 511
            pltpu.make_async_copy(
                w_ref.at[block >> 1, block & 1], held.at[side, k // 2, k % 2], sems.at[side]
            ).start()

    @pl.when(first_group < end_group)
    def _():
        fetch(first_group)

    loads = joins(joined, halves, sems, 2)
    loads.append(pltpu.make_async_copy(src_hbm, src_ref, sems.at[4]))
    loads.append(pltpu.make_async_copy(dst_hbm, dst_ref, sems.at[5]))
    for load in loads:
        load.start()
    acc[...] = jnp.zeros_like(acc)
    deg[...] = jnp.zeros_like(deg)
    for load in loads:
        load.wait()

    def body(here, carry):
        side = here & 1

        @pl.when(here + 1 < end_group)
        def _():
            fetch(here + 1)

        pltpu.make_async_copy(w_ref.at[pl.ds(0, group)], held.at[side], sems.at[side]).wait()
        slot = lax.broadcasted_iota(jnp.int32, (TILE, TILE), 0).astype(F32).astype(BF)
        lane = lax.broadcasted_iota(jnp.int32, (TILE, TILE), 1)
        one = jnp.ones((TILE, TILE), BF)
        zero = jnp.zeros((TILE, TILE), BF)

        def diagonal(first, second):
            top = jnp.concatenate([first, zero], axis=1)
            bottom = jnp.concatenate([zero, second], axis=1)
            return jnp.concatenate([top, bottom], axis=0)

        def fields(pair, k):
            return unpack(word_ref[0, (here * group + pair) * 2 + k])

        def adjacency(pair):
            dst_hot, src_hot, count = [], [], None
            for k in range(2):
                block, src_tile, dst_tile, used = fields(pair, k)
                base = jnp.where(used > 0, dst_tile * TILE, 1 << 20)
                dst = (dst_ref[pl.ds(block, 1), :] - base).astype(F32).astype(BF)
                src = (src_ref[pl.ds(block, 1), :] - src_tile * TILE).astype(F32).astype(BF)
                dst_hot.append(jnp.where(slot == dst, one, zero))
                src_hot.append(jnp.where(slot == src, one, zero))
                column = jnp.sum(dst_hot[k].astype(F32), axis=1, keepdims=True)
                extra = jnp.where(lane == lax.rem(dst_tile, owners), column, 0.0)
                count = extra if count is None else count + extra
            found = lax.dot_general(
                jnp.concatenate(dst_hot, axis=1).astype(HOT),
                diagonal(src_hot[0], src_hot[1]).astype(HOT),
                (((1,), (1,)), ((), ())),
                preferred_element_type=F32,
            )
            return found.astype(BF), count

        def message(pair):
            src_tile = fields(pair, 0)[1]
            rows = pl.ds(pl.multiple_of(src_tile * TILE, TILE), TILE)
            tile = jnp.concatenate(
                [pieces[0][rows, :], pieces[1][rows, :], joined[rows, :], pieces[2][rows, :]],
                axis=1,
            )
            weight = jnp.concatenate([held[side, pair, 0], held[side, pair, 1]], axis=1)
            out = jnp.dot(tile, weight, preferred_element_type=F32).astype(BF)
            return diagonal(out[:, :TILE], out[:, TILE:])

        total = deg[...]
        for first in range(0, group, split):
            pairs = range(first, first + split)
            found = [adjacency(pair) for pair in pairs]
            messages = [message(pair) for pair in pairs]
            sums = [
                jnp.dot(f[0], m, preferred_element_type=F32) for f, m in zip(found, messages)
            ]
            for pair, both, part in zip(pairs, sums, found):
                total = total + part[1]
                for k in range(2):
                    dst = lax.rem(fields(pair, k)[2], owners)
                    acc[dst] = acc[dst] + both[:, k * TILE : (k + 1) * TILE]
        deg[...] = total
        return carry

    lax.fori_loop(first_group, end_group, body, 0)

    deg[...] = deg[...].T
    line = lax.broadcasted_iota(jnp.int32, (DEG_ROWS, TILE), 0)
    for at in range(owners):
        degree = deg[at : at + 1, :]
        high = jnp.floor(degree * (1.0 / 256.0)) * 256.0
        low = degree - high
        out_ref[at, :TILE, :] = acc[at].astype(BF)
        rows = jnp.where(line == 0, high, jnp.where(line == 1, low, 0.0))
        out_ref[at, TILE:, :] = rows.astype(BF)


def blocks_call(words, weights, edge_src, edge_dst, pieces, owners, hubs, group=16, split=16):
    pair_count, _, model_dim, cols = weights.shape
    vmem = pl.BlockSpec(memory_space=pltpu.VMEM)
    smem = pl.BlockSpec(memory_space=pltpu.SMEM)
    anywhere = pl.BlockSpec(memory_space=pl.ANY)
    return pl.pallas_call(
        functools.partial(blocks_kernel, group=group, owners=owners, split=split, hubs=hubs),
        out_shape=jax.ShapeDtypeStruct((owners, TILE + DEG_ROWS, cols), BF),
        in_specs=[smem, anywhere, anywhere] + [vmem] * 3 + [anywhere] * 3,
        out_specs=vmem,
        scratch_shapes=[
            pltpu.VMEM((owners, TILE, cols), F32),
            pltpu.VMEM((TILE, TILE), F32),
            pltpu.VMEM((2, group, 2, model_dim, cols), BF),
            pltpu.VMEM(pieces[0].shape, BF),
            pltpu.VMEM(edge_src.shape, jnp.int32),
            pltpu.VMEM(edge_dst.shape, jnp.int32),
            pltpu.SemaphoreType.DMA((6,)),
        ],
        cost_estimate=pl.CostEstimate(
            flops=pair_count * 4 * TILE * model_dim * cols,
            bytes_accessed=pair_count * model_dim * cols * 2,
            transcendentals=0,
        ),
        compiler_params=pltpu.CompilerParams(vmem_limit_bytes=VMEM_LIMIT),
        name="hub_blocks" if hubs else "mirror_blocks",
    )(
        words,
        in_hbm(edge_src),
        in_hbm(edge_dst),
        *[in_vmem(x) for x in pieces[:3]],
        *[in_hbm(x) for x in pieces[3:]],
        weights,
    )


def square_lines(value):
    squares = jnp.sum(value * value, axis=1, keepdims=True)
    line = jnp.broadcast_to(squares, value.shape).T[:1, :]
    pieces = [line[:, i : i + TILE] for i in range(0, value.shape[0], TILE)]
    return jnp.concatenate(pieces, axis=0)


def mirror_kernel(
    feat_ref,
    mirror_hbm,
    master_ref,
    self_ref,
    x0_hbm,
    x1_hbm,
    x3_hbm,
    first_hbm,
    second_hbm,
    mixed_ref,
    squares_ref,
    right,
    turned,
    mirror_ref,
    table,
    sems,
    *,
    chunk,
    reach,
):
    step = pl.program_id(0)
    owners = mirror_ref.shape[0]
    cols = mirror_ref.shape[2]

    @pl.when(step == 0)
    def _():
        arrival = pltpu.make_async_copy(mirror_hbm, mirror_ref, sems.at[0])
        arrival.start()
        half = first_hbm.shape[0]
        targets = [
            (x0_hbm, table.at[:, :cols]),
            (x1_hbm, table.at[:, cols : 2 * cols]),
            (x3_hbm, table.at[:, 3 * cols :]),
            (first_hbm, table.at[:half, 2 * cols : 3 * cols]),
            (second_hbm, table.at[half:, 2 * cols : 3 * cols]),
        ]
        loads = [
            pltpu.make_async_copy(a, b, sems.at[1 + i]) for i, (a, b) in enumerate(targets)
        ]
        for load in loads:
            load.start()
        for p in range(4):
            at = pl.multiple_of(lax.rem(feat_ref[0] + p, 4) * cols, cols)
            turned[p * cols : (p + 1) * cols, :] = self_ref[pl.ds(at, cols), :]
        arrival.wait()
        high = mirror_ref[:, TILE, :].astype(F32)
        low = mirror_ref[:, TILE + 1, :].astype(F32)
        pad = jnp.zeros((TILE - 2 * owners, TILE), F32)
        turned_counts = jnp.concatenate([high, low, pad], axis=0).T
        lane = lax.broadcasted_iota(jnp.int32, (TILE, TILE), 1)
        for p in range(owners):
            rows = slice(p * TILE, (p + 1) * TILE)
            right[rows, :cols] = mirror_ref[p, :TILE, :]
            keep = (lane == p) | (lane == p + owners)
            right[rows, cols:] = jnp.where(keep, turned_counts, 0.0).astype(BF)
        for load in loads:
            load.wait()

    rows = pl.ds(pl.multiple_of(step * chunk, chunk), chunk)
    own = jnp.dot(table[rows, :], turned[...], preferred_element_type=F32)

    @pl.when(step * chunk < reach)
    def _():
        local = lax.broadcasted_iota(jnp.int32, (TILE, TILE), 0).astype(F32).astype(BF)
        one = jnp.ones((TILE, TILE), BF)
        zero = jnp.zeros((TILE, TILE), BF)
        columns = []
        for p in range(owners):
            column = []
            for first in range(0, chunk, TILE):
                target = master_ref[p : p + 1, :] - (step * chunk + first)
                column.append(jnp.where(local == target.astype(F32).astype(BF), one, zero))
            columns.append(jnp.concatenate(column, axis=0))
        sums = jnp.dot(jnp.concatenate(columns, axis=1), right[...], preferred_element_type=F32)
        degree = jnp.sum(sums[:, cols:], axis=1, keepdims=True)
        mixed = own + sums[:, :cols] * lax.rsqrt(jnp.maximum(degree, 1.0))
        mixed_ref[...] = mixed
        squares_ref[...] = square_lines(mixed)

    @pl.when(step * chunk >= reach)
    def _():
        mixed_ref[...] = own
        squares_ref[...] = square_lines(own)


def mirror_final(feat, mirror, master, self_weight, pieces):
    n_local, cols = pieces[0].shape
    owners = mirror.shape[0]
    chunk = 1024
    anywhere = pl.BlockSpec(memory_space=pl.ANY)
    whole = lambda shape: pl.BlockSpec(shape, lambda i, *_: (0,) * len(shape))
    return pl.pallas_call(
        functools.partial(mirror_kernel, chunk=chunk, reach=n_local - n_local // 4),
        out_shape=(
            jax.ShapeDtypeStruct((n_local, cols), F32),
            jax.ShapeDtypeStruct((n_local // TILE, TILE), F32),
        ),
        grid_spec=pltpu.PrefetchScalarGridSpec(
            num_scalar_prefetch=1,
            grid=(n_local // chunk,),
            in_specs=[anywhere, whole(master.shape), whole(self_weight.shape)]
            + [anywhere] * len(pieces),
            out_specs=(
                pl.BlockSpec((chunk, cols), lambda i, *_: (i, 0)),
                pl.BlockSpec((chunk // TILE, TILE), lambda i, *_: (i, 0)),
            ),
            scratch_shapes=[
                pltpu.VMEM((owners * TILE, 2 * cols), BF),
                pltpu.VMEM(self_weight.shape, BF),
                pltpu.VMEM(mirror.shape, BF),
                pltpu.VMEM((n_local, 4 * cols), BF),
                pltpu.SemaphoreType.DMA((1 + len(pieces),)),
            ],
        ),
        cost_estimate=pl.CostEstimate(
            flops=n_local * n_local * 4 * cols, bytes_accessed=8 << 20, transcendentals=0
        ),
        compiler_params=pltpu.CompilerParams(vmem_limit_bytes=VMEM_LIMIT),
        name="mirror_final",
    )(feat, in_hbm(mirror), master, self_weight, *[in_hbm(p) for p in pieces])


def hub_kernel(hub_ref, mixed_ref, squares_ref, out_ref, lines_ref):
    hub = jnp.sum(hub_ref[:, :TILE, :].astype(F32), axis=0)
    counts = hub_ref[:, TILE : TILE + DEG_ROWS, :].astype(F32)
    line = jnp.sum(jnp.sum(counts, axis=0), axis=0, keepdims=True)
    column = jnp.broadcast_to(line, (TILE, TILE)).T[:, :1]
    mixed = mixed_ref[:HUB_MIRRORS, :] + hub * lax.rsqrt(jnp.maximum(column, 1.0))
    out_ref[...] = mixed
    lines_ref[...] = squares_ref[...]
    lines_ref[:1, :] = square_lines(mixed)


def hub_final(hub, mixed, squares):
    vmem = pl.BlockSpec(memory_space=pltpu.VMEM)
    return pl.pallas_call(
        hub_kernel,
        out_shape=(
            jax.ShapeDtypeStruct((HUB_MIRRORS, mixed.shape[1]), F32),
            jax.ShapeDtypeStruct(squares.shape, F32),
        ),
        in_specs=[vmem] * 3,
        out_specs=(vmem, vmem),
        compiler_params=pltpu.CompilerParams(vmem_limit_bytes=VMEM_LIMIT),
        name="hub_final",
    )(hub, in_vmem(mixed), in_vmem(squares))


def scale_kernel(mixed_ref, hub_ref, a_ref, b_ref, c_ref, d_ref, gain_ref, out_ref, *, model_dim):
    lines = a_ref[...] + b_ref[...] + c_ref[...] + d_ref[...]
    norm = lax.rsqrt(lines / model_dim + 1e-05)
    gain = gain_ref[...]
    tiles, width = norm.shape
    for i in range(tiles):
        rows = slice(i * width, (i + 1) * width)
        value = hub_ref[...] if i == 0 else mixed_ref[rows, :]
        column = jnp.broadcast_to(norm[i : i + 1, :], (width, width)).T
        out_ref[rows, :] = (value * column * gain).astype(BF)


def scale(mixed, hub_mixed, lines, gain, model_dim):
    vmem = pl.BlockSpec(memory_space=pltpu.VMEM)
    return pl.pallas_call(
        functools.partial(scale_kernel, model_dim=model_dim),
        out_shape=jax.ShapeDtypeStruct(mixed.shape, BF),
        in_specs=[vmem] * 7,
        out_specs=vmem,
        compiler_params=pltpu.CompilerParams(vmem_limit_bytes=VMEM_LIMIT),
        name="scale",
    )(in_vmem(mixed), in_vmem(hub_mixed), *[in_vmem(x) for x in lines], gain)


def from_others(x, size):
    return [
        lax.ppermute(x, "feat", [((i + shift) % size, i) for i in range(size)])
        for shift in range(1, size)
    ]


def on_device(
    embeddings,
    self_weight,
    bases,
    basis_coef,
    out_gain,
    edge_src,
    edge_dst,
    block_rel,
    mirror_master_rows,
    block_count,
):
    owners = lax.axis_size("dom")
    feat_size = lax.axis_size("feat")
    feat = lax.axis_index("feat").astype(jnp.int32)
    blocks = edge_src.shape[0]
    n_local, cols = embeddings.shape
    model_dim = bases.shape[1]
    feat_at = feat.reshape(1)
    ahead = [((i + 1) % feat_size, i) for i in range(feat_size)]
    behind = [(i, (i + 1) % feat_size) for i in range(feat_size)]
    after = lax.ppermute(embeddings, "feat", ahead)
    before = lax.ppermute(embeddings, "feat", behind)

    words, lhs = prepare(
        block_count, edge_src, edge_dst, block_rel, basis_coef, owners, n_local // TILE, 16
    )
    steps = 9
    weights = mix(feat_at, lhs, bases, blocks, 0, steps)
    weights, after, before = lax.optimization_barrier((weights, after, before))
    half = n_local // 2
    halves = [
        lax.ppermute(after[:half], "feat", ahead),
        lax.ppermute(before[half:], "feat", behind),
    ]
    weights = mix(feat_at, lhs, bases, blocks, steps, None, weights)
    pieces = [embeddings, after, before] + halves
    edges = (edge_src, edge_dst)
    mirror_part = blocks_call(words, weights, *edges, pieces, owners, False)
    mirror = lax.all_to_all(mirror_part, "dom", split_axis=0, concat_axis=0, tiled=True)
    weights, _ = lax.optimization_barrier((weights, mirror_part))
    hub_part = blocks_call(words, weights, *edges, pieces, owners, True)
    hub_part, mirror = lax.optimization_barrier((hub_part, mirror))
    hub = lax.all_to_all(hub_part, "dom", split_axis=0, concat_axis=0, tiled=True)

    mixed, squares = mirror_final(
        feat.reshape(1), mirror, mirror_master_rows.reshape(owners, TILE), self_weight, pieces
    )
    hub_mixed, line = hub_final(hub, mixed, squares)
    lines = [line] + from_others(line, feat_size)
    return scale(mixed, hub_mixed, lines, out_gain.reshape(1, cols), model_dim)


def solution(mesh):
    in_specs = (
        P("dom", "feat"),
        P(None, "feat"),
        P(None, None, "feat"),
        P(),
        P("feat"),
        P("dom", None),
        P("dom", None),
        P("dom"),
        P("dom"),
        P("dom"),
    )
    out_specs = P("dom", "feat")
    return jax.shard_map(
        on_device, mesh=mesh, in_specs=in_specs, out_specs=out_specs, check_vma=False
    )
```

```python
import functools

import jax
import jax.numpy as jnp
from jax import lax
from jax.experimental import pallas as pl
from jax.experimental.pallas import tpu as pltpu
from jax.sharding import PartitionSpec as P

TILE = 128
HUB_MIRRORS = 128
CAP = 128
DEG_ROWS = 16
VMEM_LIMIT = 44 * 1024 * 1024
BF = jnp.bfloat16
F32 = jnp.float32
HOT = jnp.float8_e4m3fn


def prepare_kernel(
    live_ref,
    src_hbm,
    dst_hbm,
    rel_hbm,
    coef_hbm,
    words_ref,
    lhs_ref,
    spread,
    src_ref,
    dst_ref,
    rel_ref,
    coef_ref,
    sems,
    *,
    owners,
    src_tiles,
    group,
):
    loads = [
        pltpu.make_async_copy(a, b, sems.at[i])
        for i, (a, b) in enumerate(
            [(src_hbm, src_ref), (dst_hbm, dst_ref), (rel_hbm, rel_ref), (coef_hbm, coef_ref)]
        )
    ]
    for load in loads:
        load.start()
    for load in loads:
        load.wait()
    blocks = src_ref.shape[0]
    n_bases, relations = coef_ref.shape
    live = live_ref[0]
    src_tile = src_ref[:, :1] >> 7
    dst_tile = dst_ref[:, :1] >> 7
    index = lax.broadcasted_iota(jnp.int32, (blocks, 1), 0)
    active = index < live
    key = jnp.where(dst_tile < owners, src_tiles, 0) + src_tile
    key = jnp.where(active, key, TILE - 1)
    key_wide = jnp.broadcast_to(key, (blocks, TILE))
    key_row = key_wide.astype(F32).T[:1, :]
    lane = lax.broadcasted_iota(jnp.int32, (1, TILE), 1)
    same_key = key_wide == lane
    count = jnp.sum(same_key.astype(F32), axis=0, keepdims=True)
    count = jnp.where(lane < 2 * src_tiles, count, 0.0).astype(jnp.int32)
    pairs = (count + 1) >> 1
    earlier = lax.broadcasted_iota(jnp.int32, (TILE, TILE), 0) < lax.broadcasted_iota(
        jnp.int32, (TILE, TILE), 1
    )
    pairs_wide = jnp.broadcast_to(pairs, (8, TILE)).astype(F32).astype(BF)
    start = jnp.dot(
        pairs_wide, jnp.where(earlier, 1.0, 0.0).astype(BF), preferred_element_type=F32
    )[:1].astype(jnp.int32)
    zero = jnp.zeros_like(pairs)
    mirror_pairs = jnp.sum(
        jnp.where(lane < src_tiles, pairs, zero).astype(F32), axis=1, keepdims=True
    ).astype(jnp.int32)
    hub_pairs = jnp.sum(
        jnp.where(lane >= src_tiles, pairs, zero).astype(F32), axis=1, keepdims=True
    ).astype(jnp.int32)
    shift = group.bit_length() - 1
    mirror_groups = (mirror_pairs + group - 1) >> shift
    hub_groups = (hub_pairs + group - 1) >> shift
    start = start + jnp.where(lane >= src_tiles, mirror_groups * group - mirror_pairs, 0)
    other = lax.broadcasted_iota(jnp.int32, (1, blocks), 1)
    before = (key.astype(F32) == key_row) & (other < index)
    rank = jnp.sum(before.astype(F32), axis=1, keepdims=True).astype(jnp.int32)
    first = jnp.sum(
        jnp.where(same_key, start, 0).astype(F32), axis=1, keepdims=True
    ).astype(jnp.int32)
    place = jnp.where(active, 2 * first + rank, -1)
    word = index | (src_tile << 9) | (dst_tile << 14) | (1 << 20)
    slots = words_ref.shape[1] - TILE
    slot = lax.broadcasted_iota(jnp.int32, (1, slots), 1)
    words = jnp.sum(jnp.where(place == slot, word, 0), axis=0, keepdims=True)
    padding = lax.rem(slot, blocks) | ((slot & 31) << 14)
    words_ref[:, :slots] = jnp.where(words == 0, padding, words)
    words_ref[:, slots:] = jnp.where(
        lane == 0, mirror_groups, jnp.where(lane == 1, mirror_groups + hub_groups, 0)
    )

    rel_wide = jnp.broadcast_to(rel_ref[...].astype(F32), (TILE, blocks)).T[:, :1]
    relation = rel_wide.astype(jnp.int32)
    span = lax.broadcasted_iota(jnp.int32, (1, relations), 1)
    one_hot = jnp.where(relation == span, 1.0, 0.0).astype(BF)
    mixing = lax.dot_general(
        one_hot, coef_ref[...], (((1,), (1,)), ((), ())), preferred_element_type=F32
    )
    copies = lhs_ref.shape[1] // n_bases
    blank = jnp.zeros_like(mixing)
    for i in range(copies):
        row = jnp.concatenate([mixing if k == i else blank for k in range(copies)], axis=1)
        for half in range(copies * n_bases // TILE):
            spread[half, pl.ds(i, blocks, stride=copies), :] = row[:, half * TILE : (half + 1) * TILE]
    for half in range(copies * n_bases // TILE):
        lhs_ref[:, half * TILE : (half + 1) * TILE] = spread[half].astype(BF)


def prepare(live, edge_src, edge_dst, block_rel, basis_coef, owners, src_tiles, group):
    blocks = edge_src.shape[0]
    n_bases = basis_coef.shape[1]
    slots = 2 * group * (-(-(blocks + 2 * src_tiles) // (2 * group)) + 1)
    slots = -(-slots // TILE) * TILE
    vmem = pl.BlockSpec(memory_space=pltpu.VMEM)
    return pl.pallas_call(
        functools.partial(prepare_kernel, owners=owners, src_tiles=src_tiles, group=group),
        out_shape=(
            jax.ShapeDtypeStruct((1, slots + TILE), jnp.int32),
            jax.ShapeDtypeStruct((4 * blocks, 4 * n_bases), BF),
        ),
        in_specs=[pl.BlockSpec(memory_space=pltpu.SMEM)] + [pl.BlockSpec(memory_space=pl.ANY)] * 4,
        out_specs=(vmem, vmem),
        scratch_shapes=[
            pltpu.VMEM((4 * n_bases // TILE, 4 * blocks, TILE), F32),
            pltpu.VMEM(edge_src.shape, jnp.int32),
            pltpu.VMEM(edge_dst.shape, jnp.int32),
            pltpu.VMEM((1, blocks), jnp.int32),
            pltpu.VMEM(basis_coef.shape[::-1], BF),
            pltpu.SemaphoreType.DMA((4,)),
        ],
        compiler_params=pltpu.CompilerParams(vmem_limit_bytes=VMEM_LIMIT),
        name="prepare",
    )(
        live,
        in_hbm(edge_src),
        in_hbm(edge_dst),
        in_hbm(block_rel.reshape(1, blocks)),
        in_hbm(basis_coef.T),
    )


def mix_kernel(feat_ref, lhs_ref, bases_ref, *rest, chunk):
    w_ref, spread, rights = rest[-3:]
    n_bases, depth, cols = bases_ref.shape
    spread[:, :depth, :] = bases_ref[...].astype(F32)
    pitch = spread.shape[1]
    flat = spread.reshape(n_bases * pitch, cols)
    for d in range(depth):
        octet, half, row = d // 8, d % 8 // 4, d % 4
        rows = slice(row * n_bases, (row + 1) * n_bases)
        rights[octet, rows, half * cols : (half + 1) * cols] = flat[
            pl.ds(d, n_bases, stride=pitch), :
        ].astype(BF)
    pairs = chunk // 8
    low = lax.broadcasted_iota(jnp.int32, (pairs, 8, cols), 1) < 4
    for row in range(0, lhs_ref.shape[0], chunk):
        left = lhs_ref[row : row + chunk, :]
        pair = row // 8
        for first_octet in range(0, depth // 8, 2):
            evens, odds = [], []
            for octet in (first_octet, first_octet + 1):
                out = jnp.dot(left, rights[octet], preferred_element_type=F32)
                first = out[:, :cols].reshape(pairs, 8, cols)
                second = out[:, cols:].reshape(pairs, 8, cols)
                evens.append(jnp.where(low, first, pltpu.roll(second, 4, 1)))
                odds.append(jnp.where(low, pltpu.roll(first, 4, 1), second))
            at = slice(first_octet * 8, first_octet * 8 + 16)
            w_ref[pair : pair + pairs, 0, at] = jnp.concatenate(evens, axis=1).astype(BF)
            w_ref[pair : pair + pairs, 1, at] = jnp.concatenate(odds, axis=1).astype(BF)


def mix(feat, lhs, bases, blocks, begin=0, end=None, earlier=None):
    n_bases, model_dim, cols = bases.shape
    depth = 32
    steps = model_dim // depth
    end = steps if end is None else end
    per_part = cols // depth

    def bases_at(i, f):
        return (0, lax.rem(i + begin + f[0] * per_part, steps), 0)

    more = [] if earlier is None else [earlier]
    return pl.pallas_call(
        functools.partial(mix_kernel, chunk=512),
        out_shape=jax.ShapeDtypeStruct((blocks // 2, 2, model_dim, cols), BF),
        grid_spec=pltpu.PrefetchScalarGridSpec(
            num_scalar_prefetch=1,
            grid=(end - begin,),
            in_specs=[
                pl.BlockSpec(lhs.shape, lambda i, f: (0, 0)),
                pl.BlockSpec((n_bases, depth, cols), bases_at),
            ]
            + [pl.BlockSpec(memory_space=pl.ANY)] * len(more),
            out_specs=pl.BlockSpec(
                (blocks // 2, 2, depth, cols),
                lambda i, f: (0, 0, i + begin, 0),
            ),
            scratch_shapes=[
                pltpu.VMEM((n_bases, depth + 8, cols), F32),
                pltpu.VMEM((depth // 8, 4 * n_bases, 2 * cols), BF),
            ],
        ),
        input_output_aliases={3: 0} if more else {},
        cost_estimate=pl.CostEstimate(
            flops=8 * blocks * n_bases * depth * (end - begin) * cols,
            bytes_accessed=blocks * depth * (end - begin) * cols * 2,
            transcendentals=0,
        ),
        compiler_params=pltpu.CompilerParams(vmem_limit_bytes=VMEM_LIMIT),
        name="mix" if earlier is None else "mix_rest",
    )(feat, lhs, in_hbm(bases), *more)


def in_vmem(x):
    return pltpu.with_memory_space_constraint(x, pltpu.VMEM)


def in_hbm(x):
    return pltpu.with_memory_space_constraint(x, pltpu.HBM)


def joins(joined, halves, sems, first_sem):
    rows = halves[0].shape[0]
    return [
        pltpu.make_async_copy(half, joined.at[pl.ds(i * rows, rows)], sems.at[first_sem + i])
        for i, half in enumerate(halves)
    ]


def unpack(word):
    return word & 511, (word >> 9) & 31, (word >> 14) & 63, word >> 20


def blocks_kernel(*refs, group, owners, split, hubs):
    word_ref, src_hbm, dst_hbm = refs[:3]
    pieces, halves = refs[3:6], refs[6:8]
    w_ref, out_hbm, acc, deg, held, joined, src_ref, dst_ref, out_ref, sems = refs[8:]
    spans = word_ref.shape[1] - TILE
    first_group = word_ref[0, spans] if hubs else 0
    end_group = word_ref[0, spans + int(hubs)]

    def fetch(at):
        side = at & 1
        for k in range(2 * group):
            block = word_ref[0, at * (2 * group) + k] & 511
            pltpu.make_async_copy(
                w_ref.at[block >> 1, block & 1], held.at[side, k // 2, k % 2], sems.at[side]
            ).start()

    @pl.when(first_group < end_group)
    def _():
        fetch(first_group)

    loads = joins(joined, halves, sems, 2)
    loads.append(pltpu.make_async_copy(src_hbm, src_ref, sems.at[4]))
    loads.append(pltpu.make_async_copy(dst_hbm, dst_ref, sems.at[5]))
    for load in loads:
        load.start()
    acc[...] = jnp.zeros_like(acc)
    deg[...] = jnp.zeros_like(deg)
    for load in loads:
        load.wait()

    def body(here, carry):
        side = here & 1

        @pl.when(here + 1 < end_group)
        def _():
            fetch(here + 1)

        def arrive():
            pltpu.make_async_copy(
                w_ref.at[pl.ds(0, group)], held.at[side], sems.at[side]
            ).wait()

        if not hubs:
            arrive()
        slot = lax.broadcasted_iota(jnp.int32, (TILE, TILE), 0).astype(F32).astype(BF)
        lane = lax.broadcasted_iota(jnp.int32, (TILE, TILE), 1)
        one = jnp.ones((TILE, TILE), BF)
        zero = jnp.zeros((TILE, TILE), BF)

        def diagonal(first, second):
            top = jnp.concatenate([first, zero], axis=1)
            bottom = jnp.concatenate([zero, second], axis=1)
            return jnp.concatenate([top, bottom], axis=0)

        def fields(pair, k):
            return unpack(word_ref[0, (here * group + pair) * 2 + k])

        def adjacency(pair):
            dst_hot, src_hot, count = [], [], None
            for k in range(2):
                block, src_tile, dst_tile, used = fields(pair, k)
                base = jnp.where(used > 0, dst_tile * TILE, 1 << 20)
                dst = (dst_ref[pl.ds(block, 1), :] - base).astype(F32).astype(BF)
                src = (src_ref[pl.ds(block, 1), :] - src_tile * TILE).astype(F32).astype(BF)
                dst_hot.append(jnp.where(slot == dst, one, zero))
                src_hot.append(jnp.where(slot == src, one, zero))
                column = jnp.sum(dst_hot[k].astype(F32), axis=1, keepdims=True)
                extra = jnp.where(lane == lax.rem(dst_tile, owners), column, 0.0)
                count = extra if count is None else count + extra
            found = lax.dot_general(
                jnp.concatenate(dst_hot, axis=1).astype(HOT),
                diagonal(src_hot[0], src_hot[1]).astype(HOT),
                (((1,), (1,)), ((), ())),
                preferred_element_type=F32,
            )
            return found.astype(BF), count

        def message(pair):
            src_tile = fields(pair, 0)[1]
            rows = pl.ds(pl.multiple_of(src_tile * TILE, TILE), TILE)
            tile = jnp.concatenate(
                [pieces[0][rows, :], pieces[1][rows, :], joined[rows, :], pieces[2][rows, :]],
                axis=1,
            )
            weight = jnp.concatenate([held[side, pair, 0], held[side, pair, 1]], axis=1)
            out = jnp.dot(tile, weight, preferred_element_type=F32).astype(BF)
            return diagonal(out[:, :TILE], out[:, TILE:])

        total = deg[...]
        for first in range(0, group, split):
            pairs = range(first, first + split)
            found = [adjacency(pair) for pair in pairs]
            if hubs and first == 0:
                arrive()
            messages = [message(pair) for pair in pairs]
            sums = [
                jnp.dot(f[0], m, preferred_element_type=F32) for f, m in zip(found, messages)
            ]
            for pair, both, part in zip(pairs, sums, found):
                total = total + part[1]
                for k in range(2):
                    dst = lax.rem(fields(pair, k)[2], owners)
                    acc[dst] = acc[dst] + both[:, k * TILE : (k + 1) * TILE]
        deg[...] = total
        return carry

    lax.fori_loop(first_group, end_group, body, 0)

    deg[...] = deg[...].T
    line = lax.broadcasted_iota(jnp.int32, (DEG_ROWS, TILE), 0)
    for at in range(owners):
        degree = deg[at : at + 1, :]
        high = jnp.floor(degree * (1.0 / 256.0)) * 256.0
        low = degree - high
        out_ref[at, :TILE, :] = acc[at].astype(BF)
        rows = jnp.where(line == 0, high, jnp.where(line == 1, low, 0.0))
        out_ref[at, TILE:, :] = rows.astype(BF)
    leave = pltpu.make_async_copy(out_ref, out_hbm, sems.at[2])
    leave.start()
    leave.wait()


def blocks_call(words, weights, edge_src, edge_dst, pieces, owners, hubs, group=16, split=16):
    pair_count, _, model_dim, cols = weights.shape
    vmem = pl.BlockSpec(memory_space=pltpu.VMEM)
    smem = pl.BlockSpec(memory_space=pltpu.SMEM)
    anywhere = pl.BlockSpec(memory_space=pl.ANY)
    return pl.pallas_call(
        functools.partial(blocks_kernel, group=group, owners=owners, split=split, hubs=hubs),
        out_shape=pltpu.HBM((owners, TILE + DEG_ROWS, cols), BF),
        in_specs=[smem, anywhere, anywhere] + [vmem] * 3 + [anywhere] * 3,
        out_specs=anywhere,
        scratch_shapes=[
            pltpu.VMEM((owners, TILE, cols), F32),
            pltpu.VMEM((TILE, TILE), F32),
            pltpu.VMEM((2, group, 2, model_dim, cols), BF),
            pltpu.VMEM(pieces[0].shape, BF),
            pltpu.VMEM(edge_src.shape, jnp.int32),
            pltpu.VMEM(edge_dst.shape, jnp.int32),
            pltpu.VMEM((owners, TILE + DEG_ROWS, cols), BF),
            pltpu.SemaphoreType.DMA((6,)),
        ],
        cost_estimate=pl.CostEstimate(
            flops=pair_count * 4 * TILE * model_dim * cols,
            bytes_accessed=pair_count * model_dim * cols * 2,
            transcendentals=0,
        ),
        compiler_params=pltpu.CompilerParams(vmem_limit_bytes=VMEM_LIMIT),
        name="hub_blocks" if hubs else "mirror_blocks",
    )(
        words,
        in_hbm(edge_src),
        in_hbm(edge_dst),
        *[in_vmem(x) for x in pieces[:3]],
        *[in_hbm(x) for x in pieces[3:]],
        weights,
    )


def square_lines(value):
    squares = jnp.sum(value * value, axis=1, keepdims=True)
    line = jnp.broadcast_to(squares, value.shape).T[:1, :]
    pieces = [line[:, i : i + TILE] for i in range(0, value.shape[0], TILE)]
    return jnp.concatenate(pieces, axis=0)


def mirror_kernel(
    feat_ref,
    mirror_hbm,
    master_ref,
    self_ref,
    x0_hbm,
    x1_hbm,
    x3_hbm,
    first_hbm,
    second_hbm,
    mixed_ref,
    squares_ref,
    right,
    turned,
    mirror_ref,
    table,
    sems,
    *,
    chunk,
    reach,
):
    step = pl.program_id(0)
    owners = mirror_ref.shape[0]
    cols = mirror_ref.shape[2]

    @pl.when(step == 0)
    def _():
        arrival = pltpu.make_async_copy(mirror_hbm, mirror_ref, sems.at[0])
        arrival.start()
        half = first_hbm.shape[0]
        targets = [
            (x0_hbm, table.at[:, :cols]),
            (x1_hbm, table.at[:, cols : 2 * cols]),
            (x3_hbm, table.at[:, 3 * cols :]),
            (first_hbm, table.at[:half, 2 * cols : 3 * cols]),
            (second_hbm, table.at[half:, 2 * cols : 3 * cols]),
        ]
        loads = [
            pltpu.make_async_copy(a, b, sems.at[1 + i]) for i, (a, b) in enumerate(targets)
        ]
        for load in loads:
            load.start()
        for p in range(4):
            at = pl.multiple_of(lax.rem(feat_ref[0] + p, 4) * cols, cols)
            turned[p * cols : (p + 1) * cols, :] = self_ref[pl.ds(at, cols), :]
        arrival.wait()
        high = mirror_ref[:, TILE, :].astype(F32)
        low = mirror_ref[:, TILE + 1, :].astype(F32)
        pad = jnp.zeros((TILE - 2 * owners, TILE), F32)
        turned_counts = jnp.concatenate([high, low, pad], axis=0).T
        lane = lax.broadcasted_iota(jnp.int32, (TILE, TILE), 1)
        for p in range(owners):
            rows = slice(p * TILE, (p + 1) * TILE)
            right[rows, :cols] = mirror_ref[p, :TILE, :]
            keep = (lane == p) | (lane == p + owners)
            right[rows, cols:] = jnp.where(keep, turned_counts, 0.0).astype(BF)
        for load in loads:
            load.wait()

    rows = pl.ds(pl.multiple_of(step * chunk, chunk), chunk)
    own = jnp.dot(table[rows, :], turned[...], preferred_element_type=F32)

    @pl.when(step * chunk < reach)
    def _():
        local = lax.broadcasted_iota(jnp.int32, (TILE, TILE), 0).astype(F32).astype(BF)
        one = jnp.ones((TILE, TILE), BF)
        zero = jnp.zeros((TILE, TILE), BF)
        columns = []
        for p in range(owners):
            column = []
            for first in range(0, chunk, TILE):
                target = master_ref[p : p + 1, :] - (step * chunk + first)
                column.append(jnp.where(local == target.astype(F32).astype(BF), one, zero))
            columns.append(jnp.concatenate(column, axis=0))
        sums = jnp.dot(jnp.concatenate(columns, axis=1), right[...], preferred_element_type=F32)
        degree = jnp.sum(sums[:, cols:], axis=1, keepdims=True)
        mixed = own + sums[:, :cols] * lax.rsqrt(jnp.maximum(degree, 1.0))
        mixed_ref[...] = mixed
        squares_ref[...] = square_lines(mixed)

    @pl.when(step * chunk >= reach)
    def _():
        mixed_ref[...] = own
        squares_ref[...] = square_lines(own)


def mirror_final(feat, mirror, master, self_weight, pieces):
    n_local, cols = pieces[0].shape
    owners = mirror.shape[0]
    chunk = 1024
    anywhere = pl.BlockSpec(memory_space=pl.ANY)
    whole = lambda shape: pl.BlockSpec(shape, lambda i, *_: (0,) * len(shape))
    return pl.pallas_call(
        functools.partial(mirror_kernel, chunk=chunk, reach=n_local - n_local // 4),
        out_shape=(
            jax.ShapeDtypeStruct((n_local, cols), F32),
            jax.ShapeDtypeStruct((n_local // TILE, TILE), F32),
        ),
        grid_spec=pltpu.PrefetchScalarGridSpec(
            num_scalar_prefetch=1,
            grid=(n_local // chunk,),
            in_specs=[anywhere, whole(master.shape), whole(self_weight.shape)]
            + [anywhere] * len(pieces),
            out_specs=(
                pl.BlockSpec((chunk, cols), lambda i, *_: (i, 0)),
                pl.BlockSpec((chunk // TILE, TILE), lambda i, *_: (i, 0)),
            ),
            scratch_shapes=[
                pltpu.VMEM((owners * TILE, 2 * cols), BF),
                pltpu.VMEM(self_weight.shape, BF),
                pltpu.VMEM(mirror.shape, BF),
                pltpu.VMEM((n_local, 4 * cols), BF),
                pltpu.SemaphoreType.DMA((1 + len(pieces),)),
            ],
        ),
        cost_estimate=pl.CostEstimate(
            flops=n_local * n_local * 4 * cols, bytes_accessed=8 << 20, transcendentals=0
        ),
        compiler_params=pltpu.CompilerParams(vmem_limit_bytes=VMEM_LIMIT),
        name="mirror_final",
    )(feat, in_hbm(mirror), master, self_weight, *[in_hbm(p) for p in pieces])


def hub_kernel(hub_ref, mixed_ref, squares_ref, out_ref, lines_ref):
    hub = jnp.sum(hub_ref[:, :TILE, :].astype(F32), axis=0)
    counts = hub_ref[:, TILE : TILE + DEG_ROWS, :].astype(F32)
    line = jnp.sum(jnp.sum(counts, axis=0), axis=0, keepdims=True)
    column = jnp.broadcast_to(line, (TILE, TILE)).T[:, :1]
    mixed = mixed_ref[:HUB_MIRRORS, :] + hub * lax.rsqrt(jnp.maximum(column, 1.0))
    out_ref[...] = mixed
    lines_ref[...] = squares_ref[...]
    lines_ref[:1, :] = square_lines(mixed)


def hub_final(hub, mixed, squares):
    vmem = pl.BlockSpec(memory_space=pltpu.VMEM)
    return pl.pallas_call(
        hub_kernel,
        out_shape=(
            jax.ShapeDtypeStruct((HUB_MIRRORS, mixed.shape[1]), F32),
            jax.ShapeDtypeStruct(squares.shape, F32),
        ),
        in_specs=[vmem] * 3,
        out_specs=(vmem, vmem),
        compiler_params=pltpu.CompilerParams(vmem_limit_bytes=VMEM_LIMIT),
        name="hub_final",
    )(hub, in_vmem(mixed), in_vmem(squares))


def scale_kernel(mixed_ref, hub_ref, a_ref, b_ref, c_ref, d_ref, gain_ref, out_ref, *, model_dim):
    lines = a_ref[...] + b_ref[...] + c_ref[...] + d_ref[...]
    norm = lax.rsqrt(lines / model_dim + 1e-05)
    gain = gain_ref[...]
    tiles, width = norm.shape
    for i in range(tiles):
        rows = slice(i * width, (i + 1) * width)
        value = hub_ref[...] if i == 0 else mixed_ref[rows, :]
        column = jnp.broadcast_to(norm[i : i + 1, :], (width, width)).T
        out_ref[rows, :] = (value * column * gain).astype(BF)


def scale(mixed, hub_mixed, lines, gain, model_dim):
    vmem = pl.BlockSpec(memory_space=pltpu.VMEM)
    return pl.pallas_call(
        functools.partial(scale_kernel, model_dim=model_dim),
        out_shape=jax.ShapeDtypeStruct(mixed.shape, BF),
        in_specs=[vmem] * 7,
        out_specs=vmem,
        compiler_params=pltpu.CompilerParams(vmem_limit_bytes=VMEM_LIMIT),
        name="scale",
    )(in_vmem(mixed), in_vmem(hub_mixed), *[in_vmem(x) for x in lines], gain)


def from_others(x, size):
    return [
        lax.ppermute(x, "feat", [((i + shift) % size, i) for i in range(size)])
        for shift in range(1, size)
    ]


def on_device(
    embeddings,
    self_weight,
    bases,
    basis_coef,
    out_gain,
    edge_src,
    edge_dst,
    block_rel,
    mirror_master_rows,
    block_count,
):
    owners = lax.axis_size("dom")
    feat_size = lax.axis_size("feat")
    feat = lax.axis_index("feat").astype(jnp.int32)
    blocks = edge_src.shape[0]
    n_local, cols = embeddings.shape
    model_dim = bases.shape[1]
    feat_at = feat.reshape(1)
    ahead = [((i + 1) % feat_size, i) for i in range(feat_size)]
    behind = [(i, (i + 1) % feat_size) for i in range(feat_size)]
    after = lax.ppermute(embeddings, "feat", ahead)
    before = lax.ppermute(embeddings, "feat", behind)

    words, lhs = prepare(
        block_count, edge_src, edge_dst, block_rel, basis_coef, owners, n_local // TILE, 16
    )
    steps = 9
    weights = mix(feat_at, lhs, bases, blocks, 0, steps)
    weights, after, before = lax.optimization_barrier((weights, after, before))
    half = n_local // 2
    halves = [
        lax.ppermute(after[:half], "feat", ahead),
        lax.ppermute(before[half:], "feat", behind),
    ]
    weights = mix(feat_at, lhs, bases, blocks, steps, None, weights)
    pieces = [embeddings, after, before] + halves
    edges = (edge_src, edge_dst)
    mirror_part = blocks_call(words, weights, *edges, pieces, owners, False)
    mirror = lax.all_to_all(mirror_part, "dom", split_axis=0, concat_axis=0, tiled=True)
    weights, _ = lax.optimization_barrier((weights, mirror_part))
    hub_part = blocks_call(words, weights, *edges, pieces, owners, True)
    hub_part, mirror = lax.optimization_barrier((hub_part, mirror))
    hub = lax.all_to_all(hub_part, "dom", split_axis=0, concat_axis=0, tiled=True)

    mixed, squares = mirror_final(
        feat.reshape(1), mirror, mirror_master_rows.reshape(owners, TILE), self_weight, pieces
    )
    hub_mixed, line = hub_final(hub, mixed, squares)
    lines = [line] + from_others(line, feat_size)
    return scale(mixed, hub_mixed, lines, out_gain.reshape(1, cols), model_dim)


def solution(mesh):
    in_specs = (
        P("dom", "feat"),
        P(None, "feat"),
        P(None, None, "feat"),
        P(),
        P("feat"),
        P("dom", None),
        P("dom", None),
        P("dom"),
        P("dom"),
        P("dom"),
    )
    out_specs = P("dom", "feat")
    return jax.shard_map(
        on_device, mesh=mesh, in_specs=in_specs, out_specs=out_specs, check_vma=False
    )
```

```python
import functools

import jax
import jax.numpy as jnp
from jax import lax
from jax.experimental import pallas as pl
from jax.experimental.pallas import tpu as pltpu
from jax.sharding import PartitionSpec as P

TILE = 128
HUB_MIRRORS = 128
CAP = 128
DEG_ROWS = 16
VMEM_LIMIT = 44 * 1024 * 1024
BF = jnp.bfloat16
F32 = jnp.float32
HOT = jnp.float8_e4m3fn


def prepare_kernel(
    live_ref,
    src_hbm,
    dst_hbm,
    rel_hbm,
    coef_hbm,
    words_ref,
    lhs_ref,
    spread,
    src_ref,
    dst_ref,
    rel_ref,
    coef_ref,
    sems,
    *,
    owners,
    src_tiles,
    group,
):
    loads = [
        pltpu.make_async_copy(a, b, sems.at[i])
        for i, (a, b) in enumerate(
            [(src_hbm, src_ref), (dst_hbm, dst_ref), (rel_hbm, rel_ref), (coef_hbm, coef_ref)]
        )
    ]
    for load in loads:
        load.start()
    for load in loads:
        load.wait()
    blocks = src_ref.shape[0]
    n_bases, relations = coef_ref.shape
    live = live_ref[0]
    src_tile = src_ref[:, :1] >> 7
    dst_tile = dst_ref[:, :1] >> 7
    index = lax.broadcasted_iota(jnp.int32, (blocks, 1), 0)
    active = index < live
    key = jnp.where(dst_tile < owners, src_tiles, 0) + src_tile
    key = jnp.where(active, key, TILE - 1)
    key_wide = jnp.broadcast_to(key, (blocks, TILE))
    key_row = key_wide.astype(F32).T[:1, :]
    lane = lax.broadcasted_iota(jnp.int32, (1, TILE), 1)
    same_key = key_wide == lane
    count = jnp.sum(same_key.astype(F32), axis=0, keepdims=True)
    count = jnp.where(lane < 2 * src_tiles, count, 0.0).astype(jnp.int32)
    pairs = (count + 1) >> 1
    earlier = lax.broadcasted_iota(jnp.int32, (TILE, TILE), 0) < lax.broadcasted_iota(
        jnp.int32, (TILE, TILE), 1
    )
    pairs_wide = jnp.broadcast_to(pairs, (8, TILE)).astype(F32).astype(BF)
    start = jnp.dot(
        pairs_wide, jnp.where(earlier, 1.0, 0.0).astype(BF), preferred_element_type=F32
    )[:1].astype(jnp.int32)
    zero = jnp.zeros_like(pairs)
    mirror_pairs = jnp.sum(
        jnp.where(lane < src_tiles, pairs, zero).astype(F32), axis=1, keepdims=True
    ).astype(jnp.int32)
    hub_pairs = jnp.sum(
        jnp.where(lane >= src_tiles, pairs, zero).astype(F32), axis=1, keepdims=True
    ).astype(jnp.int32)
    shift = group.bit_length() - 1
    mirror_groups = (mirror_pairs + group - 1) >> shift
    hub_groups = (hub_pairs + group - 1) >> shift
    start = start + jnp.where(lane >= src_tiles, mirror_groups * group - mirror_pairs, 0)
    other = lax.broadcasted_iota(jnp.int32, (1, blocks), 1)
    before = (key.astype(F32) == key_row) & (other < index)
    rank = jnp.sum(before.astype(F32), axis=1, keepdims=True).astype(jnp.int32)
    first = jnp.sum(
        jnp.where(same_key, start, 0).astype(F32), axis=1, keepdims=True
    ).astype(jnp.int32)
    place = jnp.where(active, 2 * first + rank, -1)
    word = index | (src_tile << 9) | (dst_tile << 14) | (1 << 20)
    slots = words_ref.shape[1] - TILE
    slot = lax.broadcasted_iota(jnp.int32, (1, slots), 1)
    words = jnp.sum(jnp.where(place == slot, word, 0), axis=0, keepdims=True)
    padding = lax.rem(slot, blocks) | ((slot & 31) << 14)
    words_ref[:, :slots] = jnp.where(words == 0, padding, words)
    words_ref[:, slots:] = jnp.where(
        lane == 0, mirror_groups, jnp.where(lane == 1, mirror_groups + hub_groups, 0)
    )

    rel_wide = jnp.broadcast_to(rel_ref[...].astype(F32), (TILE, blocks)).T[:, :1]
    relation = rel_wide.astype(jnp.int32)
    span = lax.broadcasted_iota(jnp.int32, (1, relations), 1)
    one_hot = jnp.where(relation == span, 1.0, 0.0).astype(BF)
    mixing = lax.dot_general(
        one_hot, coef_ref[...], (((1,), (1,)), ((), ())), preferred_element_type=F32
    )
    copies = lhs_ref.shape[1] // n_bases
    blank = jnp.zeros_like(mixing)
    for i in range(copies):
        row = jnp.concatenate([mixing if k == i else blank for k in range(copies)], axis=1)
        for half in range(copies * n_bases // TILE):
            spread[half, pl.ds(i, blocks, stride=copies), :] = row[:, half * TILE : (half + 1) * TILE]
    for half in range(copies * n_bases // TILE):
        lhs_ref[:, half * TILE : (half + 1) * TILE] = spread[half].astype(BF)


def prepare(live, edge_src, edge_dst, block_rel, basis_coef, owners, src_tiles, group):
    blocks = edge_src.shape[0]
    n_bases = basis_coef.shape[1]
    slots = 2 * group * (-(-(blocks + 2 * src_tiles) // (2 * group)) + 1)
    slots = -(-slots // TILE) * TILE
    vmem = pl.BlockSpec(memory_space=pltpu.VMEM)
    return pl.pallas_call(
        functools.partial(prepare_kernel, owners=owners, src_tiles=src_tiles, group=group),
        out_shape=(
            jax.ShapeDtypeStruct((1, slots + TILE), jnp.int32),
            jax.ShapeDtypeStruct((4 * blocks, 4 * n_bases), BF),
        ),
        in_specs=[pl.BlockSpec(memory_space=pltpu.SMEM)] + [pl.BlockSpec(memory_space=pl.ANY)] * 4,
        out_specs=(vmem, vmem),
        scratch_shapes=[
            pltpu.VMEM((4 * n_bases // TILE, 4 * blocks, TILE), F32),
            pltpu.VMEM(edge_src.shape, jnp.int32),
            pltpu.VMEM(edge_dst.shape, jnp.int32),
            pltpu.VMEM((1, blocks), jnp.int32),
            pltpu.VMEM(basis_coef.shape[::-1], BF),
            pltpu.SemaphoreType.DMA((4,)),
        ],
        compiler_params=pltpu.CompilerParams(vmem_limit_bytes=VMEM_LIMIT),
        name="prepare",
    )(
        live,
        in_hbm(edge_src),
        in_hbm(edge_dst),
        in_hbm(block_rel.reshape(1, blocks)),
        in_hbm(basis_coef.T),
    )


def mix_kernel(feat_ref, lhs_ref, bases_ref, *rest, chunk):
    w_ref, spread, rights = rest[-3:]
    n_bases, depth, cols = bases_ref.shape
    spread[:, :depth, :] = bases_ref[...].astype(F32)
    pitch = spread.shape[1]
    flat = spread.reshape(n_bases * pitch, cols)
    for d in range(depth):
        octet, half, row = d // 8, d % 8 // 4, d % 4
        rows = slice(row * n_bases, (row + 1) * n_bases)
        rights[octet, rows, half * cols : (half + 1) * cols] = flat[
            pl.ds(d, n_bases, stride=pitch), :
        ].astype(BF)
    pairs = chunk // 8
    low = lax.broadcasted_iota(jnp.int32, (pairs, 8, cols), 1) < 4
    for row in range(0, lhs_ref.shape[0], chunk):
        left = lhs_ref[row : row + chunk, :]
        pair = row // 8
        for first_octet in range(0, depth // 8, 2):
            evens, odds = [], []
            for octet in (first_octet, first_octet + 1):
                out = jnp.dot(left, rights[octet], preferred_element_type=F32)
                first = out[:, :cols].reshape(pairs, 8, cols)
                second = out[:, cols:].reshape(pairs, 8, cols)
                evens.append(jnp.where(low, first, pltpu.roll(second, 4, 1)))
                odds.append(jnp.where(low, pltpu.roll(first, 4, 1), second))
            at = slice(first_octet * 8, first_octet * 8 + 16)
            w_ref[pair : pair + pairs, 0, at] = jnp.concatenate(evens, axis=1).astype(BF)
            w_ref[pair : pair + pairs, 1, at] = jnp.concatenate(odds, axis=1).astype(BF)


def mix(feat, lhs, bases, blocks, begin=0, end=None, earlier=None):
    n_bases, model_dim, cols = bases.shape
    depth = 32
    steps = model_dim // depth
    end = steps if end is None else end
    per_part = cols // depth

    def bases_at(i, f):
        return (0, lax.rem(i + begin + f[0] * per_part, steps), 0)

    more = [] if earlier is None else [earlier]
    return pl.pallas_call(
        functools.partial(mix_kernel, chunk=512),
        out_shape=jax.ShapeDtypeStruct((blocks // 2, 2, model_dim, cols), BF),
        grid_spec=pltpu.PrefetchScalarGridSpec(
            num_scalar_prefetch=1,
            grid=(end - begin,),
            in_specs=[
                pl.BlockSpec(lhs.shape, lambda i, f: (0, 0)),
                pl.BlockSpec((n_bases, depth, cols), bases_at),
            ]
            + [pl.BlockSpec(memory_space=pl.ANY)] * len(more),
            out_specs=pl.BlockSpec(
                (blocks // 2, 2, depth, cols),
                lambda i, f: (0, 0, i + begin, 0),
            ),
            scratch_shapes=[
                pltpu.VMEM((n_bases, depth + 8, cols), F32),
                pltpu.VMEM((depth // 8, 4 * n_bases, 2 * cols), BF),
            ],
        ),
        input_output_aliases={3: 0} if more else {},
        cost_estimate=pl.CostEstimate(
            flops=8 * blocks * n_bases * depth * (end - begin) * cols,
            bytes_accessed=blocks * depth * (end - begin) * cols * 2,
            transcendentals=0,
        ),
        compiler_params=pltpu.CompilerParams(vmem_limit_bytes=VMEM_LIMIT),
        name="mix" if earlier is None else "mix_rest",
    )(feat, lhs, in_hbm(bases), *more)


def in_vmem(x):
    return pltpu.with_memory_space_constraint(x, pltpu.VMEM)


def in_hbm(x):
    return pltpu.with_memory_space_constraint(x, pltpu.HBM)


def joins(joined, halves, sems, first_sem):
    rows = halves[0].shape[0]
    return [
        pltpu.make_async_copy(half, joined.at[pl.ds(i * rows, rows)], sems.at[first_sem + i])
        for i, half in enumerate(halves)
    ]


def unpack(word):
    return word & 511, (word >> 9) & 31, (word >> 14) & 63, word >> 20


def blocks_kernel(*refs, group, owners, split, hubs):
    word_ref, src_hbm, dst_hbm = refs[:3]
    pieces, halves, w_ref = refs[3:6], refs[6:8], refs[8]
    n_out = 2 if hubs else 1
    out_hbms = refs[9 : 9 + n_out]
    acc, deg, held, joined, src_ref, dst_ref, out_ref, sems = refs[9 + n_out :]
    spans = word_ref.shape[1] - TILE
    first_group = word_ref[0, spans] if hubs else 0
    end_group = word_ref[0, spans + int(hubs)]

    def fetch(at):
        side = at & 1
        for k in range(2 * group):
            block = word_ref[0, at * (2 * group) + k] & 511
            pltpu.make_async_copy(
                w_ref.at[block >> 1, block & 1], held.at[side, k // 2, k % 2], sems.at[side]
            ).start()

    @pl.when(first_group < end_group)
    def _():
        fetch(first_group)

    loads = joins(joined, halves, sems, 2)
    loads.append(pltpu.make_async_copy(src_hbm, src_ref, sems.at[4]))
    loads.append(pltpu.make_async_copy(dst_hbm, dst_ref, sems.at[5]))
    for load in loads:
        load.start()
    acc[...] = jnp.zeros_like(acc)
    deg[...] = jnp.zeros_like(deg)
    for load in loads:
        load.wait()

    def body(here, carry):
        side = here & 1

        @pl.when(here + 1 < end_group)
        def _():
            fetch(here + 1)

        def arrive():
            pltpu.make_async_copy(
                w_ref.at[pl.ds(0, group)], held.at[side], sems.at[side]
            ).wait()

        if not hubs:
            arrive()
        slot = lax.broadcasted_iota(jnp.int32, (TILE, TILE), 0).astype(F32).astype(BF)
        lane = lax.broadcasted_iota(jnp.int32, (TILE, TILE), 1)
        one = jnp.ones((TILE, TILE), BF)
        zero = jnp.zeros((TILE, TILE), BF)

        def diagonal(first, second):
            top = jnp.concatenate([first, zero], axis=1)
            bottom = jnp.concatenate([zero, second], axis=1)
            return jnp.concatenate([top, bottom], axis=0)

        def fields(pair, k):
            return unpack(word_ref[0, (here * group + pair) * 2 + k])

        def adjacency(pair):
            dst_hot, src_hot, count = [], [], None
            for k in range(2):
                block, src_tile, dst_tile, used = fields(pair, k)
                base = jnp.where(used > 0, dst_tile * TILE, 1 << 20)
                dst = (dst_ref[pl.ds(block, 1), :] - base).astype(F32).astype(BF)
                src = (src_ref[pl.ds(block, 1), :] - src_tile * TILE).astype(F32).astype(BF)
                dst_hot.append(jnp.where(slot == dst, one, zero))
                src_hot.append(jnp.where(slot == src, one, zero))
                column = jnp.sum(dst_hot[k].astype(F32), axis=1, keepdims=True)
                extra = jnp.where(lane == lax.rem(dst_tile, owners), column, 0.0)
                count = extra if count is None else count + extra
            found = lax.dot_general(
                jnp.concatenate(dst_hot, axis=1).astype(HOT),
                diagonal(src_hot[0], src_hot[1]).astype(HOT),
                (((1,), (1,)), ((), ())),
                preferred_element_type=F32,
            )
            return found.astype(BF), count

        def message(pair):
            src_tile = fields(pair, 0)[1]
            rows = pl.ds(pl.multiple_of(src_tile * TILE, TILE), TILE)
            tile = jnp.concatenate(
                [pieces[0][rows, :], pieces[1][rows, :], joined[rows, :], pieces[2][rows, :]],
                axis=1,
            )
            weight = jnp.concatenate([held[side, pair, 0], held[side, pair, 1]], axis=1)
            out = jnp.dot(tile, weight, preferred_element_type=F32).astype(BF)
            return diagonal(out[:, :TILE], out[:, TILE:])

        total = deg[...]
        for first in range(0, group, split):
            pairs = range(first, first + split)
            found = [adjacency(pair) for pair in pairs]
            if hubs and first == 0:
                arrive()
            messages = [message(pair) for pair in pairs]
            sums = [
                jnp.dot(f[0], m, preferred_element_type=F32) for f, m in zip(found, messages)
            ]
            for pair, both, part in zip(pairs, sums, found):
                total = total + part[1]
                for k in range(2):
                    dst = lax.rem(fields(pair, k)[2], owners)
                    acc[dst] = acc[dst] + both[:, k * TILE : (k + 1) * TILE]
        deg[...] = total
        return carry

    lax.fori_loop(first_group, end_group, body, 0)

    deg[...] = deg[...].T
    line = lax.broadcasted_iota(jnp.int32, (DEG_ROWS, TILE), 0)
    core = lax.axis_index("dom") & 1 if hubs else 0
    each = owners // n_out
    for i in range(owners):
        at = n_out * (i % each) + ((core ^ (i // each)) if hubs else 0)
        degree = deg[pl.ds(at, 1), :]
        high = jnp.floor(degree * (1.0 / 256.0)) * 256.0
        low = degree - high
        out_ref[i, :TILE, :] = acc[at].astype(BF)
        rows = jnp.where(line == 0, high, jnp.where(line == 1, low, 0.0))
        out_ref[i, TILE:, :] = rows.astype(BF)
    leaves = [
        pltpu.make_async_copy(out_ref.at[pl.ds(i * each, each)], out, sems.at[2 + i])
        for i, out in enumerate(out_hbms)
    ]
    for leave in leaves:
        leave.start()
    for leave in leaves:
        leave.wait()


def blocks_call(words, weights, edge_src, edge_dst, pieces, owners, hubs, group=16, split=16):
    pair_count, _, model_dim, cols = weights.shape
    vmem = pl.BlockSpec(memory_space=pltpu.VMEM)
    smem = pl.BlockSpec(memory_space=pltpu.SMEM)
    anywhere = pl.BlockSpec(memory_space=pl.ANY)
    return pl.pallas_call(
        functools.partial(blocks_kernel, group=group, owners=owners, split=split, hubs=hubs),
        out_shape=(jax.ShapeDtypeStruct((owners // 2, TILE + DEG_ROWS, cols), BF),) * 2
        if hubs
        else (pltpu.HBM((owners, TILE + DEG_ROWS, cols), BF),),
        in_specs=[smem, anywhere, anywhere] + [vmem] * 3 + [anywhere] * 3,
        out_specs=(anywhere,) * (2 if hubs else 1),
        scratch_shapes=[
            pltpu.VMEM((owners, TILE, cols), F32),
            pltpu.VMEM((TILE, TILE), F32),
            pltpu.VMEM((2, group, 2, model_dim, cols), BF),
            pltpu.VMEM(pieces[0].shape, BF),
            pltpu.VMEM(edge_src.shape, jnp.int32),
            pltpu.VMEM(edge_dst.shape, jnp.int32),
            pltpu.VMEM((owners, TILE + DEG_ROWS, cols), BF),
            pltpu.SemaphoreType.DMA((6,)),
        ],
        cost_estimate=pl.CostEstimate(
            flops=pair_count * 4 * TILE * model_dim * cols,
            bytes_accessed=pair_count * model_dim * cols * 2,
            transcendentals=0,
        ),
        compiler_params=pltpu.CompilerParams(vmem_limit_bytes=VMEM_LIMIT),
        name="hub_blocks" if hubs else "mirror_blocks",
    )(
        words,
        in_hbm(edge_src),
        in_hbm(edge_dst),
        *[in_vmem(x) for x in pieces[:3]],
        *[in_hbm(x) for x in pieces[3:]],
        weights,
    )


def square_lines(value):
    squares = jnp.sum(value * value, axis=1, keepdims=True)
    line = jnp.broadcast_to(squares, value.shape).T[:1, :]
    pieces = [line[:, i : i + TILE] for i in range(0, value.shape[0], TILE)]
    return jnp.concatenate(pieces, axis=0)


def mirror_kernel(
    feat_ref,
    mirror_hbm,
    master_ref,
    self_ref,
    x0_hbm,
    x1_hbm,
    x3_hbm,
    first_hbm,
    second_hbm,
    mixed_ref,
    squares_ref,
    right,
    turned,
    mirror_ref,
    table,
    sems,
    *,
    chunk,
    reach,
):
    step = pl.program_id(0)
    owners = mirror_ref.shape[0]
    cols = mirror_ref.shape[2]

    @pl.when(step == 0)
    def _():
        arrival = pltpu.make_async_copy(mirror_hbm, mirror_ref, sems.at[0])
        arrival.start()
        half = first_hbm.shape[0]
        targets = [
            (x0_hbm, table.at[:, :cols]),
            (x1_hbm, table.at[:, cols : 2 * cols]),
            (x3_hbm, table.at[:, 3 * cols :]),
            (first_hbm, table.at[:half, 2 * cols : 3 * cols]),
            (second_hbm, table.at[half:, 2 * cols : 3 * cols]),
        ]
        loads = [
            pltpu.make_async_copy(a, b, sems.at[1 + i]) for i, (a, b) in enumerate(targets)
        ]
        for load in loads:
            load.start()
        for p in range(4):
            at = pl.multiple_of(lax.rem(feat_ref[0] + p, 4) * cols, cols)
            turned[p * cols : (p + 1) * cols, :] = self_ref[pl.ds(at, cols), :]
        arrival.wait()
        high = mirror_ref[:, TILE, :].astype(F32)
        low = mirror_ref[:, TILE + 1, :].astype(F32)
        pad = jnp.zeros((TILE - 2 * owners, TILE), F32)
        turned_counts = jnp.concatenate([high, low, pad], axis=0).T
        lane = lax.broadcasted_iota(jnp.int32, (TILE, TILE), 1)
        for p in range(owners):
            rows = slice(p * TILE, (p + 1) * TILE)
            right[rows, :cols] = mirror_ref[p, :TILE, :]
            keep = (lane == p) | (lane == p + owners)
            right[rows, cols:] = jnp.where(keep, turned_counts, 0.0).astype(BF)
        for load in loads:
            load.wait()

    rows = pl.ds(pl.multiple_of(step * chunk, chunk), chunk)
    own = jnp.dot(table[rows, :], turned[...], preferred_element_type=F32)

    @pl.when(step * chunk < reach)
    def _():
        local = lax.broadcasted_iota(jnp.int32, (TILE, TILE), 0).astype(F32).astype(BF)
        one = jnp.ones((TILE, TILE), BF)
        zero = jnp.zeros((TILE, TILE), BF)
        columns = []
        for p in range(owners):
            column = []
            for first in range(0, chunk, TILE):
                target = master_ref[p : p + 1, :] - (step * chunk + first)
                column.append(jnp.where(local == target.astype(F32).astype(BF), one, zero))
            columns.append(jnp.concatenate(column, axis=0))
        sums = jnp.dot(jnp.concatenate(columns, axis=1), right[...], preferred_element_type=F32)
        degree = jnp.sum(sums[:, cols:], axis=1, keepdims=True)
        mixed = own + sums[:, :cols] * lax.rsqrt(jnp.maximum(degree, 1.0))
        mixed_ref[...] = mixed
        squares_ref[...] = square_lines(mixed)

    @pl.when(step * chunk >= reach)
    def _():
        mixed_ref[...] = own
        squares_ref[...] = square_lines(own)


def mirror_final(feat, mirror, master, self_weight, pieces):
    n_local, cols = pieces[0].shape
    owners = mirror.shape[0]
    chunk = 1024
    anywhere = pl.BlockSpec(memory_space=pl.ANY)
    whole = lambda shape: pl.BlockSpec(shape, lambda i, *_: (0,) * len(shape))
    return pl.pallas_call(
        functools.partial(mirror_kernel, chunk=chunk, reach=n_local - n_local // 4),
        out_shape=(
            jax.ShapeDtypeStruct((n_local, cols), F32),
            jax.ShapeDtypeStruct((n_local // TILE, TILE), F32),
        ),
        grid_spec=pltpu.PrefetchScalarGridSpec(
            num_scalar_prefetch=1,
            grid=(n_local // chunk,),
            in_specs=[anywhere, whole(master.shape), whole(self_weight.shape)]
            + [anywhere] * len(pieces),
            out_specs=(
                pl.BlockSpec((chunk, cols), lambda i, *_: (i, 0)),
                pl.BlockSpec((chunk // TILE, TILE), lambda i, *_: (i, 0)),
            ),
            scratch_shapes=[
                pltpu.VMEM((owners * TILE, 2 * cols), BF),
                pltpu.VMEM(self_weight.shape, BF),
                pltpu.VMEM(mirror.shape, BF),
                pltpu.VMEM((n_local, 4 * cols), BF),
                pltpu.SemaphoreType.DMA((1 + len(pieces),)),
            ],
        ),
        cost_estimate=pl.CostEstimate(
            flops=n_local * n_local * 4 * cols, bytes_accessed=8 << 20, transcendentals=0
        ),
        compiler_params=pltpu.CompilerParams(vmem_limit_bytes=VMEM_LIMIT),
        name="mirror_final",
    )(feat, in_hbm(mirror), master, self_weight, *[in_hbm(p) for p in pieces])


def hub_kernel(hub_ref, mixed_ref, squares_ref, out_ref, lines_ref):
    hub = jnp.sum(hub_ref[:, :TILE, :].astype(F32), axis=0)
    counts = hub_ref[:, TILE : TILE + DEG_ROWS, :].astype(F32)
    line = jnp.sum(jnp.sum(counts, axis=0), axis=0, keepdims=True)
    column = jnp.broadcast_to(line, (TILE, TILE)).T[:, :1]
    mixed = mixed_ref[:HUB_MIRRORS, :] + hub * lax.rsqrt(jnp.maximum(column, 1.0))
    out_ref[...] = mixed
    lines_ref[...] = squares_ref[...]
    lines_ref[:1, :] = square_lines(mixed)


def hub_final(hub, mixed, squares):
    vmem = pl.BlockSpec(memory_space=pltpu.VMEM)
    return pl.pallas_call(
        hub_kernel,
        out_shape=(
            jax.ShapeDtypeStruct((HUB_MIRRORS, mixed.shape[1]), F32),
            jax.ShapeDtypeStruct(squares.shape, F32),
        ),
        in_specs=[vmem] * 3,
        out_specs=(vmem, vmem),
        compiler_params=pltpu.CompilerParams(vmem_limit_bytes=VMEM_LIMIT),
        name="hub_final",
    )(hub, in_vmem(mixed), in_vmem(squares))


def scale_kernel(mixed_ref, hub_ref, a_ref, b_ref, c_ref, d_ref, gain_ref, out_ref, *, model_dim):
    lines = a_ref[...] + b_ref[...] + c_ref[...] + d_ref[...]
    norm = lax.rsqrt(lines / model_dim + 1e-05)
    gain = gain_ref[...]
    tiles, width = norm.shape
    for i in range(tiles):
        rows = slice(i * width, (i + 1) * width)
        value = hub_ref[...] if i == 0 else mixed_ref[rows, :]
        column = jnp.broadcast_to(norm[i : i + 1, :], (width, width)).T
        out_ref[rows, :] = (value * column * gain).astype(BF)


def scale(mixed, hub_mixed, lines, gain, model_dim):
    vmem = pl.BlockSpec(memory_space=pltpu.VMEM)
    return pl.pallas_call(
        functools.partial(scale_kernel, model_dim=model_dim),
        out_shape=jax.ShapeDtypeStruct(mixed.shape, BF),
        in_specs=[vmem] * 7,
        out_specs=vmem,
        compiler_params=pltpu.CompilerParams(vmem_limit_bytes=VMEM_LIMIT),
        name="scale",
    )(in_vmem(mixed), in_vmem(hub_mixed), *[in_vmem(x) for x in lines], gain)


def from_others(x, size):
    return [
        lax.ppermute(x, "feat", [((i + shift) % size, i) for i in range(size)])
        for shift in range(1, size)
    ]


def on_device(
    embeddings,
    self_weight,
    bases,
    basis_coef,
    out_gain,
    edge_src,
    edge_dst,
    block_rel,
    mirror_master_rows,
    block_count,
):
    owners = lax.axis_size("dom")
    feat_size = lax.axis_size("feat")
    feat = lax.axis_index("feat").astype(jnp.int32)
    blocks = edge_src.shape[0]
    n_local, cols = embeddings.shape
    model_dim = bases.shape[1]
    feat_at = feat.reshape(1)
    ahead = [((i + 1) % feat_size, i) for i in range(feat_size)]
    behind = [(i, (i + 1) % feat_size) for i in range(feat_size)]
    after = lax.ppermute(embeddings, "feat", ahead)
    before = lax.ppermute(embeddings, "feat", behind)

    words, lhs = prepare(
        block_count, edge_src, edge_dst, block_rel, basis_coef, owners, n_local // TILE, 16
    )
    steps = 10
    weights = mix(feat_at, lhs, bases, blocks, 0, steps)
    weights, after, before = lax.optimization_barrier((weights, after, before))
    half = n_local // 2
    halves = [
        lax.ppermute(after[:half], "feat", ahead),
        lax.ppermute(before[half:], "feat", behind),
    ]
    weights = mix(feat_at, lhs, bases, blocks, steps, None, weights)
    pieces = [embeddings, after, before] + halves
    edges = (edge_src, edge_dst)
    (mirror_part,) = blocks_call(words, weights, *edges, pieces, owners, False)
    mirror = lax.all_to_all(mirror_part, "dom", split_axis=0, concat_axis=0, tiled=True)
    weights, _ = lax.optimization_barrier((weights, mirror_part))
    kept, sent = blocks_call(words, weights, *edges, pieces, owners, True)
    came = lax.ppermute(sent, "dom", [(i, i ^ 1) for i in range(owners)])
    hub_part = (kept.astype(F32) + came.astype(F32)).astype(BF)
    hub_part, mirror = lax.optimization_barrier((hub_part, mirror))
    hub = lax.all_to_all(
        hub_part,
        "dom",
        split_axis=0,
        concat_axis=0,
        tiled=True,
        axis_index_groups=[list(range(c, owners, 2)) for c in range(2)],
    )

    mixed, squares = mirror_final(
        feat.reshape(1), mirror, mirror_master_rows.reshape(owners, TILE), self_weight, pieces
    )
    hub_mixed, line = hub_final(hub, mixed, squares)
    lines = [line] + from_others(line, feat_size)
    return scale(mixed, hub_mixed, lines, out_gain.reshape(1, cols), model_dim)


def solution(mesh):
    in_specs = (
        P("dom", "feat"),
        P(None, "feat"),
        P(None, None, "feat"),
        P(),
        P("feat"),
        P("dom", None),
        P("dom", None),
        P("dom"),
        P("dom"),
        P("dom"),
    )
    out_specs = P("dom", "feat")
    return jax.shard_map(
        on_device, mesh=mesh, in_specs=in_specs, out_specs=out_specs, check_vma=False
    )
```

```python
import functools

import jax
import jax.numpy as jnp
from jax import lax
from jax.experimental import pallas as pl
from jax.experimental.pallas import tpu as pltpu
from jax.sharding import PartitionSpec as P

TILE = 128
HUB_MIRRORS = 128
CAP = 128
DEG_ROWS = 16
VMEM_LIMIT = 44 * 1024 * 1024
BF = jnp.bfloat16
F32 = jnp.float32
HOT = jnp.float8_e4m3fn


def prepare_kernel(
    live_ref,
    src_hbm,
    dst_hbm,
    rel_hbm,
    coef_hbm,
    words_ref,
    lhs_ref,
    spread,
    src_ref,
    dst_ref,
    rel_ref,
    coef_ref,
    sems,
    *,
    owners,
    src_tiles,
    group,
):
    loads = [
        pltpu.make_async_copy(a, b, sems.at[i])
        for i, (a, b) in enumerate(
            [(src_hbm, src_ref), (dst_hbm, dst_ref), (rel_hbm, rel_ref), (coef_hbm, coef_ref)]
        )
    ]
    for load in loads:
        load.start()
    for load in loads:
        load.wait()
    blocks = src_ref.shape[0]
    n_bases, relations = coef_ref.shape
    live = live_ref[0]
    src_tile = src_ref[:, :1] >> 7
    dst_tile = dst_ref[:, :1] >> 7
    index = lax.broadcasted_iota(jnp.int32, (blocks, 1), 0)
    active = index < live
    key = jnp.where(dst_tile < owners, src_tiles, 0) + src_tile
    key = jnp.where(active, key, TILE - 1)
    key_wide = jnp.broadcast_to(key, (blocks, TILE))
    key_row = key_wide.astype(F32).T[:1, :]
    lane = lax.broadcasted_iota(jnp.int32, (1, TILE), 1)
    same_key = key_wide == lane
    count = jnp.sum(same_key.astype(F32), axis=0, keepdims=True)
    count = jnp.where(lane < 2 * src_tiles, count, 0.0).astype(jnp.int32)
    pairs = (count + 1) >> 1
    earlier = lax.broadcasted_iota(jnp.int32, (TILE, TILE), 0) < lax.broadcasted_iota(
        jnp.int32, (TILE, TILE), 1
    )
    pairs_wide = jnp.broadcast_to(pairs, (8, TILE)).astype(F32).astype(BF)
    start = jnp.dot(
        pairs_wide, jnp.where(earlier, 1.0, 0.0).astype(BF), preferred_element_type=F32
    )[:1].astype(jnp.int32)
    zero = jnp.zeros_like(pairs)
    mirror_pairs = jnp.sum(
        jnp.where(lane < src_tiles, pairs, zero).astype(F32), axis=1, keepdims=True
    ).astype(jnp.int32)
    hub_pairs = jnp.sum(
        jnp.where(lane >= src_tiles, pairs, zero).astype(F32), axis=1, keepdims=True
    ).astype(jnp.int32)
    shift = group.bit_length() - 1
    mirror_groups = (mirror_pairs + group - 1) >> shift
    hub_groups = (hub_pairs + group - 1) >> shift
    start = start + jnp.where(lane >= src_tiles, mirror_groups * group - mirror_pairs, 0)
    other = lax.broadcasted_iota(jnp.int32, (1, blocks), 1)
    before = (key.astype(F32) == key_row) & (other < index)
    rank = jnp.sum(before.astype(F32), axis=1, keepdims=True).astype(jnp.int32)
    first = jnp.sum(
        jnp.where(same_key, start, 0).astype(F32), axis=1, keepdims=True
    ).astype(jnp.int32)
    place = jnp.where(active, 2 * first + rank, -1)
    word = index | (src_tile << 9) | (dst_tile << 14) | (1 << 20)
    slots = words_ref.shape[1] - TILE
    slot = lax.broadcasted_iota(jnp.int32, (1, slots), 1)
    words = jnp.sum(jnp.where(place == slot, word, 0), axis=0, keepdims=True)
    padding = lax.rem(slot, blocks) | ((slot & 31) << 14)
    words_ref[:, :slots] = jnp.where(words == 0, padding, words)
    words_ref[:, slots:] = jnp.where(
        lane == 0, mirror_groups, jnp.where(lane == 1, mirror_groups + hub_groups, 0)
    )

    rel_wide = jnp.broadcast_to(rel_ref[...].astype(F32), (TILE, blocks)).T[:, :1]
    relation = rel_wide.astype(jnp.int32)
    span = lax.broadcasted_iota(jnp.int32, (1, relations), 1)
    one_hot = jnp.where(relation == span, 1.0, 0.0).astype(BF)
    mixing = lax.dot_general(
        one_hot, coef_ref[...], (((1,), (1,)), ((), ())), preferred_element_type=F32
    )
    copies = lhs_ref.shape[1] // n_bases
    blank = jnp.zeros_like(mixing)
    for i in range(copies):
        row = jnp.concatenate([mixing if k == i else blank for k in range(copies)], axis=1)
        for half in range(copies * n_bases // TILE):
            spread[half, pl.ds(i, blocks, stride=copies), :] = row[:, half * TILE : (half + 1) * TILE]
    for half in range(copies * n_bases // TILE):
        lhs_ref[:, half * TILE : (half + 1) * TILE] = spread[half].astype(BF)


def prepare(live, edge_src, edge_dst, block_rel, basis_coef, owners, src_tiles, group):
    blocks = edge_src.shape[0]
    n_bases = basis_coef.shape[1]
    slots = 2 * group * (-(-(blocks + 2 * src_tiles) // (2 * group)) + 1)
    slots = -(-slots // TILE) * TILE
    vmem = pl.BlockSpec(memory_space=pltpu.VMEM)
    return pl.pallas_call(
        functools.partial(prepare_kernel, owners=owners, src_tiles=src_tiles, group=group),
        out_shape=(
            jax.ShapeDtypeStruct((1, slots + TILE), jnp.int32),
            jax.ShapeDtypeStruct((4 * blocks, 4 * n_bases), BF),
        ),
        in_specs=[pl.BlockSpec(memory_space=pltpu.SMEM)] + [pl.BlockSpec(memory_space=pl.ANY)] * 4,
        out_specs=(vmem, vmem),
        scratch_shapes=[
            pltpu.VMEM((4 * n_bases // TILE, 4 * blocks, TILE), F32),
            pltpu.VMEM(edge_src.shape, jnp.int32),
            pltpu.VMEM(edge_dst.shape, jnp.int32),
            pltpu.VMEM((1, blocks), jnp.int32),
            pltpu.VMEM(basis_coef.shape[::-1], BF),
            pltpu.SemaphoreType.DMA((4,)),
        ],
        compiler_params=pltpu.CompilerParams(vmem_limit_bytes=VMEM_LIMIT),
        name="prepare",
    )(
        live,
        in_hbm(edge_src),
        in_hbm(edge_dst),
        in_hbm(block_rel.reshape(1, blocks)),
        in_hbm(basis_coef.T),
    )


def mix_kernel(feat_ref, lhs_ref, bases_ref, *rest, chunk):
    w_ref, spread, rights = rest[-3:]
    n_bases, depth, cols = bases_ref.shape
    spread[:, :depth, :] = bases_ref[...].astype(F32)
    pitch = spread.shape[1]
    flat = spread.reshape(n_bases * pitch, cols)
    for d in range(depth):
        octet, half, row = d // 8, d % 8 // 4, d % 4
        rows = slice(row * n_bases, (row + 1) * n_bases)
        rights[octet, rows, half * cols : (half + 1) * cols] = flat[
            pl.ds(d, n_bases, stride=pitch), :
        ].astype(BF)
    pairs = chunk // 8
    low = lax.broadcasted_iota(jnp.int32, (pairs, 8, cols), 1) < 4
    for row in range(0, lhs_ref.shape[0], chunk):
        left = lhs_ref[row : row + chunk, :]
        pair = row // 8
        for first_octet in range(0, depth // 8, 2):
            evens, odds = [], []
            for octet in (first_octet, first_octet + 1):
                out = jnp.dot(left, rights[octet], preferred_element_type=F32)
                first = out[:, :cols].reshape(pairs, 8, cols)
                second = out[:, cols:].reshape(pairs, 8, cols)
                evens.append(jnp.where(low, first, pltpu.roll(second, 4, 1)))
                odds.append(jnp.where(low, pltpu.roll(first, 4, 1), second))
            at = slice(first_octet * 8, first_octet * 8 + 16)
            w_ref[pair : pair + pairs, 0, at] = jnp.concatenate(evens, axis=1).astype(BF)
            w_ref[pair : pair + pairs, 1, at] = jnp.concatenate(odds, axis=1).astype(BF)


def mix(feat, lhs, bases, blocks, begin=0, end=None, earlier=None):
    n_bases, model_dim, cols = bases.shape
    depth = 32
    steps = model_dim // depth
    end = steps if end is None else end
    per_part = cols // depth

    def bases_at(i, f):
        return (0, lax.rem(i + begin + f[0] * per_part, steps), 0)

    more = [] if earlier is None else [earlier]
    return pl.pallas_call(
        functools.partial(mix_kernel, chunk=512),
        out_shape=jax.ShapeDtypeStruct((blocks // 2, 2, model_dim, cols), BF),
        grid_spec=pltpu.PrefetchScalarGridSpec(
            num_scalar_prefetch=1,
            grid=(end - begin,),
            in_specs=[
                pl.BlockSpec(lhs.shape, lambda i, f: (0, 0)),
                pl.BlockSpec((n_bases, depth, cols), bases_at),
            ]
            + [pl.BlockSpec(memory_space=pl.ANY)] * len(more),
            out_specs=pl.BlockSpec(
                (blocks // 2, 2, depth, cols),
                lambda i, f: (0, 0, i + begin, 0),
            ),
            scratch_shapes=[
                pltpu.VMEM((n_bases, depth + 8, cols), F32),
                pltpu.VMEM((depth // 8, 4 * n_bases, 2 * cols), BF),
            ],
        ),
        input_output_aliases={3: 0} if more else {},
        cost_estimate=pl.CostEstimate(
            flops=8 * blocks * n_bases * depth * (end - begin) * cols,
            bytes_accessed=blocks * depth * (end - begin) * cols * 2,
            transcendentals=0,
        ),
        compiler_params=pltpu.CompilerParams(vmem_limit_bytes=VMEM_LIMIT),
        name="mix" if earlier is None else "mix_rest",
    )(feat, lhs, in_hbm(bases), *more)


def in_vmem(x):
    return pltpu.with_memory_space_constraint(x, pltpu.VMEM)


def in_hbm(x):
    return pltpu.with_memory_space_constraint(x, pltpu.HBM)


def joins(joined, halves, sems, first_sem):
    rows = halves[0].shape[0]
    return [
        pltpu.make_async_copy(half, joined.at[pl.ds(i * rows, rows)], sems.at[first_sem + i])
        for i, half in enumerate(halves)
    ]


def unpack(word):
    return word & 511, (word >> 9) & 31, (word >> 14) & 63, word >> 20


def blocks_kernel(*refs, group, owners, split, hubs):
    word_ref, src_hbm, dst_hbm = refs[:3]
    pieces, halves, w_ref = refs[3:6], refs[6:8], refs[8]
    n_out = 2 if hubs else 1
    out_hbms = refs[9 : 9 + n_out]
    acc, deg, held, joined, src_ref, dst_ref, out_ref, sems = refs[9 + n_out :]
    spans = word_ref.shape[1] - TILE
    first_group = word_ref[0, spans] if hubs else 0
    end_group = word_ref[0, spans + int(hubs)]

    def fetch(at):
        side = at & 1
        for k in range(2 * group):
            block = word_ref[0, at * (2 * group) + k] & 511
            pltpu.make_async_copy(
                w_ref.at[block >> 1, block & 1], held.at[side, k // 2, k % 2], sems.at[side]
            ).start()

    @pl.when(first_group < end_group)
    def _():
        fetch(first_group)

    loads = joins(joined, halves, sems, 2)
    loads.append(pltpu.make_async_copy(src_hbm, src_ref, sems.at[4]))
    loads.append(pltpu.make_async_copy(dst_hbm, dst_ref, sems.at[5]))
    for load in loads:
        load.start()
    acc[...] = jnp.zeros_like(acc)
    deg[...] = jnp.zeros_like(deg)
    for load in loads:
        load.wait()

    def body(here, carry):
        side = here & 1

        @pl.when(here + 1 < end_group)
        def _():
            fetch(here + 1)

        def arrive():
            pltpu.make_async_copy(
                w_ref.at[pl.ds(0, group)], held.at[side], sems.at[side]
            ).wait()

        if not hubs:
            arrive()
        slot = lax.broadcasted_iota(jnp.int32, (TILE, TILE), 0).astype(F32).astype(BF)
        lane = lax.broadcasted_iota(jnp.int32, (TILE, TILE), 1)
        one = jnp.ones((TILE, TILE), BF)
        zero = jnp.zeros((TILE, TILE), BF)

        def diagonal(first, second):
            top = jnp.concatenate([first, zero], axis=1)
            bottom = jnp.concatenate([zero, second], axis=1)
            return jnp.concatenate([top, bottom], axis=0)

        def fields(pair, k):
            return unpack(word_ref[0, (here * group + pair) * 2 + k])

        def adjacency(pair):
            dst_hot, src_hot, count = [], [], None
            for k in range(2):
                block, src_tile, dst_tile, used = fields(pair, k)
                base = jnp.where(used > 0, dst_tile * TILE, 1 << 20)
                dst = (dst_ref[pl.ds(block, 1), :] - base).astype(F32).astype(BF)
                src = (src_ref[pl.ds(block, 1), :] - src_tile * TILE).astype(F32).astype(BF)
                dst_hot.append(jnp.where(slot == dst, one, zero))
                src_hot.append(jnp.where(slot == src, one, zero))
                column = jnp.sum(dst_hot[k].astype(F32), axis=1, keepdims=True)
                extra = jnp.where(lane == lax.rem(dst_tile, owners), column, 0.0)
                count = extra if count is None else count + extra
            found = lax.dot_general(
                jnp.concatenate(dst_hot, axis=1).astype(HOT),
                diagonal(src_hot[0], src_hot[1]).astype(HOT),
                (((1,), (1,)), ((), ())),
                preferred_element_type=F32,
            )
            return found.astype(BF), count

        def message(pair):
            src_tile = fields(pair, 0)[1]
            rows = pl.ds(pl.multiple_of(src_tile * TILE, TILE), TILE)
            tile = jnp.concatenate(
                [pieces[0][rows, :], pieces[1][rows, :], joined[rows, :], pieces[2][rows, :]],
                axis=1,
            )
            weight = jnp.concatenate([held[side, pair, 0], held[side, pair, 1]], axis=1)
            out = jnp.dot(tile, weight, preferred_element_type=F32).astype(BF)
            return diagonal(out[:, :TILE], out[:, TILE:])

        total = deg[...]
        for first in range(0, group, split):
            pairs = range(first, first + split)
            found = [adjacency(pair) for pair in pairs]
            if hubs and first == 0:
                arrive()
            messages = [message(pair) for pair in pairs]
            sums = [
                jnp.dot(f[0], m, preferred_element_type=F32) for f, m in zip(found, messages)
            ]
            for pair, both, part in zip(pairs, sums, found):
                total = total + part[1]
                for k in range(2):
                    dst = lax.rem(fields(pair, k)[2], owners)
                    acc[dst] = acc[dst] + both[:, k * TILE : (k + 1) * TILE]
        deg[...] = total
        return carry

    lax.fori_loop(first_group, end_group, body, 0)

    deg[...] = deg[...].T
    line = lax.broadcasted_iota(jnp.int32, (DEG_ROWS, TILE), 0)
    core = lax.axis_index("dom") & 1 if hubs else 0
    each = owners // n_out
    for i in range(owners):
        at = n_out * (i % each) + ((core ^ (i // each)) if hubs else 0)
        degree = deg[pl.ds(at, 1), :]
        high = jnp.floor(degree * (1.0 / 256.0)) * 256.0
        low = degree - high
        out_ref[i, :TILE, :] = acc[at].astype(BF)
        rows = jnp.where(line == 0, high, jnp.where(line == 1, low, 0.0))
        out_ref[i, TILE:, :] = rows.astype(BF)
    leaves = [
        pltpu.make_async_copy(out_ref.at[pl.ds(i * each, each)], out, sems.at[2 + i])
        for i, out in enumerate(out_hbms)
    ]
    for leave in leaves:
        leave.start()
    for leave in leaves:
        leave.wait()


def blocks_call(words, weights, edge_src, edge_dst, pieces, owners, hubs, group=16, split=16):
    pair_count, _, model_dim, cols = weights.shape
    vmem = pl.BlockSpec(memory_space=pltpu.VMEM)
    smem = pl.BlockSpec(memory_space=pltpu.SMEM)
    anywhere = pl.BlockSpec(memory_space=pl.ANY)
    return pl.pallas_call(
        functools.partial(blocks_kernel, group=group, owners=owners, split=split, hubs=hubs),
        out_shape=(jax.ShapeDtypeStruct((owners // 2, TILE + DEG_ROWS, cols), BF),) * 2
        if hubs
        else (pltpu.HBM((owners, TILE + DEG_ROWS, cols), BF),),
        in_specs=[smem, anywhere, anywhere] + [vmem] * 3 + [anywhere] * 3,
        out_specs=(anywhere,) * (2 if hubs else 1),
        scratch_shapes=[
            pltpu.VMEM((owners, TILE, cols), F32),
            pltpu.VMEM((TILE, TILE), F32),
            pltpu.VMEM((2, group, 2, model_dim, cols), BF),
            pltpu.VMEM(pieces[0].shape, BF),
            pltpu.VMEM(edge_src.shape, jnp.int32),
            pltpu.VMEM(edge_dst.shape, jnp.int32),
            pltpu.VMEM((owners, TILE + DEG_ROWS, cols), BF),
            pltpu.SemaphoreType.DMA((6,)),
        ],
        cost_estimate=pl.CostEstimate(
            flops=pair_count * 4 * TILE * model_dim * cols,
            bytes_accessed=pair_count * model_dim * cols * 2,
            transcendentals=0,
        ),
        compiler_params=pltpu.CompilerParams(vmem_limit_bytes=VMEM_LIMIT),
        name="hub_blocks" if hubs else "mirror_blocks",
    )(
        words,
        in_hbm(edge_src),
        in_hbm(edge_dst),
        *[in_vmem(x) for x in pieces[:3]],
        *[in_hbm(x) for x in pieces[3:]],
        weights,
    )


def square_lines(value):
    squares = jnp.sum(value * value, axis=1, keepdims=True)
    line = jnp.broadcast_to(squares, value.shape).T[:1, :]
    pieces = [line[:, i : i + TILE] for i in range(0, value.shape[0], TILE)]
    return jnp.concatenate(pieces, axis=0)


def mirror_kernel(
    feat_ref,
    mirror_hbm,
    master_ref,
    self_ref,
    x0_hbm,
    x1_hbm,
    x3_hbm,
    first_hbm,
    second_hbm,
    mixed_ref,
    squares_ref,
    right,
    turned,
    mirror_ref,
    table,
    sems,
    *,
    chunk,
    reach,
):
    step = pl.program_id(0)
    owners = mirror_ref.shape[0]
    cols = mirror_ref.shape[2]

    @pl.when(step == 0)
    def _():
        arrival = pltpu.make_async_copy(mirror_hbm, mirror_ref, sems.at[0])
        arrival.start()
        half = first_hbm.shape[0]
        targets = [
            (x0_hbm, table.at[:, :cols]),
            (x1_hbm, table.at[:, cols : 2 * cols]),
            (x3_hbm, table.at[:, 3 * cols :]),
            (first_hbm, table.at[:half, 2 * cols : 3 * cols]),
            (second_hbm, table.at[half:, 2 * cols : 3 * cols]),
        ]
        loads = [
            pltpu.make_async_copy(a, b, sems.at[1 + i]) for i, (a, b) in enumerate(targets)
        ]
        for load in loads:
            load.start()
        for p in range(4):
            at = pl.multiple_of(lax.rem(feat_ref[0] + p, 4) * cols, cols)
            turned[p * cols : (p + 1) * cols, :] = self_ref[pl.ds(at, cols), :]
        arrival.wait()
        high = mirror_ref[:, TILE, :].astype(F32)
        low = mirror_ref[:, TILE + 1, :].astype(F32)
        pad = jnp.zeros((TILE - 2 * owners, TILE), F32)
        turned_counts = jnp.concatenate([high, low, pad], axis=0).T
        lane = lax.broadcasted_iota(jnp.int32, (TILE, TILE), 1)
        for p in range(owners):
            rows = slice(p * TILE, (p + 1) * TILE)
            right[rows, :cols] = mirror_ref[p, :TILE, :]
            keep = (lane == p) | (lane == p + owners)
            right[rows, cols:] = jnp.where(keep, turned_counts, 0.0).astype(BF)
        for load in loads:
            load.wait()

    rows = pl.ds(pl.multiple_of(step * chunk, chunk), chunk)
    own = jnp.dot(table[rows, :], turned[...], preferred_element_type=F32)

    @pl.when(step * chunk < reach)
    def _():
        local = lax.broadcasted_iota(jnp.int32, (TILE, TILE), 0).astype(F32).astype(BF)
        one = jnp.ones((TILE, TILE), BF)
        zero = jnp.zeros((TILE, TILE), BF)
        columns = []
        for p in range(owners):
            column = []
            for first in range(0, chunk, TILE):
                target = master_ref[p : p + 1, :] - (step * chunk + first)
                column.append(jnp.where(local == target.astype(F32).astype(BF), one, zero))
            columns.append(jnp.concatenate(column, axis=0))
        sums = jnp.dot(jnp.concatenate(columns, axis=1), right[...], preferred_element_type=F32)
        degree = jnp.sum(sums[:, cols:], axis=1, keepdims=True)
        mixed = own + sums[:, :cols] * lax.rsqrt(jnp.maximum(degree, 1.0))
        mixed_ref[...] = mixed
        squares_ref[...] = square_lines(mixed)

    @pl.when(step * chunk >= reach)
    def _():
        mixed_ref[...] = own
        squares_ref[...] = square_lines(own)


def mirror_final(feat, mirror, master, self_weight, pieces):
    n_local, cols = pieces[0].shape
    owners = mirror.shape[0]
    chunk = 1024
    anywhere = pl.BlockSpec(memory_space=pl.ANY)
    whole = lambda shape: pl.BlockSpec(shape, lambda i, *_: (0,) * len(shape))
    return pl.pallas_call(
        functools.partial(mirror_kernel, chunk=chunk, reach=n_local - n_local // 4),
        out_shape=(
            jax.ShapeDtypeStruct((n_local, cols), F32),
            jax.ShapeDtypeStruct((n_local // TILE, TILE), F32),
        ),
        grid_spec=pltpu.PrefetchScalarGridSpec(
            num_scalar_prefetch=1,
            grid=(n_local // chunk,),
            in_specs=[anywhere, whole(master.shape), whole(self_weight.shape)]
            + [anywhere] * len(pieces),
            out_specs=(
                pl.BlockSpec((chunk, cols), lambda i, *_: (i, 0)),
                pl.BlockSpec((chunk // TILE, TILE), lambda i, *_: (i, 0)),
            ),
            scratch_shapes=[
                pltpu.VMEM((owners * TILE, 2 * cols), BF),
                pltpu.VMEM(self_weight.shape, BF),
                pltpu.VMEM(mirror.shape, BF),
                pltpu.VMEM((n_local, 4 * cols), BF),
                pltpu.SemaphoreType.DMA((1 + len(pieces),)),
            ],
        ),
        cost_estimate=pl.CostEstimate(
            flops=n_local * n_local * 4 * cols, bytes_accessed=8 << 20, transcendentals=0
        ),
        compiler_params=pltpu.CompilerParams(vmem_limit_bytes=VMEM_LIMIT),
        name="mirror_final",
    )(feat, in_hbm(mirror), master, self_weight, *[in_hbm(p) for p in pieces])


def hub_kernel(hub_ref, mixed_ref, squares_ref, out_ref, lines_ref):
    hub = jnp.sum(hub_ref[:, :TILE, :].astype(F32), axis=0)
    counts = hub_ref[:, TILE : TILE + DEG_ROWS, :].astype(F32)
    line = jnp.sum(jnp.sum(counts, axis=0), axis=0, keepdims=True)
    column = jnp.broadcast_to(line, (TILE, TILE)).T[:, :1]
    mixed = mixed_ref[:HUB_MIRRORS, :] + hub * lax.rsqrt(jnp.maximum(column, 1.0))
    out_ref[...] = mixed
    lines_ref[...] = squares_ref[...]
    lines_ref[:1, :] = square_lines(mixed)


def hub_final(hub, mixed, squares):
    vmem = pl.BlockSpec(memory_space=pltpu.VMEM)
    return pl.pallas_call(
        hub_kernel,
        out_shape=(
            jax.ShapeDtypeStruct((HUB_MIRRORS, mixed.shape[1]), F32),
            jax.ShapeDtypeStruct(squares.shape, F32),
        ),
        in_specs=[vmem] * 3,
        out_specs=(vmem, vmem),
        compiler_params=pltpu.CompilerParams(vmem_limit_bytes=VMEM_LIMIT),
        name="hub_final",
    )(hub, in_vmem(mixed), in_vmem(squares))


def scale_kernel(mixed_ref, hub_ref, a_ref, b_ref, gain_ref, out_ref, *, model_dim):
    lines = a_ref[...] + b_ref[...]
    norm = lax.rsqrt(lines / model_dim + 1e-05)
    gain = gain_ref[...]
    tiles, width = norm.shape
    for i in range(tiles):
        rows = slice(i * width, (i + 1) * width)
        value = hub_ref[...] if i == 0 else mixed_ref[rows, :]
        column = jnp.broadcast_to(norm[i : i + 1, :], (width, width)).T
        out_ref[rows, :] = (value * column * gain).astype(BF)


def scale(mixed, hub_mixed, lines, gain, model_dim):
    vmem = pl.BlockSpec(memory_space=pltpu.VMEM)
    return pl.pallas_call(
        functools.partial(scale_kernel, model_dim=model_dim),
        out_shape=jax.ShapeDtypeStruct(mixed.shape, BF),
        in_specs=[vmem] * 5,
        out_specs=vmem,
        compiler_params=pltpu.CompilerParams(vmem_limit_bytes=VMEM_LIMIT),
        name="scale",
    )(in_vmem(mixed), in_vmem(hub_mixed), *[in_vmem(x) for x in lines], gain)


def on_device(
    embeddings,
    self_weight,
    bases,
    basis_coef,
    out_gain,
    edge_src,
    edge_dst,
    block_rel,
    mirror_master_rows,
    block_count,
):
    owners = lax.axis_size("dom")
    feat_size = lax.axis_size("feat")
    feat = lax.axis_index("feat").astype(jnp.int32)
    blocks = edge_src.shape[0]
    n_local, cols = embeddings.shape
    model_dim = bases.shape[1]
    feat_at = feat.reshape(1)
    ahead = [((i + 1) % feat_size, i) for i in range(feat_size)]
    behind = [(i, (i + 1) % feat_size) for i in range(feat_size)]
    after = lax.ppermute(embeddings, "feat", ahead)
    before = lax.ppermute(embeddings, "feat", behind)

    words, lhs = prepare(
        block_count, edge_src, edge_dst, block_rel, basis_coef, owners, n_local // TILE, 16
    )
    steps = 10
    weights = mix(feat_at, lhs, bases, blocks, 0, steps)
    weights, after, before = lax.optimization_barrier((weights, after, before))
    half = n_local // 2
    halves = [
        lax.ppermute(after[:half], "feat", ahead),
        lax.ppermute(before[half:], "feat", behind),
    ]
    weights = mix(feat_at, lhs, bases, blocks, steps, None, weights)
    pieces = [embeddings, after, before] + halves
    edges = (edge_src, edge_dst)
    (mirror_part,) = blocks_call(words, weights, *edges, pieces, owners, False)
    mirror = lax.all_to_all(mirror_part, "dom", split_axis=0, concat_axis=0, tiled=True)
    weights, _ = lax.optimization_barrier((weights, mirror_part))
    kept, sent = blocks_call(words, weights, *edges, pieces, owners, True)
    came = lax.ppermute(sent, "dom", [(i, i ^ 1) for i in range(owners)])
    hub_part = (kept.astype(F32) + came.astype(F32)).astype(BF)
    hub_part, mirror = lax.optimization_barrier((hub_part, mirror))
    hub = lax.all_to_all(
        hub_part,
        "dom",
        split_axis=0,
        concat_axis=0,
        tiled=True,
        axis_index_groups=[list(range(c, owners, 2)) for c in range(2)],
    )

    mixed, squares = mirror_final(
        feat.reshape(1), mirror, mirror_master_rows.reshape(owners, TILE), self_weight, pieces
    )
    hub_mixed, line = hub_final(hub, mixed, squares)
    pair = line + lax.ppermute(line, "feat", [(i, i ^ 1) for i in range(feat_size)])
    lines = [pair, lax.ppermute(pair, "feat", [(i, feat_size - 1 - i) for i in range(feat_size)])]
    return scale(mixed, hub_mixed, lines, out_gain.reshape(1, cols), model_dim)


def solution(mesh):
    in_specs = (
        P("dom", "feat"),
        P(None, "feat"),
        P(None, None, "feat"),
        P(),
        P("feat"),
        P("dom", None),
        P("dom", None),
        P("dom"),
        P("dom"),
        P("dom"),
    )
    out_specs = P("dom", "feat")
    return jax.shard_map(
        on_device, mesh=mesh, in_specs=in_specs, out_specs=out_specs, check_vma=False
    )
```
